32 devices in a mesh: group: 2 (over x), expert: 16 (over z, y, core).
Axes of the slice: x: 2, y: 2, z: 4, core: 2. Of those that a mesh axis runs over, the one named last changes fastest.
Arguments:
- tokens: bfloat16 [4096, 3584], P(('group', 'expert')), parts along dimension 0, may hold values from -6 to 6
- norm_gain: float32 [3584], replicated, may hold values from 0.1 to 1.9
- final_gain: float32 [3584], replicated, may hold values from 0.1 to 1.9
- gate_weight: bfloat16 [3584, 8192], P(None, 'expert'), may hold values from -0.09375 to 0.09375
- up_weight: bfloat16 [3584, 8192], P(None, 'expert'), may hold values from -0.09375 to 0.09375
- down_weight: bfloat16 [8192, 3584], P('expert'), may hold values from -0.125 to 0.125
- picks: int32 [4096, 2], P(('group', 'expert')), parts along dimension 0, may hold values from 0 to 3, all different within a row; in each aligned block of 128 rows (0 to 127, 128 to 255, ...) at most 80 rows name the same one
- gates: float32 [4096, 2], P(('group', 'expert')), parts along dimension 0, may hold values from 0.2 to 1
- target_rows: bfloat16 [4096, 3584], P(('group', 'expert')), parts along dimension 0, may hold values from -0.09375 to 0.09375
- rest_lse: float32 [4096], P(('group', 'expert')), parts along dimension 0, may hold values from -2 to 4
- segment_ids: int32 [4096], P(('group', 'expert')), parts along dimension 0, may hold values from 0 to 15, never falling along the last dimension, each value on 1 to 256 neighbouring positions
- ref_logps: float32 [32], P('group'), parts along dimension 0, may hold values from -192 to 192
Outputs:
- sequence_logps: float32 [32], P('group'), parts along dimension 0
- pair_loss: float32 [16], P('group'), parts along dimension 0
The draws below stay inside these ranges and needn't reach their ends.
There are 2 independent parts, one for each index of `group`. The reference program is written for one: setup_inputs(seed, part) draws one part's arguments, and reference() takes and returns one part's arrays. A program takes and returns all parts, laid end to end along the dimension named above; an argument that names none is the same for every part. Nothing has to cross between parts.
Inputs may be any that keep to these rules, and one draw needn't show every extreme that they name: Among the rows of one device no expert is picked more than 80 times, a bound that some block reaches; the picks of one token differ. `segment_ids`: never falling along the tokens; each sequence has 1 to 256 tokens and one has exactly that many; sequence 2p is the chosen and 2p + 1 the rejected answer of pair p.
All inputs are finite; a program needn't handle non-finite values.
Results may differ from the reference program's by a relative error of at most 0.0005.
Values may be sent and summed in bfloat16 or wider, within the bound.
No kernel may reach another device: no remote copies, remote signals or barrier semaphores. Data moves between devices by JAX's collectives and lax.ppermute only.
A program may use at most 128 MiB of HBM per device.

```python
import math
import jax
import jax.numpy as jnp
import numpy as np
from jax import lax

D = 3584
FFE = 2048
HID_DEV = 512
TOPK = 2
TOK_DEV = 128
SEQ_MEAN = 128
EXPERTS = 4
CAP = 80
TOKENS = 2048
SEQS = 16
N_EXPERT = 16


def levels(stream_key, dims, split, least, top_value):
    def one(dim, blocks):
        heights = jax.random.uniform(jax.random.fold_in(jax.random.fold_in(stream_key, 6), dim), (blocks,), jnp.float32, least / len(split), top_value / len(split))
        return jnp.repeat(jnp.exp(heights), dims[dim] // blocks).reshape((-1,) + (1,) * (len(dims) - dim - 1))

    loudness = one(*split[0])
    for cut in split[1:]:
        loudness = loudness * one(*cut)
    return loudness


def split_up(count, total, most, skew):
    weights = [(1 << 20) // math.isqrt(standing ** skew) + 1 for standing in range(2, count + 1)]
    rest, counts = total - most - (count - 1), [1] * (count - 1)
    while rest > 0:
        candidates = [i for i in range(count - 1) if counts[i] < most]
        mass, budget = sum([weights[i] for i in candidates]), rest
        for i in candidates:
            more = min(most - counts[i], max(1, budget * weights[i] // mass), rest)
            counts[i] = counts[i] + more
            rest = rest - more
    return np.array([most] + counts)


def uneven(key, amount, total, reach, skew):
    if amount == 2:
        one = jax.random.randint(key, (), max(1, total - reach), min(reach, total - 1) + 1)
        return jnp.stack([one, total - one])
    tallies = jnp.asarray(split_up(amount, total, reach, skew), jnp.int32)
    twos = (amount - 1) // 2
    donor, sink = tallies[1:1 + 2 * twos:2], tallies[2:2 + 2 * twos:2]
    slack = jnp.minimum(donor - 1, reach - sink)
    moved = jax.random.randint(jax.random.fold_in(key, 1), (twos,), 0, 1 << 20) % (slack + 1)
    tallies = tallies.at[1:1 + 2 * twos:2].set(donor - moved).at[2:2 + 2 * twos:2].set(sink + moved)
    return tallies[jax.random.permutation(jax.random.fold_in(key, 2), amount)]


def routed_block(key, own, number, rows, amount, top, reach, lean):
    sequence = jax.random.permutation(key, amount)
    packed, usual = shares(amount, rows * top, reach, lean, True), shares(amount, rows * top, reach, lean, False)
    places = jnp.arange(amount)

    def named(tallies, turn):
        used = int((tallies > 0).sum())
        fixed = max(1, used // 4)
        shifted = fixed + (places - fixed + turn * (used - fixed)) % max(1, amount - fixed)
        return jnp.zeros((amount,), jnp.int32).at[sequence[jnp.where(places < fixed, places, shifted)]].set(jnp.asarray(tallies, jnp.int32))

    tallies = jnp.where(number % 4 == 0, named(packed, number // 4), named(usual, number - number // 4 - 1))
    mixed = jax.random.permutation(jax.random.fold_in(own, 3), amount)
    giver, taker = mixed[0:amount // 2 * 2:2], mixed[1:amount // 2 * 2:2]
    room = jnp.minimum(tallies[giver] - 1, reach - tallies[taker]) // 2
    room = jnp.where((giver == sequence[0]) | (taker == sequence[0]) | (tallies[taker] == 0), 0, jnp.maximum(room, 0))
    shifted = jax.random.randint(jax.random.fold_in(own, 4), (amount // 2,), 0, 1 << 20) % (room + 1)
    tallies = tallies.at[giver].add(-shifted).at[taker].add(shifted)
    members = jnp.searchsorted(jnp.cumsum(tallies), jnp.arange(rows * top), side="right").astype(jnp.int32)
    table = members.reshape(top, rows).T
    table = table[jax.random.permutation(jax.random.fold_in(own, 1), rows)]
    turn = jax.random.randint(jax.random.fold_in(own, 2), (rows, 1), 0, top)
    return jnp.take_along_axis(table, (jnp.arange(top)[None, :] + turn) % top, axis=1)


def shares(number_of, total, bound, skew, full):
    loads = [(1 << 20) // math.isqrt(rank ** skew) + 1 for rank in range(1, number_of + 1)]
    largest = bound if full else min(bound, max(-(-total // number_of), total * loads[0] // sum(loads)))
    least = 1 if total - largest >= number_of - 1 else 0
    holding, surplus = [largest] + [least] * (number_of - 1), total - largest - least * (number_of - 1)
    while surplus > 0:
        candidates = [i for i in range(1, number_of) if holding[i] < largest] or [i for i in range(1, number_of) if holding[i] < bound]
        pool, budget = sum([loads[i] for i in candidates]), surplus
        for i in candidates:
            more = min(bound - holding[i], max(1, budget * loads[i] // pool), surplus)
            holding[i] = holding[i] + more
            surplus = surplus - more
    return np.array(holding)


def centred(stream_key, dims, deviation, most, split=(), held_as=jnp.bfloat16):
    array = jax.random.normal(stream_key, dims, jnp.float32) * deviation
    if len(split) > 0:
        array = levels(stream_key, dims, split, -0.22, 0.18) * array
    return jnp.clip(array, min=-most, max=most).astype(held_as)


def setup_inputs(seed: int = 0, part: int = 0) -> dict:
    splits = jax.random.split(jax.random.key(seed), 13)
    part_keys = jax.random.split(jax.random.fold_in(splits[12], part), 13)
    tokens = centred(part_keys[0], (TOKENS, D), 1.0, 6.0, ((0, 16),))
    norm_gain = jnp.clip(1.0 + 0.18 * jax.random.normal(splits[1], (D,), jnp.float32), 0.1, 1.9)
    final_gain = jnp.clip(1.0 + 0.18 * jax.random.normal(splits[2], (D,), jnp.float32), 0.1, 1.9)
    gate_weight = centred(splits[3], (D, EXPERTS * FFE), D ** -0.5, 0.09375, ((1, 16),))
    up_weight = centred(splits[4], (D, EXPERTS * FFE), D ** -0.5, 0.09375, ((1, 16),))
    down_weight = centred(splits[5], (EXPERTS * FFE, D), FFE ** -0.5, 0.125, ((0, 16),))
    picks_keys = jax.random.split(jax.random.fold_in(part_keys[6], 1), TOKENS // TOK_DEV)
    picks_turns = jax.random.permutation(jax.random.fold_in(part_keys[6], 3), TOKENS // TOK_DEV)
    picks = jax.vmap(lambda own, number: routed_block(jax.random.fold_in(part_keys[6], 2), own, number, TOK_DEV, EXPERTS, TOPK, CAP, 2))(picks_keys, picks_turns).reshape((TOKENS, TOPK))
    gates = jnp.clip(0.2 + 0.8 * jax.random.uniform(part_keys[7], (TOKENS, TOPK), jnp.float32) ** levels(part_keys[7], (TOKENS, TOPK), ((0, 16),), -0.2, 0.2), 0.2, 1.0)
    target_rows = centred(part_keys[8], (TOKENS, D), D ** -0.5, 0.09375, ((0, 16),))
    rest_lse = jnp.clip(-2.0 + 6.0 * jax.random.uniform(part_keys[9], (TOKENS,), jnp.float32) ** levels(part_keys[9], (TOKENS,), ((0, 16),), -0.2, 0.2), -2.0, 4.0)
    segment_ids = jnp.searchsorted(jnp.cumsum(uneven(part_keys[10], SEQS, TOKENS, 2 * SEQ_MEAN, 2)), jnp.arange(TOKENS), side="right").astype(jnp.int32)
    ref_logps = centred(part_keys[11], (SEQS,), 30.0, 192.0, (), jnp.float32)
    return {"tokens": tokens, "norm_gain": norm_gain, "final_gain": final_gain, "gate_weight": gate_weight, "up_weight": up_weight, "down_weight": down_weight, "picks": picks, "gates": gates, "target_rows": target_rows, "rest_lse": rest_lse, "segment_ids": segment_ids, "ref_logps": ref_logps}


EPS = 1e-06
BETA = 0.01

def rms_scale(rows, gain):
    values = rows.astype(jnp.float32)
    scale = lax.rsqrt(lax.optimization_barrier(jnp.mean(values * values, axis=-1, keepdims=True)) + EPS)
    return values * scale * gain.astype(jnp.float32)

def reference(tokens, norm_gain, final_gain, gate_weight, up_weight, down_weight, picks, gates, target_rows, rest_lse, segment_ids, ref_logps):
    spread = FFE // HID_DEV
    normed = rms_scale(tokens, norm_gain).astype(jnp.bfloat16)
    blocks = picks.reshape(N_EXPERT, TOK_DEV * TOPK)
    onehot = (blocks[:, :, None] == jnp.arange(EXPERTS, dtype=jnp.int32)[None, None, :]).astype(jnp.int32)
    slot = lax.optimization_barrier(jnp.sum((jnp.cumsum(onehot, axis=1) - onehot) * onehot, axis=2))
    place = jnp.arange(N_EXPERT, dtype=jnp.int32)[:, None] * CAP + slot
    row_ids = jnp.repeat(jnp.arange(TOKENS, dtype=jnp.int32), TOPK).reshape(N_EXPERT, TOK_DEV * TOPK)
    table = jnp.zeros((EXPERTS, N_EXPERT * CAP, D), jnp.bfloat16).at[blocks, place].set(normed[row_ids])

    def one_expert(index):
        rows_e = table[index]
        start = (index * FFE).astype(jnp.int32)
        w_gate = lax.dynamic_slice_in_dim(gate_weight, start, FFE, 1)
        w_up = lax.dynamic_slice_in_dim(up_weight, start, FFE, 1)
        w_down = lax.dynamic_slice_in_dim(down_weight, start, FFE, 0)
        gate = jnp.dot(rows_e, w_gate, preferred_element_type=jnp.float32)
        up = jnp.dot(rows_e, w_up, preferred_element_type=jnp.float32)
        hidden = (jax.nn.silu(gate) * up).astype(jnp.bfloat16)
        parts = jnp.einsum('rsh,shd->rsd', hidden.reshape(-1, spread, HID_DEV).astype(jnp.float32), w_down.reshape(spread, HID_DEV, D).astype(jnp.float32), precision=lax.Precision.HIGHEST)
        parts = lax.optimization_barrier(parts.astype(jnp.bfloat16))
        return lax.optimization_barrier(jnp.sum(parts.astype(jnp.float32), axis=1))
    expert_out = lax.map(one_expert, jnp.arange(EXPERTS, dtype=jnp.int32))
    picked = expert_out[blocks, place].reshape(TOKENS, TOPK, D)
    moe = lax.optimization_barrier(jnp.sum(gates[:, :, None] * picked, axis=1))
    stream = tokens.astype(jnp.float32) + moe
    final = rms_scale(stream, final_gain).astype(jnp.bfloat16)
    logit = lax.optimization_barrier(jnp.sum(final.astype(jnp.float32) * target_rows.astype(jnp.float32), axis=1))
    token_logp = logit - jnp.logaddexp(logit, rest_lse)
    sequence_logps = jax.ops.segment_sum(token_logp, segment_ids, num_segments=SEQS)
    margin = sequence_logps[0::2] - ref_logps[0::2] - (sequence_logps[1::2] - ref_logps[1::2])
    pair_loss = -jax.nn.log_sigmoid(BETA * margin)
    return (sequence_logps, pair_loss)
```

```python
import functools

import jax
import jax.numpy as jnp
from jax import lax
from jax.experimental import pallas as pl
from jax.experimental.pallas import tpu as pltpu
from jax.sharding import PartitionSpec as P

FFE = 2048
HID_DEV = 512
TOPK = 2

EPS = 1e-06
BETA = 0.01

F32 = jnp.float32
BF16 = jnp.bfloat16
VMEM_LIMIT = 56 * 1024 * 1024


def swap(value, mask):
    pairs = [(source, source ^ mask) for source in range(lax.axis_size("expert"))]
    return lax.ppermute(value, "expert", pairs)


def iota(shape, dim):
    return lax.broadcasted_iota(jnp.int32, shape, dim)


def routing(own, picks, rows):
    tokens = picks.shape[1]
    expert = jnp.bitwise_xor(own, iota((rows, tokens), 0))
    hit = [picks[k : k + 1, :] == expert for k in range(TOPK)]
    member = hit[0] | hit[1]
    earlier = (iota((tokens, tokens), 0) < iota((tokens, tokens), 1)).astype(BF16)
    slot = jnp.dot(member.astype(F32).astype(BF16), earlier, preferred_element_type=F32)
    slot = jnp.where(member, slot.astype(jnp.int32), -1)
    return hit, slot


def pack_kernel(own_ref, tokens_ref, gain_ref, picks_ref, *out_refs):
    capacity = out_refs[0].shape[0]
    tokens = tokens_ref.shape[0]
    values = tokens_ref[...].astype(F32)
    scale = lax.rsqrt(jnp.mean(values * values, axis=-1, keepdims=True) + EPS)
    normed = (values * scale * gain_ref[...]).astype(BF16)
    _, slot = routing(own_ref[0], picks_ref[...], max(8, len(out_refs)))
    place = iota((capacity, tokens), 0)
    for k, out_ref in enumerate(out_refs):
        chosen = (slot[k : k + 1, :] == place).astype(F32).astype(BF16)
        out_ref[...] = jnp.dot(chosen, normed, preferred_element_type=F32).astype(BF16)


def pack(own, tokens, gain, picks, experts, capacity):
    rows, width = tokens.shape
    smem = pl.BlockSpec(memory_space=pltpu.SMEM)
    vmem = pl.BlockSpec(memory_space=pltpu.VMEM)
    return pl.pallas_call(
        pack_kernel,
        out_shape=[jax.ShapeDtypeStruct((capacity, width), BF16)] * experts,
        in_specs=[smem, vmem, vmem, vmem],
        out_specs=[vmem] * experts,
        compiler_params=pltpu.CompilerParams(vmem_limit_bytes=VMEM_LIMIT),
        cost_estimate=pl.CostEstimate(
            flops=2 * experts * capacity * rows * width,
            bytes_accessed=2 * width * (rows + experts * capacity),
            transcendentals=rows,
        ),
        name="pack",
    )(own, tokens, gain, picks)


def expert_kernel(a_ref, b_ref, c_ref, d_ref, gate_ref, up_ref, down_ref, own_ref, other_ref, rows, total):
    step = pl.program_id(0)
    capacity = a_ref.shape[0]

    @pl.when(step == 0)
    def _():
        for n, ref in enumerate((a_ref, b_ref, c_ref, d_ref)):
            rows[n * capacity : (n + 1) * capacity, :] = ref[...]

    gate = jnp.dot(rows[...], gate_ref[...], preferred_element_type=F32)
    up = jnp.dot(rows[...], up_ref[...], preferred_element_type=F32)
    hidden = (jax.nn.silu(gate) * up).astype(BF16)
    part = jnp.dot(hidden, down_ref[...], preferred_element_type=F32)

    @pl.when(step == 0)
    def _():
        total[...] = part

    @pl.when(step == 1)
    def _():
        whole = (total[...] + part).astype(BF16)
        own_ref[...] = whole[: 2 * capacity]
        other_ref[...] = whole[2 * capacity :]


def expert_block(blocks, gate_weight, up_weight, down_weight):
    capacity, width = blocks[0].shape
    hidden = gate_weight.shape[1]
    half = hidden // 2
    row_spec = pl.BlockSpec((capacity, width), lambda h: (0, 0))
    out_spec = pl.BlockSpec((2 * capacity, width), lambda h: (0, 0))
    return pl.pallas_call(
        expert_kernel,
        out_shape=[jax.ShapeDtypeStruct((2 * capacity, width), BF16)] * 2,
        grid=(2,),
        in_specs=[row_spec] * 4
        + [pl.BlockSpec((width, half), lambda h: (0, h))] * 2
        + [pl.BlockSpec((half, width), lambda h: (h, 0))],
        out_specs=[out_spec] * 2,
        scratch_shapes=[
            pltpu.VMEM((4 * capacity, width), BF16),
            pltpu.VMEM((4 * capacity, width), F32),
        ],
        compiler_params=pltpu.CompilerParams(vmem_limit_bytes=VMEM_LIMIT),
        cost_estimate=pl.CostEstimate(
            flops=2 * 3 * 4 * capacity * width * hidden,
            bytes_accessed=2 * width * (3 * hidden + 8 * capacity),
            transcendentals=4 * capacity * hidden,
        ),
        name="expert_block",
    )(*blocks, gate_weight, up_weight, down_weight)


def score_kernel(own_ref, tokens_ref, gain_ref, picks_ref, gates_ref, target_ref, rest_ref, seg_ref, *refs):
    *block_refs, out_ref, stacked, stream = refs
    capacity = block_refs[0].shape[0]
    tokens, width = tokens_ref.shape
    experts = len(block_refs)
    for k, ref in enumerate(block_refs):
        stacked[k * capacity : (k + 1) * capacity, :] = ref[...]
    hit, slot = routing(own_ref[0], picks_ref[...], max(8, experts))
    weight = sum(jnp.where(hit[k], gates_ref[k : k + 1, :], 0.0) for k in range(TOPK))
    place = iota((capacity, tokens), 0)
    parts = [
        jnp.where(slot[k : k + 1, :] == place, weight[k : k + 1, :], 0.0) for k in range(experts)
    ]
    spread = jnp.concatenate(parts, axis=0)
    coarse = spread.astype(BF16)
    fine = (spread - coarse.astype(F32)).astype(BF16)
    chunk = width // 7 if width % 7 == 0 else width
    over_rows = (((0,), (0,)), ((), ()))
    squares = jnp.zeros((tokens, 1), F32)
    for start in range(0, width, chunk):
        cols = slice(start, start + chunk)
        rows = stacked[:, cols]
        moe = lax.dot_general(coarse, rows, over_rows, preferred_element_type=F32)
        moe = moe + lax.dot_general(fine, rows, over_rows, preferred_element_type=F32)
        value = tokens_ref[:, cols].astype(F32) + moe
        stream[:, cols] = value
        squares = squares + jnp.sum(value * value, axis=-1, keepdims=True)
    scale = lax.rsqrt(squares / width + EPS)
    logit = jnp.zeros((tokens, 1), F32)
    for start in range(0, width, chunk):
        cols = slice(start, start + chunk)
        final = (stream[:, cols] * scale * gain_ref[:, cols]).astype(BF16).astype(F32)
        logit = logit + jnp.sum(final * target_ref[:, cols].astype(F32), axis=-1, keepdims=True)
    turn = iota((tokens, tokens), 0) == iota((tokens, tokens), 1)
    logit = jnp.sum(jnp.where(turn, logit, 0.0), axis=0, keepdims=True)
    gap = rest_ref[...] - logit
    token_logp = -(jnp.maximum(gap, 0.0) + jnp.log1p(jnp.exp(-jnp.abs(gap))))
    sequences = out_ref.shape[1]
    inside = iota((sequences, tokens), 0) == seg_ref[...]
    sums = jnp.sum(jnp.where(inside, token_logp, 0.0), axis=1, keepdims=True)
    turn = iota((sequences, sequences), 0) == iota((sequences, sequences), 1)
    out_ref[...] = jnp.sum(jnp.where(turn, sums, 0.0), axis=0, keepdims=True)


def score(own, tokens, gain, picks, gates, target, rest, seg, blocks, sequences):
    rows, width = tokens.shape
    capacity = blocks[0].shape[0]
    experts = len(blocks)
    smem = pl.BlockSpec(memory_space=pltpu.SMEM)
    vmem = pl.BlockSpec(memory_space=pltpu.VMEM)
    return pl.pallas_call(
        score_kernel,
        out_shape=jax.ShapeDtypeStruct((1, sequences), F32),
        in_specs=[smem] + [vmem] * (7 + experts),
        out_specs=vmem,
        scratch_shapes=[
            pltpu.VMEM((experts * capacity, width), BF16),
            pltpu.VMEM((rows, width), F32),
        ],
        compiler_params=pltpu.CompilerParams(vmem_limit_bytes=VMEM_LIMIT),
        cost_estimate=pl.CostEstimate(
            flops=4 * experts * capacity * rows * width,
            bytes_accessed=2 * width * (2 * rows + experts * capacity),
            transcendentals=rows,
        ),
        name="score",
    )(own, tokens, gain, picks, gates, target, rest, seg, *blocks)


def add(first, second):
    return (first.astype(F32) + second.astype(F32)).astype(BF16)


def per_device(
    tokens,
    norm_gain,
    final_gain,
    gate_weight,
    up_weight,
    down_weight,
    picks,
    gates,
    target_rows,
    rest_lse,
    segment_ids,
    ref_logps,
):
    tok_rows = tokens.shape[0]
    spread = FFE // HID_DEV
    devices = lax.axis_size("expert")
    experts = devices // spread
    capacity = (tok_rows * TOPK * 5 // (experts * 4) + 3) // 4 * 4
    capacity = (capacity + 15) // 16 * 16
    own = (lax.axis_index("expert") // spread).astype(jnp.int32).reshape(1)
    picks_t = picks.T
    core, side = 1, 2

    sent = pack(own, tokens, norm_gain[None, :], picks_t, experts, capacity)
    near = [sent[0]] + [swap(sent[k], k * spread) for k in range(1, experts)]
    back = []
    for k in range(experts):
        far = swap(near[k], side)
        blocks = [near[k], far, swap(near[k], core), swap(far, core)]
        own_part, other_part = expert_block(blocks, gate_weight, up_weight, down_weight)
        both = add(own_part, swap(other_part, core))
        total = add(both[:capacity], swap(both[capacity:], side))
        back.append(total if k == 0 else swap(total, k * spread))
    local = score(
        own,
        tokens,
        final_gain[None, :],
        picks_t,
        gates.T,
        target_rows,
        rest_lse[None, :],
        segment_ids[None, :],
        back,
        ref_logps.shape[0],
    )
    mask = 1
    while mask < devices:
        local = local + swap(local, mask)
        mask *= 2
    sequence_logps = local[0]
    margin = sequence_logps[0::2] - ref_logps[0::2] - (sequence_logps[1::2] - ref_logps[1::2])
    pair_loss = -jax.nn.log_sigmoid(BETA * margin)
    return (sequence_logps, pair_loss)


def solution(mesh):
    placed = (
        P(("group", "expert"), None),
        P(),
        P(),
        P(None, "expert"),
        P(None, "expert"),
        P("expert", None),
        P(("group", "expert"), None),
        P(("group", "expert"), None),
        P(("group", "expert"), None),
        P(("group", "expert")),
        P(("group", "expert")),
        P("group"),
    )
    return jax.shard_map(
        per_device, mesh=mesh, in_specs=placed, out_specs=(P("group"), P("group")), check_vma=False
    )
```

```python
import functools

import jax
import jax.numpy as jnp
from jax import lax
from jax.experimental import pallas as pl
from jax.experimental.pallas import tpu as pltpu
from jax.sharding import PartitionSpec as P

FFE = 2048
HID_DEV = 512
TOPK = 2

EPS = 1e-06
BETA = 0.01

F32 = jnp.float32
BF16 = jnp.bfloat16
VMEM_LIMIT = 24 * 1024 * 1024


def swap(value, mask):
    pairs = [(source, source ^ mask) for source in range(lax.axis_size("expert"))]
    return lax.ppermute(value, "expert", pairs)


def iota(shape, dim):
    return lax.broadcasted_iota(jnp.int32, shape, dim)


def routing(own, picks, rows):
    tokens = picks.shape[1]
    expert = jnp.bitwise_xor(own, iota((rows, tokens), 0))
    hit = [picks[k : k + 1, :] == expert for k in range(TOPK)]
    member = hit[0] | hit[1]
    earlier = (iota((tokens, tokens), 0) < iota((tokens, tokens), 1)).astype(BF16)
    slot = jnp.dot(member.astype(F32).astype(BF16), earlier, preferred_element_type=F32)
    slot = jnp.where(member, slot.astype(jnp.int32), -1)
    return hit, slot


def pack_kernel(own_ref, tokens_ref, gain_ref, picks_ref, *out_refs):
    capacity = out_refs[0].shape[0]
    tokens = tokens_ref.shape[0]
    values = tokens_ref[...].astype(F32)
    scale = lax.rsqrt(jnp.mean(values * values, axis=-1, keepdims=True) + EPS)
    normed = (values * scale * gain_ref[...]).astype(BF16)
    _, slot = routing(own_ref[0], picks_ref[...], max(8, len(out_refs)))
    place = iota((capacity, tokens), 0)
    for k, out_ref in enumerate(out_refs):
        chosen = (slot[k : k + 1, :] == place).astype(F32).astype(BF16)
        out_ref[...] = jnp.dot(chosen, normed, preferred_element_type=F32).astype(BF16)


def pack(own, tokens, gain, picks, experts, capacity):
    rows, width = tokens.shape
    smem = pl.BlockSpec(memory_space=pltpu.SMEM)
    vmem = pl.BlockSpec(memory_space=pltpu.VMEM)
    return pl.pallas_call(
        pack_kernel,
        out_shape=[jax.ShapeDtypeStruct((capacity, width), BF16)] * experts,
        in_specs=[smem, vmem, vmem, vmem],
        out_specs=[vmem] * experts,
        compiler_params=pltpu.CompilerParams(vmem_limit_bytes=VMEM_LIMIT),
        cost_estimate=pl.CostEstimate(
            flops=2 * experts * capacity * rows * width,
            bytes_accessed=2 * width * (rows + experts * capacity),
            transcendentals=rows,
        ),
        name="pack",
    )(own, tokens, gain, picks)


def expert_kernel(a_ref, b_ref, c_ref, d_ref, gate_ref, up_ref, down_ref, own_ref, other_ref, rows):
    capacity = a_ref.shape[0]
    for n, ref in enumerate((a_ref, b_ref, c_ref, d_ref)):
        rows[n * capacity : (n + 1) * capacity, :] = ref[...]
    gate = jnp.dot(rows[...], gate_ref[...], preferred_element_type=F32)
    up = jnp.dot(rows[...], up_ref[...], preferred_element_type=F32)
    hidden = (jax.nn.silu(gate) * up).astype(BF16)
    width = down_ref.shape[1]
    chunk = width // 7
    for start in range(0, width, chunk):
        cols = slice(start, start + chunk)
        part = jnp.dot(hidden, down_ref[:, cols], preferred_element_type=F32).astype(BF16)
        own_ref[:, cols] = part[: 2 * capacity]
        other_ref[:, cols] = part[2 * capacity :]


def expert_block(blocks, gate_weight, up_weight, down_weight):
    capacity, width = blocks[0].shape
    hidden = gate_weight.shape[1]
    vmem = pl.BlockSpec(memory_space=pltpu.VMEM)
    return pl.pallas_call(
        expert_kernel,
        out_shape=[jax.ShapeDtypeStruct((2 * capacity, width), BF16)] * 2,
        in_specs=[vmem] * 7,
        out_specs=[vmem] * 2,
        scratch_shapes=[pltpu.VMEM((4 * capacity, width), BF16)],
        compiler_params=pltpu.CompilerParams(vmem_limit_bytes=VMEM_LIMIT),
        cost_estimate=pl.CostEstimate(
            flops=2 * 3 * 4 * capacity * width * hidden,
            bytes_accessed=2 * width * (3 * hidden + 8 * capacity),
            transcendentals=4 * capacity * hidden,
        ),
        name="expert_block",
    )(*blocks, gate_weight, up_weight, down_weight)


def score_kernel(own_ref, tokens_ref, gain_ref, picks_ref, gates_ref, target_ref, rest_ref, seg_ref, *refs):
    *block_refs, out_ref, stacked, stream = refs
    capacity = block_refs[0].shape[0]
    tokens, width = tokens_ref.shape
    experts = len(block_refs)
    for k, ref in enumerate(block_refs):
        stacked[k * capacity : (k + 1) * capacity, :] = ref[...]
    hit, slot = routing(own_ref[0], picks_ref[...], max(8, experts))
    weight = sum(jnp.where(hit[k], gates_ref[k : k + 1, :], 0.0) for k in range(TOPK))
    place = iota((capacity, tokens), 0)
    parts = [
        jnp.where(slot[k : k + 1, :] == place, weight[k : k + 1, :], 0.0) for k in range(experts)
    ]
    spread = jnp.concatenate(parts, axis=0)
    coarse = spread.astype(BF16)
    fine = (spread - coarse.astype(F32)).astype(BF16)
    chunk = width // 7 if width % 7 == 0 else width
    over_rows = (((0,), (0,)), ((), ()))
    squares = jnp.zeros((tokens, 1), F32)
    for start in range(0, width, chunk):
        cols = slice(start, start + chunk)
        rows = stacked[:, cols]
        moe = lax.dot_general(coarse, rows, over_rows, preferred_element_type=F32)
        moe = moe + lax.dot_general(fine, rows, over_rows, preferred_element_type=F32)
        value = tokens_ref[:, cols].astype(F32) + moe
        stream[:, cols] = value
        squares = squares + jnp.sum(value * value, axis=-1, keepdims=True)
    scale = lax.rsqrt(squares / width + EPS)
    logit = jnp.zeros((tokens, 1), F32)
    for start in range(0, width, chunk):
        cols = slice(start, start + chunk)
        final = (stream[:, cols] * scale * gain_ref[:, cols]).astype(BF16).astype(F32)
        logit = logit + jnp.sum(final * target_ref[:, cols].astype(F32), axis=-1, keepdims=True)
    turn = iota((tokens, tokens), 0) == iota((tokens, tokens), 1)
    logit = jnp.sum(jnp.where(turn, logit, 0.0), axis=0, keepdims=True)
    gap = rest_ref[...] - logit
    token_logp = -(jnp.maximum(gap, 0.0) + jnp.log1p(jnp.exp(-jnp.abs(gap))))
    sequences = out_ref.shape[1]
    inside = iota((sequences, tokens), 0) == seg_ref[...]
    sums = jnp.sum(jnp.where(inside, token_logp, 0.0), axis=1, keepdims=True)
    turn = iota((sequences, sequences), 0) == iota((sequences, sequences), 1)
    out_ref[...] = jnp.sum(jnp.where(turn, sums, 0.0), axis=0, keepdims=True)


def score(own, tokens, gain, picks, gates, target, rest, seg, blocks, sequences):
    rows, width = tokens.shape
    capacity = blocks[0].shape[0]
    experts = len(blocks)
    smem = pl.BlockSpec(memory_space=pltpu.SMEM)
    vmem = pl.BlockSpec(memory_space=pltpu.VMEM)
    return pl.pallas_call(
        score_kernel,
        out_shape=jax.ShapeDtypeStruct((1, sequences), F32),
        in_specs=[smem] + [vmem] * (7 + experts),
        out_specs=vmem,
        scratch_shapes=[
            pltpu.VMEM((experts * capacity, width), BF16),
            pltpu.VMEM((rows, width), F32),
        ],
        compiler_params=pltpu.CompilerParams(vmem_limit_bytes=VMEM_LIMIT),
        cost_estimate=pl.CostEstimate(
            flops=4 * experts * capacity * rows * width,
            bytes_accessed=2 * width * (2 * rows + experts * capacity),
            transcendentals=rows,
        ),
        name="score",
    )(own, tokens, gain, picks, gates, target, rest, seg, *blocks)


def after(*values):
    return lax.optimization_barrier(values)


def add(first, second):
    return (first.astype(F32) + second.astype(F32)).astype(BF16)


def per_device(
    tokens,
    norm_gain,
    final_gain,
    gate_weight,
    up_weight,
    down_weight,
    picks,
    gates,
    target_rows,
    rest_lse,
    segment_ids,
    ref_logps,
):
    tok_rows = tokens.shape[0]
    spread = FFE // HID_DEV
    devices = lax.axis_size("expert")
    experts = devices // spread
    capacity = (tok_rows * TOPK * 5 // (experts * 4) + 3) // 4 * 4
    capacity = (capacity + 15) // 16 * 16
    own = (lax.axis_index("expert") // spread).astype(jnp.int32).reshape(1)
    picks_t = picks.T
    core, side = 1, 2

    sent = pack(own, tokens, norm_gain[None, :], picks_t, experts, capacity)
    near = list(sent)
    for k in range(1, min(3, experts)):
        near[k] = swap(sent[k], k * spread)
    back = []
    for k in range(experts):
        far = swap(near[k], side)
        blocks = [near[k], far, swap(near[k], core), swap(far, core)]
        own_part, other_part = expert_block(blocks, gate_weight, up_weight, down_weight)
        if k + 3 < experts:
            near[k + 2], outgoing, own_part = after(near[k + 2], sent[k + 3], own_part)
            near[k + 3] = swap(outgoing, (k + 3) * spread)
        both = add(own_part, swap(other_part, core))
        total = add(both[:capacity], swap(both[capacity:], side))
        back.append(total if k == 0 else swap(total, k * spread))
    local = score(
        own,
        tokens,
        final_gain[None, :],
        picks_t,
        gates.T,
        target_rows,
        rest_lse[None, :],
        segment_ids[None, :],
        back,
        ref_logps.shape[0],
    )
    mask = 1
    while mask < devices:
        local = local + swap(local, mask)
        mask *= 2
    sequence_logps = local[0]
    margin = sequence_logps[0::2] - ref_logps[0::2] - (sequence_logps[1::2] - ref_logps[1::2])
    pair_loss = -jax.nn.log_sigmoid(BETA * margin)
    return (sequence_logps, pair_loss)


def solution(mesh):
    placed = (
        P(("group", "expert"), None),
        P(),
        P(),
        P(None, "expert"),
        P(None, "expert"),
        P("expert", None),
        P(("group", "expert"), None),
        P(("group", "expert"), None),
        P(("group", "expert"), None),
        P(("group", "expert")),
        P(("group", "expert")),
        P("group"),
    )
    return jax.shard_map(
        per_device, mesh=mesh, in_specs=placed, out_specs=(P("group"), P("group")), check_vma=False
    )
```

```python
import functools

import jax
import jax.numpy as jnp
from jax import lax
from jax.experimental import pallas as pl
from jax.experimental.pallas import tpu as pltpu
from jax.sharding import PartitionSpec as P

FFE = 2048
HID_DEV = 512
TOPK = 2

PIECE = 16

EPS = 1e-06
BETA = 0.01

F32 = jnp.float32
BF16 = jnp.bfloat16
VMEM_LIMIT = 20 * 1024 * 1024
COST = pl.CostEstimate(flops=1024, bytes_accessed=1024, transcendentals=0)


def swap(value, mask):
    pairs = [(source, source ^ mask) for source in range(lax.axis_size("expert"))]
    return lax.ppermute(value, "expert", pairs)


def iota(shape, dim):
    return lax.broadcasted_iota(jnp.int32, shape, dim)


def routing(own, picks, rows):
    tokens = picks.shape[1]
    expert = jnp.bitwise_xor(own, iota((rows, tokens), 0))
    hit = [picks[k : k + 1, :] == expert for k in range(TOPK)]
    member = hit[0] | hit[1]
    earlier = (iota((tokens, tokens), 0) < iota((tokens, tokens), 1)).astype(BF16)
    slot = jnp.dot(member.astype(F32).astype(BF16), earlier, preferred_element_type=F32)
    slot = jnp.where(member, slot.astype(jnp.int32), -1)
    return hit, slot


def pack_kernel(chunks, own_ref, tokens_ref, gain_ref, picks_ref, *out_refs):
    tokens = tokens_ref.shape[0]
    values = tokens_ref[...].astype(F32)
    scale = lax.rsqrt(jnp.mean(values * values, axis=-1, keepdims=True) + EPS)
    normed = (values * scale * gain_ref[...]).astype(BF16)
    _, slot = routing(own_ref[0], picks_ref[...], max(8, 1 + max(k for k, _, _ in chunks)))
    for (k, first, count), out_ref in zip(chunks, out_refs):
        place = first + iota((count, tokens), 0)
        chosen = (slot[k : k + 1, :] == place).astype(F32).astype(BF16)
        out_ref[...] = jnp.dot(chosen, normed, preferred_element_type=F32).astype(BF16)


def pack(own, tokens, gain, picks, chunks):
    rows, width = tokens.shape
    smem = pl.BlockSpec(memory_space=pltpu.SMEM)
    vmem = pl.BlockSpec(memory_space=pltpu.VMEM)
    return pl.pallas_call(
        functools.partial(pack_kernel, chunks),
        out_shape=[jax.ShapeDtypeStruct((count, width), BF16) for _, _, count in chunks],
        in_specs=[smem, vmem, vmem, vmem],
        out_specs=[vmem] * len(chunks),
        compiler_params=pltpu.CompilerParams(vmem_limit_bytes=VMEM_LIMIT),
        cost_estimate=COST,
        name="pack",
    )(own, tokens, gain, picks)


def expert_kernel(blocks, gate_ref, up_ref, down_ref, *refs):
    block_refs, out_refs, rows = refs[:blocks], refs[blocks:-1], refs[-1]
    first = 0
    for ref in block_refs:
        rows[first : first + ref.shape[0], :] = ref[...]
        first += ref.shape[0]
    gate = jnp.dot(rows[...], gate_ref[...], preferred_element_type=F32)
    up = jnp.dot(rows[...], up_ref[...], preferred_element_type=F32)
    hidden = (jax.nn.silu(gate) * up).astype(BF16)
    width = down_ref.shape[1]
    chunk = width // 7 if width % 7 == 0 else width
    for start in range(0, width, chunk):
        cols = slice(start, start + chunk)
        part = jnp.dot(hidden, down_ref[:, cols], preferred_element_type=F32).astype(BF16)
        first = 0
        for out_ref in out_refs:
            out_ref[:, cols] = part[first : first + out_ref.shape[0]]
            first += out_ref.shape[0]


def expert_block(blocks, gate_weight, up_weight, down_weight):
    count, width = blocks[0].shape
    outs = [count] * 3 + [PIECE] * (count // PIECE)
    vmem = pl.BlockSpec(memory_space=pltpu.VMEM)
    return pl.pallas_call(
        functools.partial(expert_kernel, len(blocks)),
        out_shape=[jax.ShapeDtypeStruct((rows, width), BF16) for rows in outs],
        in_specs=[vmem] * (3 + len(blocks)),
        out_specs=[vmem] * len(outs),
        scratch_shapes=[pltpu.VMEM((4 * count, width), BF16)],
        compiler_params=pltpu.CompilerParams(vmem_limit_bytes=VMEM_LIMIT),
        cost_estimate=COST,
        name="expert_block",
    )(gate_weight, up_weight, down_weight, *blocks)


def score_kernel(capacity, own_ref, tokens_ref, gain_ref, picks_ref, gates_ref, target_ref, rest_ref, seg_ref, *refs):
    *block_refs, out_ref, stacked, stream = refs
    tokens, width = tokens_ref.shape
    experts = stacked.shape[0] // capacity
    first = 0
    for ref in block_refs:
        stacked[first : first + ref.shape[0], :] = ref[...]
        first += ref.shape[0]
    hit, slot = routing(own_ref[0], picks_ref[...], max(8, experts))
    weight = sum(jnp.where(hit[k], gates_ref[k : k + 1, :], 0.0) for k in range(TOPK))
    place = iota((capacity, tokens), 0)
    parts = [
        jnp.where(slot[k : k + 1, :] == place, weight[k : k + 1, :], 0.0) for k in range(experts)
    ]
    spread = jnp.concatenate(parts, axis=0)
    coarse = spread.astype(BF16)
    fine = (spread - coarse.astype(F32)).astype(BF16)
    chunk = width // 7 if width % 7 == 0 else width
    over_rows = (((0,), (0,)), ((), ()))
    squares = jnp.zeros((tokens, 1), F32)
    for start in range(0, width, chunk):
        cols = slice(start, start + chunk)
        rows = stacked[:, cols]
        moe = lax.dot_general(coarse, rows, over_rows, preferred_element_type=F32)
        moe = moe + lax.dot_general(fine, rows, over_rows, preferred_element_type=F32)
        value = tokens_ref[:, cols].astype(F32) + moe
        stream[:, cols] = value
        squares = squares + jnp.sum(value * value, axis=-1, keepdims=True)
    scale = lax.rsqrt(squares / width + EPS)
    logit = jnp.zeros((tokens, 1), F32)
    for start in range(0, width, chunk):
        cols = slice(start, start + chunk)
        final = (stream[:, cols] * scale * gain_ref[:, cols]).astype(BF16).astype(F32)
        logit = logit + jnp.sum(final * target_ref[:, cols].astype(F32), axis=-1, keepdims=True)
    turn = iota((tokens, tokens), 0) == iota((tokens, tokens), 1)
    logit = jnp.sum(jnp.where(turn, logit, 0.0), axis=0, keepdims=True)
    gap = rest_ref[...] - logit
    token_logp = -(jnp.maximum(gap, 0.0) + jnp.log1p(jnp.exp(-jnp.abs(gap))))
    sequences = out_ref.shape[1]
    inside = iota((sequences, tokens), 0) == seg_ref[...]
    sums = jnp.sum(jnp.where(inside, token_logp, 0.0), axis=1, keepdims=True)
    turn = iota((sequences, sequences), 0) == iota((sequences, sequences), 1)
    out_ref[...] = jnp.sum(jnp.where(turn, sums, 0.0), axis=0, keepdims=True)


def score(own, tokens, gain, picks, gates, target, rest, seg, blocks, capacity, sequences):
    rows, width = tokens.shape
    slots = sum(block.shape[0] for block in blocks)
    smem = pl.BlockSpec(memory_space=pltpu.SMEM)
    vmem = pl.BlockSpec(memory_space=pltpu.VMEM)
    return pl.pallas_call(
        functools.partial(score_kernel, capacity),
        out_shape=jax.ShapeDtypeStruct((1, sequences), F32),
        in_specs=[smem] + [vmem] * (7 + len(blocks)),
        out_specs=vmem,
        scratch_shapes=[
            pltpu.VMEM((slots, width), BF16),
            pltpu.VMEM((rows, width), F32),
        ],
        compiler_params=pltpu.CompilerParams(vmem_limit_bytes=VMEM_LIMIT),
        cost_estimate=COST,
        name="score",
    )(own, tokens, gain, picks, gates, target, rest, seg, *blocks)


class Order:
    def __init__(self, token):
        self.token = token

    def mark(self, *values):
        *values, self.token = lax.optimization_barrier((*values, self.token))
        return values

    def mark_one(self, value):
        return self.mark(value)[0]

    def late(self, value):
        return lax.optimization_barrier((value, self.token))[0]


def cut_kernel(whole_ref, *refs):
    for n, ref in enumerate(refs):
        ref[...] = whole_ref[n * PIECE : (n + 1) * PIECE, :]


def cut(whole):
    rows, width = whole.shape
    vmem = pl.BlockSpec(memory_space=pltpu.VMEM)
    return pl.pallas_call(
        cut_kernel,
        out_shape=[jax.ShapeDtypeStruct((PIECE, width), BF16)] * (rows // PIECE),
        in_specs=[vmem],
        out_specs=[vmem] * (rows // PIECE),
        compiler_params=pltpu.CompilerParams(vmem_limit_bytes=VMEM_LIMIT),
        cost_estimate=COST,
        name="cut",
    )(whole)


def total_kernel(*refs):
    *refs, out_ref = refs
    out_ref[...] = sum(ref[...].astype(F32) for ref in refs).astype(BF16)


def joined_kernel(whole_ref, *refs):
    *refs, out_ref = refs
    for n, ref in enumerate(refs):
        rows = slice(n * PIECE, (n + 1) * PIECE)
        out_ref[rows, :] = (whole_ref[rows, :].astype(F32) + ref[...].astype(F32)).astype(BF16)


def total(*values, kernel=total_kernel):
    vmem = pl.BlockSpec(memory_space=pltpu.VMEM)
    return pl.pallas_call(
        kernel,
        out_shape=jax.ShapeDtypeStruct(values[0].shape, BF16),
        in_specs=[vmem] * len(values),
        out_specs=vmem,
        compiler_params=pltpu.CompilerParams(vmem_limit_bytes=VMEM_LIMIT),
        cost_estimate=COST,
        name="total",
    )(*values)


def per_device(
    tokens,
    norm_gain,
    final_gain,
    gate_weight,
    up_weight,
    down_weight,
    picks,
    gates,
    target_rows,
    rest_lse,
    segment_ids,
    ref_logps,
):
    tok_rows = tokens.shape[0]
    spread = FFE // HID_DEV
    devices = lax.axis_size("expert")
    experts = devices // spread
    capacity = (tok_rows * TOPK * 5 // (experts * 4) + 3) // 4 * 4
    capacity = (capacity + 15) // 16 * 16
    own = (lax.axis_index("expert") // spread).astype(jnp.int32).reshape(1)
    picks_t = picks.T
    core, side = 1, 2
    weights = (gate_weight, up_weight, down_weight)

    half = (capacity // 2 + 15) // 16 * 16 if capacity >= 64 else capacity
    cuts = [(first, min(half, capacity - first)) for first in range(0, capacity, half)]
    chunks = [(k, 0, capacity) for k in range(min(2, experts))]
    near_count = len(chunks)
    chunks += [(k, first, count) for k in range(2, experts) for first, count in cuts]
    travelling = list(range(near_count, len(chunks)))
    sent = pack(own, tokens, norm_gain[None, :], picks_t, tuple(chunks))
    order = Order(own)
    near, far, beside, across = list(sent), {}, {}, {}
    mine, theirs, other_mine, other_theirs, back = {}, {}, {}, {}, {}

    def leave(n):
        near[n] = swap(order.late(near[n]), chunks[n][0] * spread)

    def arrive(n):
        near[n] = order.mark_one(near[n])

    def share(n):
        far[n], beside[n] = swap(order.late(near[n]), side), swap(order.late(near[n]), core)

    def meet(n):
        far[n] = order.mark_one(far[n])
        pieces = order.mark(*cut(far[n])) if n in travelling else [far[n]]
        across[n] = [swap(piece, core) for piece in pieces]

    def work(n):
        rows = [order.late(rows) for rows in (near[n], far[n], beside[n], *across[n])]
        mine[n], theirs[n], other, *pieces = order.mark(*expert_block(rows, *weights))
        other_theirs[n] = [swap(piece, core) for piece in pieces]
        other_mine[n] = swap(other, core)

    def half_way(n):
        pieces = order.mark(*other_theirs[n])
        theirs[n] = order.mark_one(total(theirs[n], *pieces, kernel=joined_kernel))

    def cross(n):
        theirs[n] = swap(order.late(theirs[n]), side)

    def home(n):
        back[n] = order.mark_one(total(mine[n], other_mine[n], order.mark_one(theirs[n])))

    def leave_back(n):
        back[n] = swap(order.late(back[n]), chunks[n][0] * spread)

    def arrive_back(n):
        back[n] = order.mark_one(back[n])

    far_count = len(travelling)
    begin_back = max(far_count, 4)
    steps = begin_back + far_count

    def at(step):
        return travelling[step] if 0 <= step < far_count else None

    for step in range(steps):
        out, shared, worked, crossing, back_now = (
            at(step), at(step - 1), at(step - 2), at(step - 3), at(step - begin_back)
        )
        if out is not None:
            leave(out)
        if back_now is not None:
            leave_back(back_now)
        if shared is not None:
            share(shared)
        if step == 0:
            share(0)
            leave(1)
            meet(0)
        if worked is not None:
            work(worked)
        if shared is not None:
            meet(shared)
        if worked is not None:
            half_way(worked)
            cross(worked)
        if crossing is not None:
            home(crossing)
        if step == 1:
            arrive(1)
            share(1)
        if step == 2:
            meet(1)
        if step == 3:
            work(0)
        if step == 4:
            work(1)
        if step == steps - 3:
            half_way(1)
            cross(1)
        if step == steps - 2:
            half_way(0)
            cross(0)
            home(1)
            leave_back(1)
        if step == steps - 1:
            home(0)
        if out is not None:
            arrive(out)
        if back_now is not None:
            arrive_back(back_now)
    blocks = [back[n] for n in range(len(chunks))]
    local = score(
        own,
        tokens,
        final_gain[None, :],
        picks_t,
        gates.T,
        target_rows,
        rest_lse[None, :],
        segment_ids[None, :],
        blocks,
        capacity,
        ref_logps.shape[0],
    )
    mask = 1
    while mask < devices:
        local = local + swap(local, mask)
        mask *= 2
    sequence_logps = local[0]
    margin = sequence_logps[0::2] - ref_logps[0::2] - (sequence_logps[1::2] - ref_logps[1::2])
    pair_loss = -jax.nn.log_sigmoid(BETA * margin)
    return (sequence_logps, pair_loss)


def solution(mesh):
    placed = (
        P(("group", "expert"), None),
        P(),
        P(),
        P(None, "expert"),
        P(None, "expert"),
        P("expert", None),
        P(("group", "expert"), None),
        P(("group", "expert"), None),
        P(("group", "expert"), None),
        P(("group", "expert")),
        P(("group", "expert")),
        P("group"),
    )
    return jax.shard_map(
        per_device, mesh=mesh, in_specs=placed, out_specs=(P("group"), P("group")), check_vma=False
    )
```

```python
import functools

import jax
import jax.numpy as jnp
from jax import lax
from jax.experimental import pallas as pl
from jax.experimental.pallas import tpu as pltpu
from jax.sharding import PartitionSpec as P

FFE = 2048
HID_DEV = 512
TOPK = 2

EPS = 1e-06
BETA = 0.01

F32 = jnp.float32
BF16 = jnp.bfloat16
VMEM_LIMIT = 20 * 1024 * 1024
COST = pl.CostEstimate(flops=1024, bytes_accessed=1024, transcendentals=0)


def swap(value, mask):
    pairs = [(source, source ^ mask) for source in range(lax.axis_size("expert"))]
    return lax.ppermute(value, "expert", pairs)


def iota(shape, dim):
    return lax.broadcasted_iota(jnp.int32, shape, dim)


def routing(own, picks, rows):
    tokens = picks.shape[1]
    expert = jnp.bitwise_xor(own, iota((rows, tokens), 0))
    hit = [picks[k : k + 1, :] == expert for k in range(TOPK)]
    member = hit[0] | hit[1]
    earlier = (iota((tokens, tokens), 0) < iota((tokens, tokens), 1)).astype(BF16)
    slot = jnp.dot(member.astype(F32).astype(BF16), earlier, preferred_element_type=F32)
    slot = jnp.where(member, slot.astype(jnp.int32), -1)
    return hit, slot


def pack_kernel(chunks, own_ref, tokens_ref, gain_ref, picks_ref, *out_refs):
    tokens = tokens_ref.shape[0]
    values = tokens_ref[...].astype(F32)
    scale = lax.rsqrt(jnp.mean(values * values, axis=-1, keepdims=True) + EPS)
    normed = (values * scale * gain_ref[...]).astype(BF16)
    _, slot = routing(own_ref[0], picks_ref[...], max(8, 1 + max(k for k, _, _ in chunks)))
    for (k, first, count), out_ref in zip(chunks, out_refs):
        place = first + iota((count, tokens), 0)
        chosen = (slot[k : k + 1, :] == place).astype(F32).astype(BF16)
        out_ref[...] = jnp.dot(chosen, normed, preferred_element_type=F32).astype(BF16)


def pack(own, tokens, gain, picks, chunks):
    rows, width = tokens.shape
    smem = pl.BlockSpec(memory_space=pltpu.SMEM)
    vmem = pl.BlockSpec(memory_space=pltpu.VMEM)
    return pl.pallas_call(
        functools.partial(pack_kernel, chunks),
        out_shape=[jax.ShapeDtypeStruct((count, width), BF16) for _, _, count in chunks],
        in_specs=[smem, vmem, vmem, vmem],
        out_specs=[vmem] * len(chunks),
        compiler_params=pltpu.CompilerParams(vmem_limit_bytes=VMEM_LIMIT),
        cost_estimate=COST,
        name="pack",
    )(own, tokens, gain, picks)


def expert_kernel(near_ref, far_ref, *refs):
    weight_refs, (mine_ref, theirs_ref, rows) = refs[:-3], refs[-3:]
    count = near_ref.shape[0]
    rows[:count, :] = near_ref[...]
    rows[count:, :] = far_ref[...]
    halves = [weight_refs[n : n + 3] for n in range(0, len(weight_refs), 3)]
    hidden = []
    for gate_ref, up_ref, _ in halves:
        gate = jnp.dot(rows[...], gate_ref[...], preferred_element_type=F32)
        up = jnp.dot(rows[...], up_ref[...], preferred_element_type=F32)
        hidden.append((jax.nn.silu(gate) * up).astype(BF16))
    width = near_ref.shape[1]
    chunk = width // 7 if width % 7 == 0 else width
    for start in range(0, width, chunk):
        cols = slice(start, start + chunk)
        part = sum(
            jnp.dot(value, down_ref[:, cols], preferred_element_type=F32)
            for value, (_, _, down_ref) in zip(hidden, halves)
        ).astype(BF16)
        mine_ref[:, cols] = part[:count]
        theirs_ref[:, cols] = part[count:]


def expert_block(near, far, weights):
    count, width = near.shape
    vmem = pl.BlockSpec(memory_space=pltpu.VMEM)
    return pl.pallas_call(
        expert_kernel,
        out_shape=[jax.ShapeDtypeStruct((count, width), BF16)] * 2,
        in_specs=[vmem] * (2 + len(weights)),
        out_specs=[vmem] * 2,
        scratch_shapes=[pltpu.VMEM((2 * count, width), BF16)],
        compiler_params=pltpu.CompilerParams(vmem_limit_bytes=VMEM_LIMIT),
        cost_estimate=COST,
        name="expert_block",
    )(near, far, *weights)


def score_kernel(capacity, own_ref, tokens_ref, gain_ref, picks_ref, gates_ref, target_ref, rest_ref, seg_ref, *refs):
    *block_refs, out_ref, stacked, stream = refs
    tokens, width = tokens_ref.shape
    experts = stacked.shape[0] // capacity
    first = 0
    for ref in block_refs:
        stacked[first : first + ref.shape[0], :] = ref[...]
        first += ref.shape[0]
    hit, slot = routing(own_ref[0], picks_ref[...], max(8, experts))
    weight = sum(jnp.where(hit[k], gates_ref[k : k + 1, :], 0.0) for k in range(TOPK))
    place = iota((capacity, tokens), 0)
    parts = [
        jnp.where(slot[k : k + 1, :] == place, weight[k : k + 1, :], 0.0) for k in range(experts)
    ]
    spread = jnp.concatenate(parts, axis=0)
    coarse = spread.astype(BF16)
    fine = (spread - coarse.astype(F32)).astype(BF16)
    chunk = width // 7 if width % 7 == 0 else width
    over_rows = (((0,), (0,)), ((), ()))
    squares = jnp.zeros((tokens, 1), F32)
    for start in range(0, width, chunk):
        cols = slice(start, start + chunk)
        rows = stacked[:, cols]
        moe = lax.dot_general(coarse, rows, over_rows, preferred_element_type=F32)
        moe = moe + lax.dot_general(fine, rows, over_rows, preferred_element_type=F32)
        value = tokens_ref[:, cols].astype(F32) + moe
        stream[:, cols] = value
        squares = squares + jnp.sum(value * value, axis=-1, keepdims=True)
    scale = lax.rsqrt(squares / width + EPS)
    logit = jnp.zeros((tokens, 1), F32)
    for start in range(0, width, chunk):
        cols = slice(start, start + chunk)
        final = (stream[:, cols] * scale * gain_ref[:, cols]).astype(BF16).astype(F32)
        logit = logit + jnp.sum(final * target_ref[:, cols].astype(F32), axis=-1, keepdims=True)
    turn = iota((tokens, tokens), 0) == iota((tokens, tokens), 1)
    logit = jnp.sum(jnp.where(turn, logit, 0.0), axis=0, keepdims=True)
    gap = rest_ref[...] - logit
    token_logp = -(jnp.maximum(gap, 0.0) + jnp.log1p(jnp.exp(-jnp.abs(gap))))
    sequences = out_ref.shape[1]
    inside = iota((sequences, tokens), 0) == seg_ref[...]
    sums = jnp.sum(jnp.where(inside, token_logp, 0.0), axis=1, keepdims=True)
    turn = iota((sequences, sequences), 0) == iota((sequences, sequences), 1)
    out_ref[...] = jnp.sum(jnp.where(turn, sums, 0.0), axis=0, keepdims=True)


def score(own, tokens, gain, picks, gates, target, rest, seg, blocks, capacity, sequences):
    rows, width = tokens.shape
    slots = sum(block.shape[0] for block in blocks)
    smem = pl.BlockSpec(memory_space=pltpu.SMEM)
    vmem = pl.BlockSpec(memory_space=pltpu.VMEM)
    return pl.pallas_call(
        functools.partial(score_kernel, capacity),
        out_shape=jax.ShapeDtypeStruct((1, sequences), F32),
        in_specs=[smem] + [vmem] * (7 + len(blocks)),
        out_specs=vmem,
        scratch_shapes=[
            pltpu.VMEM((slots, width), BF16),
            pltpu.VMEM((rows, width), F32),
        ],
        compiler_params=pltpu.CompilerParams(vmem_limit_bytes=VMEM_LIMIT),
        cost_estimate=COST,
        name="score",
    )(own, tokens, gain, picks, gates, target, rest, seg, *blocks)


class Order:
    def __init__(self, token):
        self.token = token

    def mark(self, *values):
        *values, self.token = lax.optimization_barrier((*values, self.token))
        return values

    def mark_one(self, value):
        return self.mark(value)[0]

    def late(self, value):
        return lax.optimization_barrier((value, self.token))[0]


def hold_kernel(own_ref, *refs):
    *_, out_ref = refs
    out_ref[0] = own_ref[0]


def hold(own, arrays):
    smem = pl.BlockSpec(memory_space=pltpu.SMEM)
    vmem = pl.BlockSpec(memory_space=pltpu.VMEM)
    return pl.pallas_call(
        hold_kernel,
        out_shape=jax.ShapeDtypeStruct((1,), jnp.int32),
        in_specs=[smem] + [vmem] * len(arrays),
        out_specs=smem,
        compiler_params=pltpu.CompilerParams(vmem_limit_bytes=VMEM_LIMIT),
        cost_estimate=COST,
        name="hold",
    )(own, *arrays)


def total_kernel(*refs):
    *refs, out_ref = refs
    out_ref[...] = sum(ref[...].astype(F32) for ref in refs).astype(BF16)


def total(*values):
    vmem = pl.BlockSpec(memory_space=pltpu.VMEM)
    return pl.pallas_call(
        total_kernel,
        out_shape=jax.ShapeDtypeStruct(values[0].shape, BF16),
        in_specs=[vmem] * len(values),
        out_specs=vmem,
        compiler_params=pltpu.CompilerParams(vmem_limit_bytes=VMEM_LIMIT),
        cost_estimate=COST,
        name="total",
    )(*values)


def per_device(
    tokens,
    norm_gain,
    final_gain,
    gate_weight,
    up_weight,
    down_weight,
    picks,
    gates,
    target_rows,
    rest_lse,
    segment_ids,
    ref_logps,
):
    tok_rows = tokens.shape[0]
    spread = FFE // HID_DEV
    devices = lax.axis_size("expert")
    experts = devices // spread
    capacity = (tok_rows * TOPK * 5 // (experts * 4) + 3) // 4 * 4
    capacity = (capacity + 15) // 16 * 16
    own = (lax.axis_index("expert") // spread).astype(jnp.int32).reshape(1)
    picks_t = picks.T
    core, side = 1, 2
    weights = [gate_weight, up_weight, down_weight]
    weights += [swap(weight, core) for weight in weights]

    half = capacity // 2 // 16 * 16 if capacity >= 64 else capacity
    cuts = [(0, half), (half, capacity - half)] if half < capacity else [(0, capacity)]
    chunks = [(k, 0, capacity) for k in range(min(2, experts))]
    travelling = len(chunks)
    chunks += [(k, first, count) for k in range(2, experts) for first, count in cuts]
    sent = pack(own, tokens, norm_gain[None, :], picks_t, tuple(chunks))
    order = Order(own)
    near, far, mine, theirs, back = list(sent), {}, {}, {}, {}

    def leave(n):
        near[n] = swap(order.late(near[n]), chunks[n][0] * spread)

    def arrive(n):
        near[n] = order.mark_one(near[n])

    def share(n):
        far[n] = swap(order.late(near[n]), side)

    def meet(n):
        far[n] = order.mark_one(far[n])

    def work(n):
        mine[n], part = order.mark(*expert_block(order.late(near[n]), order.late(far[n]), weights))
        theirs[n] = swap(part, side)

    def home(n):
        back[n] = order.mark_one(total(mine[n], order.mark_one(theirs[n])))

    def leave_back(n):
        back[n] = swap(order.late(back[n]), chunks[n][0] * spread)

    def arrive_back(n):
        back[n] = order.mark_one(back[n])

    count = len(chunks) - travelling
    begin_back = max(count, 4)
    steps = max(begin_back + count, 8)
    for step in range(steps):
        out, shared, worked, crossing, coming = (
            travelling + step - late if 0 <= step - late < count else None
            for late in (0, 1, 2, 3, begin_back)
        )
        if out is not None:
            leave(out)
        if coming is not None:
            leave_back(coming)
        if step == 0:
            share(0)
            own = order.mark_one(hold(order.late(own), weights[:3]))
        if step == 1:
            meet(0)
        if shared is not None:
            share(shared)
        if worked is not None:
            work(worked)
        if step == 2 and experts > 1:
            arrive(1)
            share(1)
        if step == steps - 4 and experts > 1:
            meet(1)
            work(1)
        if shared is not None:
            meet(shared)
        if crossing is not None:
            home(crossing)
        if step == 1 and experts > 1:
            leave(1)
        if step == steps - 3:
            if experts > 1:
                home(1)
                leave_back(1)
            work(0)
        if step == steps - 1:
            home(0)
        if out is not None:
            arrive(out)
        if coming is not None:
            arrive_back(coming)
    blocks = [back[n] for n in range(len(chunks))]
    local = score(
        own,
        tokens,
        final_gain[None, :],
        picks_t,
        gates.T,
        target_rows,
        rest_lse[None, :],
        segment_ids[None, :],
        blocks,
        capacity,
        ref_logps.shape[0],
    )
    mask = 1
    while mask < devices:
        local = local + swap(local, mask)
        mask *= 2
    sequence_logps = local[0]
    margin = sequence_logps[0::2] - ref_logps[0::2] - (sequence_logps[1::2] - ref_logps[1::2])
    pair_loss = -jax.nn.log_sigmoid(BETA * margin)
    return (sequence_logps, pair_loss)


def solution(mesh):
    placed = (
        P(("group", "expert"), None),
        P(),
        P(),
        P(None, "expert"),
        P(None, "expert"),
        P("expert", None),
        P(("group", "expert"), None),
        P(("group", "expert"), None),
        P(("group", "expert"), None),
        P(("group", "expert")),
        P(("group", "expert")),
        P("group"),
    )
    return jax.shard_map(
        per_device, mesh=mesh, in_specs=placed, out_specs=(P("group"), P("group")), check_vma=False
    )
```

```python
import functools

import jax
import jax.numpy as jnp
from jax import lax
from jax.experimental import pallas as pl
from jax.experimental.pallas import tpu as pltpu
from jax.sharding import PartitionSpec as P

FFE = 2048
HID_DEV = 512
TOPK = 2

EPS = 1e-06
BETA = 0.01

F32 = jnp.float32
BF16 = jnp.bfloat16
VMEM_LIMIT = 10 * 1024 * 1024
COST = pl.CostEstimate(flops=1024, bytes_accessed=1024, transcendentals=0)


def swap(value, mask):
    pairs = [(source, source ^ mask) for source in range(lax.axis_size("expert"))]
    return lax.ppermute(value, "expert", pairs)


def iota(shape, dim):
    return lax.broadcasted_iota(jnp.int32, shape, dim)


def routing(own, picks, rows):
    tokens = picks.shape[1]
    expert = jnp.bitwise_xor(own, iota((rows, tokens), 0))
    hit = [picks[k : k + 1, :] == expert for k in range(TOPK)]
    member = hit[0] | hit[1]
    earlier = (iota((tokens, tokens), 0) < iota((tokens, tokens), 1)).astype(BF16)
    slot = jnp.dot(member.astype(F32).astype(BF16), earlier, preferred_element_type=F32)
    slot = jnp.where(member, slot.astype(jnp.int32), -1)
    return hit, slot


def pack_kernel(
    chunks, own_ref, tokens_ref, gain_ref, picks_ref, gate_ref, up_ref, down_ref, *refs
):
    *out_refs, weights_ref, arrived = refs
    width, hidden = gate_ref.shape
    sources = [gate_ref, up_ref]
    sources += [down_ref.at[:, pl.ds(first, hidden)] for first in range(0, width, hidden)]
    copies, first = [], 0
    for n, source in enumerate(sources):
        there = weights_ref.at[pl.ds(first, source.shape[0]), :]
        copies.append(pltpu.make_async_copy(source, there, arrived.at[n]))
        first += source.shape[0]
    for copy in copies:
        copy.start()
    tokens = tokens_ref.shape[0]
    values = tokens_ref[...].astype(F32)
    scale = lax.rsqrt(jnp.mean(values * values, axis=-1, keepdims=True) + EPS)
    normed = (values * scale * gain_ref[...]).astype(BF16)
    _, slot = routing(own_ref[0], picks_ref[...], max(8, 1 + max(k for k, _, _ in chunks)))
    for (k, first, count), out_ref in zip(chunks, out_refs):
        place = first + iota((count, tokens), 0)
        chosen = (slot[k : k + 1, :] == place).astype(F32).astype(BF16)
        out_ref[...] = jnp.dot(chosen, normed, preferred_element_type=F32).astype(BF16)
    for copy in copies:
        copy.wait()


def pack(own, tokens, gain, picks, weights, chunks):
    width, hidden = weights[0].shape
    smem = pl.BlockSpec(memory_space=pltpu.SMEM)
    vmem = pl.BlockSpec(memory_space=pltpu.VMEM)
    anywhere = pl.BlockSpec(memory_space=pltpu.HBM)
    shapes = [(count, width) for _, _, count in chunks] + [(3 * width, hidden)]
    return pl.pallas_call(
        functools.partial(pack_kernel, chunks),
        out_shape=[jax.ShapeDtypeStruct(shape, BF16) for shape in shapes],
        in_specs=[smem, vmem, vmem, vmem] + [anywhere] * 3,
        out_specs=[vmem] * len(shapes),
        scratch_shapes=[pltpu.SemaphoreType.DMA((2 + width // hidden,))],
        compiler_params=pltpu.CompilerParams(vmem_limit_bytes=VMEM_LIMIT),
        cost_estimate=COST,
        name="pack",
    )(own, tokens, gain, picks, *(pltpu.with_memory_space_constraint(w, pltpu.HBM) for w in weights))


def expert_kernel(blocks, slices, *refs):
    block_refs, weight_refs = refs[:blocks], refs[blocks : blocks + slices]
    out_refs, rows = refs[blocks + slices : -1], refs[-1]
    first = 0
    for ref in block_refs:
        rows[first : first + ref.shape[0], :] = ref[...]
        first += ref.shape[0]
    width = rows.shape[1]
    size = weight_refs[0].shape[1]
    hidden = []
    for ref in weight_refs:
        gate = jnp.dot(rows[...], ref[:width, :], preferred_element_type=F32)
        up = jnp.dot(rows[...], ref[width : 2 * width, :], preferred_element_type=F32)
        hidden.append((jax.nn.silu(gate) * up).astype(BF16))
    for start in range(0, width, size):
        part = sum(
            jnp.dot(value, ref[pl.ds(2 * width + start, size), :], preferred_element_type=F32)
            for value, ref in zip(hidden, weight_refs)
        ).astype(BF16)
        first = 0
        for ref in out_refs:
            ref[:, start : start + size] = part[first : first + ref.shape[0]]
            first += ref.shape[0]


def expert_block(blocks, weights, outs):
    width = blocks[0].shape[1]
    vmem = pl.BlockSpec(memory_space=pltpu.VMEM)
    return pl.pallas_call(
        functools.partial(expert_kernel, len(blocks), len(weights)),
        out_shape=[jax.ShapeDtypeStruct((rows, width), BF16) for rows in outs],
        in_specs=[vmem] * (len(blocks) + len(weights)),
        out_specs=[vmem] * len(outs),
        scratch_shapes=[pltpu.VMEM((sum(outs), width), BF16)],
        compiler_params=pltpu.CompilerParams(vmem_limit_bytes=VMEM_LIMIT),
        cost_estimate=COST,
        name="expert_block",
    )(*blocks, *weights)


def score_kernel(capacity, own_ref, tokens_ref, gain_ref, picks_ref, gates_ref, target_ref, rest_ref, seg_ref, *refs):
    *block_refs, out_ref, stacked, stream = refs
    tokens, width = tokens_ref.shape
    experts = stacked.shape[0] // capacity
    first = 0
    for ref in block_refs:
        stacked[first : first + ref.shape[0], :] = ref[...]
        first += ref.shape[0]
    hit, slot = routing(own_ref[0], picks_ref[...], max(8, experts))
    weight = sum(jnp.where(hit[k], gates_ref[k : k + 1, :], 0.0) for k in range(TOPK))
    place = iota((capacity, tokens), 0)
    parts = [
        jnp.where(slot[k : k + 1, :] == place, weight[k : k + 1, :], 0.0) for k in range(experts)
    ]
    spread = jnp.concatenate(parts, axis=0)
    coarse = spread.astype(BF16)
    fine = (spread - coarse.astype(F32)).astype(BF16)
    chunk = width // 7 if width % 7 == 0 else width
    over_rows = (((0,), (0,)), ((), ()))
    squares = jnp.zeros((tokens, 1), F32)
    for start in range(0, width, chunk):
        cols = slice(start, start + chunk)
        rows = stacked[:, cols]
        moe = lax.dot_general(coarse, rows, over_rows, preferred_element_type=F32)
        moe = moe + lax.dot_general(fine, rows, over_rows, preferred_element_type=F32)
        value = tokens_ref[:, cols].astype(F32) + moe
        stream[:, cols] = value
        squares = squares + jnp.sum(value * value, axis=-1, keepdims=True)
    scale = lax.rsqrt(squares / width + EPS)
    logit = jnp.zeros((tokens, 1), F32)
    for start in range(0, width, chunk):
        cols = slice(start, start + chunk)
        final = (stream[:, cols] * scale * gain_ref[:, cols]).astype(BF16).astype(F32)
        logit = logit + jnp.sum(final * target_ref[:, cols].astype(F32), axis=-1, keepdims=True)
    turn = iota((tokens, tokens), 0) == iota((tokens, tokens), 1)
    logit = jnp.sum(jnp.where(turn, logit, 0.0), axis=0, keepdims=True)
    gap = rest_ref[...] - logit
    token_logp = -(jnp.maximum(gap, 0.0) + jnp.log1p(jnp.exp(-jnp.abs(gap))))
    sequences = out_ref.shape[1]
    inside = iota((sequences, tokens), 0) == seg_ref[...]
    sums = jnp.sum(jnp.where(inside, token_logp, 0.0), axis=1, keepdims=True)
    turn = iota((sequences, sequences), 0) == iota((sequences, sequences), 1)
    out_ref[...] = jnp.sum(jnp.where(turn, sums, 0.0), axis=0, keepdims=True)


def score(own, tokens, gain, picks, gates, target, rest, seg, blocks, capacity, sequences):
    rows, width = tokens.shape
    slots = sum(block.shape[0] for block in blocks)
    smem = pl.BlockSpec(memory_space=pltpu.SMEM)
    vmem = pl.BlockSpec(memory_space=pltpu.VMEM)
    return pl.pallas_call(
        functools.partial(score_kernel, capacity),
        out_shape=jax.ShapeDtypeStruct((1, sequences), F32),
        in_specs=[smem] + [vmem] * (7 + len(blocks)),
        out_specs=vmem,
        scratch_shapes=[
            pltpu.VMEM((slots, width), BF16),
            pltpu.VMEM((rows, width), F32),
        ],
        compiler_params=pltpu.CompilerParams(vmem_limit_bytes=VMEM_LIMIT),
        cost_estimate=COST,
        name="score",
    )(own, tokens, gain, picks, gates, target, rest, seg, *blocks)


class Order:
    def __init__(self, token):
        self.token = token

    def mark(self, *values):
        *values, self.token = lax.optimization_barrier((*values, self.token))
        return values

    def mark_one(self, value):
        return self.mark(value)[0]

    def late(self, value):
        return lax.optimization_barrier((value, self.token))[0]


def cut_kernel(whole_ref, *refs):
    first = 0
    for ref in refs:
        ref[...] = whole_ref[first : first + ref.shape[0], :]
        first += ref.shape[0]


def cut(whole, pieces):
    vmem = pl.BlockSpec(memory_space=pltpu.VMEM)
    return pl.pallas_call(
        cut_kernel,
        out_shape=[jax.ShapeDtypeStruct((count, whole.shape[1]), BF16) for _, count in pieces],
        in_specs=[vmem],
        out_specs=[vmem] * len(pieces),
        compiler_params=pltpu.CompilerParams(vmem_limit_bytes=VMEM_LIMIT),
        cost_estimate=COST,
        name="cut",
    )(whole)


def total_kernel(whole_ref, *refs):
    *refs, out_ref = refs
    first = 0
    for ref in refs:
        rows = slice(first, first + ref.shape[0])
        out_ref[rows, :] = (whole_ref[rows, :].astype(F32) + ref[...].astype(F32)).astype(BF16)
        first += ref.shape[0]


def total(whole, pieces):
    vmem = pl.BlockSpec(memory_space=pltpu.VMEM)
    return pl.pallas_call(
        total_kernel,
        out_shape=jax.ShapeDtypeStruct(whole.shape, BF16),
        in_specs=[vmem] * (1 + len(pieces)),
        out_specs=vmem,
        compiler_params=pltpu.CompilerParams(vmem_limit_bytes=VMEM_LIMIT),
        cost_estimate=COST,
        name="total",
    )(whole, *pieces)


def per_device(
    tokens,
    norm_gain,
    final_gain,
    gate_weight,
    up_weight,
    down_weight,
    picks,
    gates,
    target_rows,
    rest_lse,
    segment_ids,
    ref_logps,
):
    tok_rows = tokens.shape[0]
    spread = FFE // HID_DEV
    devices = lax.axis_size("expert")
    experts = devices // spread
    capacity = (tok_rows * TOPK * 5 // (experts * 4) + 3) // 4 * 4
    capacity = (capacity + 15) // 16 * 16
    own = (lax.axis_index("expert") // spread).astype(jnp.int32).reshape(1)
    picks_t = picks.T
    core, side = 1, 2
    cut_at = capacity * 5 // 8 // 16 * 16
    pieces = [(0, cut_at), (cut_at, capacity - cut_at)] if cut_at else [(0, capacity)]
    counts = [count for _, count in pieces]
    chunks = [(0, 0, capacity)] + [(1, first, count) for first, count in pieces]
    chunks += [(k, 0, capacity) for k in range(2, experts)]
    packed = pack(own, tokens, norm_gain[None, :], picks_t, (gate_weight, up_weight, down_weight), tuple(chunks))
    near = {0: packed[:1], 1: packed[1 : 1 + len(pieces)]}
    near.update((k, [packed[k - 1 + len(pieces)]]) for k in range(2, experts))
    weights = [packed[-1], swap(packed[-1], core)]
    order = Order(own)
    far, mine, theirs, back = {}, {}, {}, {}

    def leave(k):
        near[k] = [swap(order.late(rows), k * spread) for rows in near[k]]

    def arrive(k):
        near[k] = order.mark(*near[k])

    def share(k):
        rows = near[k] if k < 2 else order.mark(*cut(near[k][0], pieces))
        far[k] = [swap(order.late(piece), side) for piece in rows]

    def meet(k):
        far[k] = order.mark(*far[k])

    def work(k):
        rows = [order.late(rows) for rows in (*near[k], *far[k])]
        own_counts = [count for count in (counts if k == 1 else [capacity])]
        parts = order.mark(*expert_block(rows, weights, own_counts + counts))
        mine[k], theirs[k] = parts[: len(own_counts)], parts[len(own_counts) :]

    def cross(k):
        theirs[k] = [swap(order.late(piece), side) for piece in theirs[k]]

    def home(k):
        other = order.mark(*theirs[k])
        if k == 1:
            back[k] = order.mark(*(total(rows, [piece]) for rows, piece in zip(mine[k], other)))
        else:
            back[k] = order.mark(total(mine[k][0], other))

    def leave_back(k):
        back[k] = [swap(order.late(rows), k * spread) for rows in back[k]]

    def arrive_back(k):
        back[k] = order.mark(*back[k])

    share(0)
    leave(1)
    leave(2)
    meet(0)
    arrive(1)
    share(1)
    meet(1)
    arrive(2)
    for k in range(3, experts + 1):
        share(k - 1)
        if k < experts:
            leave(k)
        if k > 3:
            home(k - 2)
            leave_back(k - 2)
        meet(k - 1)
        work(k - 1)
        cross(k - 1)
        if k == 3:
            work(0)
            work(1)
        if k < experts:
            arrive(k)
        if k > 3:
            arrive_back(k - 2)
    home(experts - 1)
    cross(1)
    leave_back(experts - 1)
    home(1)
    leave_back(1)
    cross(0)
    home(0)
    arrive_back(experts - 1)
    arrive_back(1)
    blocks = [rows for k in range(experts) for rows in back[k]]
    local = score(
        own,
        tokens,
        final_gain[None, :],
        picks_t,
        gates.T,
        target_rows,
        rest_lse[None, :],
        segment_ids[None, :],
        blocks,
        capacity,
        ref_logps.shape[0],
    )
    mask = 1
    while mask < devices:
        local = local + swap(local, mask)
        mask *= 2
    sequence_logps = local[0]
    margin = sequence_logps[0::2] - ref_logps[0::2] - (sequence_logps[1::2] - ref_logps[1::2])
    pair_loss = -jax.nn.log_sigmoid(BETA * margin)
    return (sequence_logps, pair_loss)


def solution(mesh):
    placed = (
        P(("group", "expert"), None),
        P(),
        P(),
        P(None, "expert"),
        P(None, "expert"),
        P("expert", None),
        P(("group", "expert"), None),
        P(("group", "expert"), None),
        P(("group", "expert"), None),
        P(("group", "expert")),
        P(("group", "expert")),
        P("group"),
    )
    return jax.shard_map(
        per_device, mesh=mesh, in_specs=placed, out_specs=(P("group"), P("group")), check_vma=False
    )
```

```python
import functools

import jax
import jax.numpy as jnp
from jax import lax
from jax.experimental import pallas as pl
from jax.experimental.pallas import tpu as pltpu
from jax.sharding import PartitionSpec as P

FFE = 2048
HID_DEV = 512
TOPK = 2

EPS = 1e-06
BETA = 0.01

F32 = jnp.float32
BF16 = jnp.bfloat16
VMEM_LIMIT = 10 * 1024 * 1024
COST = pl.CostEstimate(flops=1024, bytes_accessed=1024, transcendentals=0)


def swap(value, mask):
    pairs = [(source, source ^ mask) for source in range(lax.axis_size("expert"))]
    return lax.ppermute(value, "expert", pairs)


def iota(shape, dim):
    return lax.broadcasted_iota(jnp.int32, shape, dim)


def routing(own, picks, rows):
    tokens = picks.shape[1]
    expert = jnp.bitwise_xor(own, iota((rows, tokens), 0))
    hit = [picks[k : k + 1, :] == expert for k in range(TOPK)]
    member = hit[0] | hit[1]
    earlier = (iota((tokens, tokens), 0) < iota((tokens, tokens), 1)).astype(BF16)
    slot = jnp.dot(member.astype(F32).astype(BF16), earlier, preferred_element_type=F32)
    slot = jnp.where(member, slot.astype(jnp.int32), -1)
    return hit, slot


def pack_kernel(own_ref, tokens_hbm, gain_ref, picks_hbm, gate_hbm, up_hbm, down_hbm, *refs):
    *out_refs, weights_ref, tokens_ref, picks_ref, arrived = refs
    width, hidden = gate_hbm.shape
    moves = [(tokens_hbm, tokens_ref), (picks_hbm, picks_ref)]
    sources = [gate_hbm, up_hbm]
    sources += [down_hbm.at[:, pl.ds(first, hidden)] for first in range(0, width, hidden)]
    first = 0
    for source in sources:
        moves.append((source, weights_ref.at[pl.ds(first, source.shape[0]), :]))
        first += source.shape[0]
    copies = [pltpu.make_async_copy(*move, arrived.at[n]) for n, move in enumerate(moves)]
    for copy in copies:
        copy.start()
    copies[0].wait()
    copies[1].wait()
    tokens = tokens_ref.shape[0]
    values = tokens_ref[...].astype(F32)
    scale = lax.rsqrt(jnp.mean(values * values, axis=-1, keepdims=True) + EPS)
    normed = (values * scale * gain_ref[...]).astype(BF16)
    _, slot = routing(own_ref[0], picks_ref[...], max(8, len(out_refs)))
    for k, out_ref in enumerate(out_refs):
        place = iota((out_ref.shape[0], tokens), 0)
        chosen = (slot[k : k + 1, :] == place).astype(F32).astype(BF16)
        out_ref[...] = jnp.dot(chosen, normed, preferred_element_type=F32).astype(BF16)
    for copy in copies[2:]:
        copy.wait()


def pack(own, tokens, gain, picks, weights, experts, capacity):
    width, hidden = weights[0].shape
    smem = pl.BlockSpec(memory_space=pltpu.SMEM)
    vmem = pl.BlockSpec(memory_space=pltpu.VMEM)
    hbm = pl.BlockSpec(memory_space=pltpu.HBM)
    shapes = [(capacity, width)] * experts + [(3 * width, hidden)]
    there = [pltpu.with_memory_space_constraint(array, pltpu.HBM) for array in (tokens, picks, *weights)]
    return pl.pallas_call(
        pack_kernel,
        out_shape=[jax.ShapeDtypeStruct(shape, BF16) for shape in shapes],
        in_specs=[smem, hbm, vmem, hbm] + [hbm] * 3,
        out_specs=[vmem] * len(shapes),
        scratch_shapes=[
            pltpu.VMEM(tokens.shape, BF16),
            pltpu.VMEM(picks.shape, jnp.int32),
            pltpu.SemaphoreType.DMA((4 + width // hidden,)),
        ],
        compiler_params=pltpu.CompilerParams(vmem_limit_bytes=VMEM_LIMIT),
        cost_estimate=COST,
        name="pack",
    )(own, there[0], gain, *there[1:])


def expert_kernel(first, near_ref, far_ref, *refs):
    *weight_refs, mine_ref, theirs_ref, rows = refs
    count = far_ref.shape[0]
    rows[:count, :] = near_ref[first : first + count, :]
    rows[count:, :] = far_ref[...]
    width = rows.shape[1]
    size = weight_refs[0].shape[1]
    hidden = []
    for ref in weight_refs:
        gate = jnp.dot(rows[...], ref[:width, :], preferred_element_type=F32)
        up = jnp.dot(rows[...], ref[width : 2 * width, :], preferred_element_type=F32)
        hidden.append((jax.nn.silu(gate) * up).astype(BF16))
    for start in range(0, width, size):
        part = sum(
            jnp.dot(value, ref[pl.ds(2 * width + start, size), :], preferred_element_type=F32)
            for value, ref in zip(hidden, weight_refs)
        ).astype(BF16)
        mine_ref[:, start : start + size] = part[:count]
        theirs_ref[:, start : start + size] = part[count:]


def expert_block(near, first, far, weights):
    count, width = far.shape
    vmem = pl.BlockSpec(memory_space=pltpu.VMEM)
    return pl.pallas_call(
        functools.partial(expert_kernel, first),
        out_shape=[jax.ShapeDtypeStruct((count, width), BF16)] * 2,
        in_specs=[vmem] * (2 + len(weights)),
        out_specs=[vmem] * 2,
        scratch_shapes=[pltpu.VMEM((2 * count, width), BF16)],
        compiler_params=pltpu.CompilerParams(vmem_limit_bytes=VMEM_LIMIT),
        cost_estimate=COST,
        name="expert_block",
    )(near, far, *weights)


def score_kernel(capacity, own_ref, tokens_ref, gain_ref, picks_ref, gates_ref, target_ref, rest_ref, seg_ref, *refs):
    *block_refs, out_ref, stacked, stream = refs
    tokens, width = tokens_ref.shape
    experts = stacked.shape[0] // capacity
    first = 0
    for ref in block_refs:
        stacked[first : first + ref.shape[0], :] = ref[...]
        first += ref.shape[0]
    hit, slot = routing(own_ref[0], picks_ref[...], max(8, experts))
    weight = sum(jnp.where(hit[k], gates_ref[k : k + 1, :], 0.0) for k in range(TOPK))
    place = iota((capacity, tokens), 0)
    parts = [
        jnp.where(slot[k : k + 1, :] == place, weight[k : k + 1, :], 0.0) for k in range(experts)
    ]
    spread = jnp.concatenate(parts, axis=0)
    coarse = spread.astype(BF16)
    fine = (spread - coarse.astype(F32)).astype(BF16)
    chunk = width // 7 if width % 7 == 0 else width
    over_rows = (((0,), (0,)), ((), ()))
    squares = jnp.zeros((tokens, 1), F32)
    for start in range(0, width, chunk):
        cols = slice(start, start + chunk)
        rows = stacked[:, cols]
        moe = lax.dot_general(coarse, rows, over_rows, preferred_element_type=F32)
        moe = moe + lax.dot_general(fine, rows, over_rows, preferred_element_type=F32)
        value = tokens_ref[:, cols].astype(F32) + moe
        stream[:, cols] = value
        squares = squares + jnp.sum(value * value, axis=-1, keepdims=True)
    scale = lax.rsqrt(squares / width + EPS)
    logit = jnp.zeros((tokens, 1), F32)
    for start in range(0, width, chunk):
        cols = slice(start, start + chunk)
        final = (stream[:, cols] * scale * gain_ref[:, cols]).astype(BF16).astype(F32)
        logit = logit + jnp.sum(final * target_ref[:, cols].astype(F32), axis=-1, keepdims=True)
    turn = iota((tokens, tokens), 0) == iota((tokens, tokens), 1)
    logit = jnp.sum(jnp.where(turn, logit, 0.0), axis=0, keepdims=True)
    gap = rest_ref[...] - logit
    token_logp = -(jnp.maximum(gap, 0.0) + jnp.log1p(jnp.exp(-jnp.abs(gap))))
    sequences = out_ref.shape[1]
    inside = iota((sequences, tokens), 0) == seg_ref[...]
    sums = jnp.sum(jnp.where(inside, token_logp, 0.0), axis=1, keepdims=True)
    turn = iota((sequences, sequences), 0) == iota((sequences, sequences), 1)
    out_ref[...] = jnp.sum(jnp.where(turn, sums, 0.0), axis=0, keepdims=True)


def score(own, tokens, gain, picks, gates, target, rest, seg, blocks, capacity, sequences):
    rows, width = tokens.shape
    slots = sum(block.shape[0] for block in blocks)
    smem = pl.BlockSpec(memory_space=pltpu.SMEM)
    vmem = pl.BlockSpec(memory_space=pltpu.VMEM)
    return pl.pallas_call(
        functools.partial(score_kernel, capacity),
        out_shape=jax.ShapeDtypeStruct((1, sequences), F32),
        in_specs=[smem] + [vmem] * (7 + len(blocks)),
        out_specs=vmem,
        scratch_shapes=[
            pltpu.VMEM((slots, width), BF16),
            pltpu.VMEM((rows, width), F32),
        ],
        compiler_params=pltpu.CompilerParams(vmem_limit_bytes=VMEM_LIMIT),
        cost_estimate=COST,
        name="score",
    )(own, tokens, gain, picks, gates, target, rest, seg, *blocks)


class Order:
    def __init__(self, token):
        self.token = token

    def mark(self, *values):
        *values, self.token = lax.optimization_barrier((*values, self.token))
        return values

    def mark_one(self, value):
        return self.mark(value)[0]

    def late(self, value):
        return lax.optimization_barrier((value, self.token))[0]


def cut_kernel(whole_ref, *refs):
    first = 0
    for ref in refs:
        ref[...] = whole_ref[first : first + ref.shape[0], :]
        first += ref.shape[0]


def cut(whole, pieces):
    vmem = pl.BlockSpec(memory_space=pltpu.VMEM)
    return pl.pallas_call(
        cut_kernel,
        out_shape=[jax.ShapeDtypeStruct((count, whole.shape[1]), BF16) for _, count in pieces],
        in_specs=[vmem],
        out_specs=[vmem] * len(pieces),
        compiler_params=pltpu.CompilerParams(vmem_limit_bytes=VMEM_LIMIT),
        cost_estimate=COST,
        name="cut",
    )(whole)


def total_kernel(count, *refs):
    *refs, out_ref = refs
    for side in (refs[:count], refs[count:]):
        first = 0
        for ref in side:
            rows = slice(first, first + ref.shape[0])
            if side[0] is refs[0]:
                out_ref[rows, :] = ref[...]
            else:
                out_ref[rows, :] = (out_ref[rows, :].astype(F32) + ref[...].astype(F32)).astype(BF16)
            first += ref.shape[0]


def total(ours, others):
    rows = sum(piece.shape[0] for piece in ours)
    vmem = pl.BlockSpec(memory_space=pltpu.VMEM)
    return pl.pallas_call(
        functools.partial(total_kernel, len(ours)),
        out_shape=jax.ShapeDtypeStruct((rows, ours[0].shape[1]), BF16),
        in_specs=[vmem] * (len(ours) + len(others)),
        out_specs=vmem,
        compiler_params=pltpu.CompilerParams(vmem_limit_bytes=VMEM_LIMIT),
        cost_estimate=COST,
        name="total",
    )(*ours, *others)


def per_device(
    tokens,
    norm_gain,
    final_gain,
    gate_weight,
    up_weight,
    down_weight,
    picks,
    gates,
    target_rows,
    rest_lse,
    segment_ids,
    ref_logps,
):
    tok_rows = tokens.shape[0]
    spread = FFE // HID_DEV
    devices = lax.axis_size("expert")
    experts = devices // spread
    capacity = (tok_rows * TOPK * 5 // (experts * 4) + 3) // 4 * 4
    capacity = (capacity + 15) // 16 * 16
    own = (lax.axis_index("expert") // spread).astype(jnp.int32).reshape(1)
    picks_t = picks.T
    core, side = 1, 2
    cut_at = capacity * 5 // 8 // 16 * 16
    pieces = [(0, cut_at), (cut_at, capacity - cut_at)] if cut_at else [(0, capacity)]
    weights = (gate_weight, up_weight, down_weight)
    *near, staged = pack(own, tokens, norm_gain[None, :], picks_t, weights, experts, capacity)
    weights = [staged, swap(staged, core)]
    order = Order(own)
    far, mine, theirs, back = {}, {}, {}, {}

    def leave(k):
        near[k] = swap(order.late(near[k]), k * spread)

    def arrive(k):
        near[k] = order.mark_one(near[k])

    def share(k):
        far[k] = [swap(order.late(piece), side) for piece in order.mark(*cut(near[k], pieces))]

    def work(k):
        mine[k], theirs[k] = [], []
        for (first, _), piece in zip(pieces, far[k]):
            there = order.mark_one(piece)
            part, other = order.mark(*expert_block(order.late(near[k]), first, there, weights))
            mine[k].append(part)
            theirs[k].append(swap(other, side))

    def work_whole(k):
        rows = (order.late(near[k]), 0, order.late(far[k]))
        mine[k], theirs[k] = order.mark(*expert_block(*rows, weights))

    def home(k):
        theirs[k] = order.mark(*theirs[k])
        back[k] = order.mark_one(total(mine[k], theirs[k]))

    def leave_back(k):
        back[k] = swap(order.late(back[k]), k * spread)

    def arrive_back(k):
        back[k] = order.mark_one(back[k])

    far[0], far[1] = swap(near[0], side), swap(near[1], side)
    leave(1)
    leave(2)
    far[0], far[1], near[1], near[2] = order.mark(far[0], far[1], near[1], near[2])
    for k in range(3, experts + 1):
        share(k - 1)
        if k < experts:
            leave(k)
        if k == 3:
            far[1] = swap(order.late(far[1]), spread)
        if k > 3:
            home(k - 2)
            leave_back(k - 2)
        if k == experts:
            work_whole(1)
            theirs[1] = swap(theirs[1], spread)
        work(k - 1)
        if k == 3:
            work_whole(0)
        if k < experts:
            arrive(k)
        if k == 3:
            far[1] = order.mark_one(far[1])
        if k > 3:
            arrive_back(k - 2)
    home(experts - 1)
    leave_back(experts - 1)
    mine[1] = [swap(order.late(mine[1]), spread)]
    mine[0], theirs[0] = [mine[0]], [swap(order.late(theirs[0]), side)]
    theirs[1] = order.mark(*cut(order.mark_one(theirs[1]), pieces))
    theirs[1] = [swap(order.late(piece), side) for piece in theirs[1]]
    home(0)
    mine[1] = order.mark(*mine[1])
    home(1)
    arrive_back(experts - 1)
    blocks = [back[k] for k in range(experts)]
    local = score(
        own,
        tokens,
        final_gain[None, :],
        picks_t,
        gates.T,
        target_rows,
        rest_lse[None, :],
        segment_ids[None, :],
        blocks,
        capacity,
        ref_logps.shape[0],
    )
    mask = 1
    while mask < devices:
        local = local + swap(local, mask)
        mask *= 2
    sequence_logps = local[0]
    margin = sequence_logps[0::2] - ref_logps[0::2] - (sequence_logps[1::2] - ref_logps[1::2])
    pair_loss = -jax.nn.log_sigmoid(BETA * margin)
    return (sequence_logps, pair_loss)


def solution(mesh):
    placed = (
        P(("group", "expert"), None),
        P(),
        P(),
        P(None, "expert"),
        P(None, "expert"),
        P("expert", None),
        P(("group", "expert"), None),
        P(("group", "expert"), None),
        P(("group", "expert"), None),
        P(("group", "expert")),
        P(("group", "expert")),
        P("group"),
    )
    return jax.shard_map(
        per_device, mesh=mesh, in_specs=placed, out_specs=(P("group"), P("group")), check_vma=False
    )
```

```python
import functools

import jax
import jax.numpy as jnp
from jax import lax
from jax.experimental import pallas as pl
from jax.experimental.pallas import tpu as pltpu
from jax.sharding import PartitionSpec as P

FFE = 2048
HID_DEV = 512
TOPK = 2

EPS = 1e-06
BETA = 0.01

F32 = jnp.float32
BF16 = jnp.bfloat16
VMEM_LIMIT = 10 * 1024 * 1024
COST = pl.CostEstimate(flops=1024, bytes_accessed=1024, transcendentals=0)


def swap(value, mask):
    pairs = [(source, source ^ mask) for source in range(lax.axis_size("expert"))]
    return lax.ppermute(value, "expert", pairs)


def iota(shape, dim):
    return lax.broadcasted_iota(jnp.int32, shape, dim)


def routing(own, picks, rows):
    tokens = picks.shape[1]
    expert = jnp.bitwise_xor(own, iota((rows, tokens), 0))
    hit = [picks[k : k + 1, :] == expert for k in range(TOPK)]
    member = hit[0] | hit[1]
    earlier = (iota((tokens, tokens), 0) < iota((tokens, tokens), 1)).astype(BF16)
    slot = jnp.dot(member.astype(F32).astype(BF16), earlier, preferred_element_type=F32)
    slot = jnp.where(member, slot.astype(jnp.int32), -1)
    return hit, slot


def pack_kernel(own_ref, tokens_hbm, gain_ref, picks_hbm, gate_hbm, up_hbm, down_hbm, *refs):
    *out_refs, weights_ref, tokens_ref, picks_ref, arrived = refs
    width, hidden = gate_hbm.shape
    moves = [(tokens_hbm, tokens_ref), (picks_hbm, picks_ref)]
    sources = [gate_hbm, up_hbm]
    sources += [down_hbm.at[:, pl.ds(first, hidden)] for first in range(0, width, hidden)]
    first = 0
    for source in sources:
        moves.append((source, weights_ref.at[pl.ds(first, source.shape[0]), :]))
        first += source.shape[0]
    copies = [pltpu.make_async_copy(*move, arrived.at[n]) for n, move in enumerate(moves)]
    for copy in copies:
        copy.start()
    copies[0].wait()
    copies[1].wait()
    tokens = tokens_ref.shape[0]
    values = tokens_ref[...].astype(F32)
    scale = lax.rsqrt(jnp.mean(values * values, axis=-1, keepdims=True) + EPS)
    normed = (values * scale * gain_ref[...]).astype(BF16)
    _, slot = routing(own_ref[0], picks_ref[...], max(8, len(out_refs)))
    for k, out_ref in enumerate(out_refs):
        place = iota((out_ref.shape[0], tokens), 0)
        chosen = (slot[k : k + 1, :] == place).astype(F32).astype(BF16)
        out_ref[...] = jnp.dot(chosen, normed, preferred_element_type=F32).astype(BF16)
    for copy in copies[2:]:
        copy.wait()


def pack(own, tokens, gain, picks, weights, experts, capacity):
    width, hidden = weights[0].shape
    smem = pl.BlockSpec(memory_space=pltpu.SMEM)
    vmem = pl.BlockSpec(memory_space=pltpu.VMEM)
    hbm = pl.BlockSpec(memory_space=pltpu.HBM)
    shapes = [(capacity, width)] * experts + [(3 * width, hidden)]
    there = [pltpu.with_memory_space_constraint(array, pltpu.HBM) for array in (tokens, picks, *weights)]
    return pl.pallas_call(
        pack_kernel,
        out_shape=[jax.ShapeDtypeStruct(shape, BF16) for shape in shapes],
        in_specs=[smem, hbm, vmem, hbm] + [hbm] * 3,
        out_specs=[vmem] * len(shapes),
        scratch_shapes=[
            pltpu.VMEM(tokens.shape, BF16),
            pltpu.VMEM(picks.shape, jnp.int32),
            pltpu.SemaphoreType.DMA((4 + width // hidden,)),
        ],
        compiler_params=pltpu.CompilerParams(vmem_limit_bytes=VMEM_LIMIT),
        cost_estimate=COST,
        name="pack",
    )(own, there[0], gain, *there[1:])


def expert_kernel(first, near_ref, far_ref, *refs):
    *weight_refs, mine_ref, theirs_ref, rows = refs
    count = far_ref.shape[0]
    rows[:count, :] = near_ref[first : first + count, :]
    rows[count:, :] = far_ref[...]
    width = rows.shape[1]
    size = weight_refs[0].shape[1]
    hidden = []
    for ref in weight_refs:
        gate = jnp.dot(rows[...], ref[:width, :], preferred_element_type=F32)
        up = jnp.dot(rows[...], ref[width : 2 * width, :], preferred_element_type=F32)
        hidden.append((jax.nn.silu(gate) * up).astype(BF16))
    for start in range(0, width, size):
        part = sum(
            jnp.dot(value, ref[pl.ds(2 * width + start, size), :], preferred_element_type=F32)
            for value, ref in zip(hidden, weight_refs)
        ).astype(BF16)
        mine_ref[:, start : start + size] = part[:count]
        theirs_ref[:, start : start + size] = part[count:]


def expert_block(near, first, far, weights):
    count, width = far.shape
    vmem = pl.BlockSpec(memory_space=pltpu.VMEM)
    return pl.pallas_call(
        functools.partial(expert_kernel, first),
        out_shape=[jax.ShapeDtypeStruct((count, width), BF16)] * 2,
        in_specs=[vmem] * (2 + len(weights)),
        out_specs=[vmem] * 2,
        scratch_shapes=[pltpu.VMEM((2 * count, width), BF16)],
        compiler_params=pltpu.CompilerParams(vmem_limit_bytes=VMEM_LIMIT),
        cost_estimate=COST,
        name="expert_block",
    )(near, far, *weights)


def score_kernel(capacity, own_ref, tokens_ref, gain_ref, picks_ref, gates_ref, target_ref, rest_ref, seg_ref, *refs):
    *block_refs, out_ref, stacked, stream = refs
    tokens, width = tokens_ref.shape
    experts = stacked.shape[0] // capacity
    first = 0
    for ref in block_refs:
        stacked[first : first + ref.shape[0], :] = ref[...]
        first += ref.shape[0]
    hit, slot = routing(own_ref[0], picks_ref[...], max(8, experts))
    weight = sum(jnp.where(hit[k], gates_ref[k : k + 1, :], 0.0) for k in range(TOPK))
    place = iota((capacity, tokens), 0)
    parts = [
        jnp.where(slot[k : k + 1, :] == place, weight[k : k + 1, :], 0.0) for k in range(experts)
    ]
    spread = jnp.concatenate(parts, axis=0)
    coarse = spread.astype(BF16)
    fine = (spread - coarse.astype(F32)).astype(BF16)
    chunk = width // 7 if width % 7 == 0 else width
    over_rows = (((0,), (0,)), ((), ()))
    squares = jnp.zeros((tokens, 1), F32)
    for start in range(0, width, chunk):
        cols = slice(start, start + chunk)
        rows = stacked[:, cols]
        moe = lax.dot_general(coarse, rows, over_rows, preferred_element_type=F32)
        moe = moe + lax.dot_general(fine, rows, over_rows, preferred_element_type=F32)
        value = tokens_ref[:, cols].astype(F32) + moe
        stream[:, cols] = value
        squares = squares + jnp.sum(value * value, axis=-1, keepdims=True)
    scale = lax.rsqrt(squares / width + EPS)
    logit = jnp.zeros((tokens, 1), F32)
    for start in range(0, width, chunk):
        cols = slice(start, start + chunk)
        final = (stream[:, cols] * scale * gain_ref[:, cols]).astype(BF16).astype(F32)
        logit = logit + jnp.sum(final * target_ref[:, cols].astype(F32), axis=-1, keepdims=True)
    turn = iota((tokens, tokens), 0) == iota((tokens, tokens), 1)
    logit = jnp.sum(jnp.where(turn, logit, 0.0), axis=0, keepdims=True)
    gap = rest_ref[...] - logit
    token_logp = -(jnp.maximum(gap, 0.0) + jnp.log1p(jnp.exp(-jnp.abs(gap))))
    sequences = out_ref.shape[1]
    inside = iota((sequences, tokens), 0) == seg_ref[...]
    sums = jnp.sum(jnp.where(inside, token_logp, 0.0), axis=1, keepdims=True)
    turn = iota((sequences, sequences), 0) == iota((sequences, sequences), 1)
    out_ref[...] = jnp.sum(jnp.where(turn, sums, 0.0), axis=0, keepdims=True)


def score(own, tokens, gain, picks, gates, target, rest, seg, blocks, capacity, sequences):
    rows, width = tokens.shape
    slots = sum(block.shape[0] for block in blocks)
    smem = pl.BlockSpec(memory_space=pltpu.SMEM)
    vmem = pl.BlockSpec(memory_space=pltpu.VMEM)
    return pl.pallas_call(
        functools.partial(score_kernel, capacity),
        out_shape=jax.ShapeDtypeStruct((1, sequences), F32),
        in_specs=[smem] + [vmem] * (7 + len(blocks)),
        out_specs=vmem,
        scratch_shapes=[
            pltpu.VMEM((slots, width), BF16),
            pltpu.VMEM((rows, width), F32),
        ],
        compiler_params=pltpu.CompilerParams(vmem_limit_bytes=VMEM_LIMIT),
        cost_estimate=COST,
        name="score",
    )(own, tokens, gain, picks, gates, target, rest, seg, *blocks)


class Order:
    def __init__(self, token):
        self.token = token

    def mark(self, *values):
        *values, self.token = lax.optimization_barrier((*values, self.token))
        return values

    def mark_one(self, value):
        return self.mark(value)[0]

    def late(self, value):
        return lax.optimization_barrier((value, self.token))[0]


def cut_kernel(whole_ref, *refs):
    first = 0
    for ref in refs:
        ref[...] = whole_ref[first : first + ref.shape[0], :]
        first += ref.shape[0]


def cut(whole, pieces):
    vmem = pl.BlockSpec(memory_space=pltpu.VMEM)
    return pl.pallas_call(
        cut_kernel,
        out_shape=[jax.ShapeDtypeStruct((count, whole.shape[1]), BF16) for _, count in pieces],
        in_specs=[vmem],
        out_specs=[vmem] * len(pieces),
        compiler_params=pltpu.CompilerParams(vmem_limit_bytes=VMEM_LIMIT),
        cost_estimate=COST,
        name="cut",
    )(whole)


def total_kernel(count, *refs):
    *refs, out_ref = refs
    for side in (refs[:count], refs[count:]):
        first = 0
        for ref in side:
            rows = slice(first, first + ref.shape[0])
            if side[0] is refs[0]:
                out_ref[rows, :] = ref[...]
            else:
                out_ref[rows, :] = (out_ref[rows, :].astype(F32) + ref[...].astype(F32)).astype(BF16)
            first += ref.shape[0]


def total(ours, others):
    rows = sum(piece.shape[0] for piece in ours)
    vmem = pl.BlockSpec(memory_space=pltpu.VMEM)
    return pl.pallas_call(
        functools.partial(total_kernel, len(ours)),
        out_shape=jax.ShapeDtypeStruct((rows, ours[0].shape[1]), BF16),
        in_specs=[vmem] * (len(ours) + len(others)),
        out_specs=vmem,
        compiler_params=pltpu.CompilerParams(vmem_limit_bytes=VMEM_LIMIT),
        cost_estimate=COST,
        name="total",
    )(*ours, *others)


def per_device(
    tokens,
    norm_gain,
    final_gain,
    gate_weight,
    up_weight,
    down_weight,
    picks,
    gates,
    target_rows,
    rest_lse,
    segment_ids,
    ref_logps,
):
    tok_rows = tokens.shape[0]
    spread = FFE // HID_DEV
    devices = lax.axis_size("expert")
    experts = devices // spread
    capacity = (tok_rows * TOPK * 5 // (experts * 4) + 3) // 4 * 4
    capacity = (capacity + 15) // 16 * 16
    own = (lax.axis_index("expert") // spread).astype(jnp.int32).reshape(1)
    picks_t = picks.T
    core, side = 1, 2
    cut_at = capacity * 5 // 8 // 16 * 16
    pieces = [(0, cut_at), (cut_at, capacity - cut_at)] if cut_at else [(0, capacity)]
    weights = (gate_weight, up_weight, down_weight)
    *near, staged = pack(own, tokens, norm_gain[None, :], picks_t, weights, experts, capacity)
    weights = [staged, swap(staged, core)]
    order = Order(own)
    far, mine, theirs, back = {}, {}, {}, {}

    def leave(k):
        near[k] = swap(order.late(near[k]), k * spread)

    def arrive(k):
        near[k] = order.mark_one(near[k])

    def share(k):
        far[k] = [swap(order.late(piece), side) for piece in order.mark(*cut(near[k], pieces))]

    def work(k):
        mine[k], theirs[k] = [], []
        for (first, _), piece in zip(pieces, far[k]):
            there = order.mark_one(piece)
            part, other = order.mark(*expert_block(order.late(near[k]), first, there, weights))
            mine[k].append(part)
            theirs[k].append(swap(other, side))

    def work_whole(k):
        rows = (order.late(near[k]), 0, order.late(far[k]))
        mine[k], theirs[k] = order.mark(*expert_block(*rows, weights))

    def home(k):
        theirs[k] = order.mark(*theirs[k])
        back[k] = order.mark_one(total(mine[k], theirs[k]))

    def leave_back(k):
        back[k] = swap(order.late(back[k]), k * spread)

    def arrive_back(k):
        back[k] = order.mark_one(back[k])

    far[0], far[1] = swap(near[0], side), swap(near[1], side)
    leave(1)
    leave(2)
    far[0], weights[1] = order.mark(far[0], weights[1])
    work_whole(0)
    arrive(2)
    arrive(1)
    far[1] = order.mark_one(far[1])
    for k in range(3, experts + 1):
        share(k - 1)
        if k < experts:
            leave(k)
        if k == 3:
            far[1] = swap(order.late(far[1]), spread)
        if k > 3:
            home(k - 2)
            leave_back(k - 2)
        if k == experts:
            work_whole(1)
            theirs[1] = [swap(piece, spread) for piece in order.mark(*cut(theirs[1], pieces))]
        work(k - 1)
        if k < experts:
            arrive(k)
        if k == 3:
            far[1] = order.mark_one(far[1])
        if k > 3:
            arrive_back(k - 2)
    theirs[1] = order.mark(*theirs[1])
    home(experts - 1)
    leave_back(experts - 1)
    mine[1] = [swap(order.late(mine[1]), spread)]
    mine[0], theirs[0] = [mine[0]], [swap(order.late(theirs[0]), side)]
    theirs[1] = [swap(order.late(piece), side) for piece in theirs[1]]
    arrive_back(experts - 1)
    home(0)
    mine[1] = order.mark(*mine[1])
    home(1)
    blocks = [back[k] for k in range(experts)]
    local = score(
        own,
        tokens,
        final_gain[None, :],
        picks_t,
        gates.T,
        target_rows,
        rest_lse[None, :],
        segment_ids[None, :],
        blocks,
        capacity,
        ref_logps.shape[0],
    )
    mask = 1
    while mask < devices:
        local = local + swap(local, mask)
        mask *= 2
    sequence_logps = local[0]
    margin = sequence_logps[0::2] - ref_logps[0::2] - (sequence_logps[1::2] - ref_logps[1::2])
    pair_loss = -jax.nn.log_sigmoid(BETA * margin)
    return (sequence_logps, pair_loss)


def solution(mesh):
    placed = (
        P(("group", "expert"), None),
        P(),
        P(),
        P(None, "expert"),
        P(None, "expert"),
        P("expert", None),
        P(("group", "expert"), None),
        P(("group", "expert"), None),
        P(("group", "expert"), None),
        P(("group", "expert")),
        P(("group", "expert")),
        P("group"),
    )
    return jax.shard_map(
        per_device, mesh=mesh, in_specs=placed, out_specs=(P("group"), P("group")), check_vma=False
    )
```

```python
import functools

import jax
import jax.numpy as jnp
from jax import lax
from jax.experimental import pallas as pl
from jax.experimental.pallas import tpu as pltpu
from jax.sharding import PartitionSpec as P

FFE = 2048
HID_DEV = 512
TOPK = 2

EPS = 1e-06
BETA = 0.01

F32 = jnp.float32
BF16 = jnp.bfloat16
VMEM_LIMIT = 10 * 1024 * 1024
COST = pl.CostEstimate(flops=1024, bytes_accessed=1024, transcendentals=0)


def swap(value, mask):
    pairs = [(source, source ^ mask) for source in range(lax.axis_size("expert"))]
    return lax.ppermute(value, "expert", pairs)


def iota(shape, dim):
    return lax.broadcasted_iota(jnp.int32, shape, dim)


def routing(own, picks, rows):
    tokens = picks.shape[1]
    expert = jnp.bitwise_xor(own, iota((rows, tokens), 0))
    hit = [picks[k : k + 1, :] == expert for k in range(TOPK)]
    member = hit[0] | hit[1]
    earlier = (iota((tokens, tokens), 0) < iota((tokens, tokens), 1)).astype(BF16)
    slot = jnp.dot(member.astype(F32).astype(BF16), earlier, preferred_element_type=F32)
    slot = jnp.where(member, slot.astype(jnp.int32), -1)
    return hit, slot


def pack_kernel(own_ref, tokens_hbm, gain_ref, picks_hbm, gate_hbm, up_hbm, down_hbm, *refs):
    *out_refs, weights_ref, tokens_ref, picks_ref, arrived = refs
    width, hidden = gate_hbm.shape
    moves = [(tokens_hbm, tokens_ref), (picks_hbm, picks_ref)]
    sources = [gate_hbm, up_hbm]
    sources += [down_hbm.at[:, pl.ds(first, hidden)] for first in range(0, width, hidden)]
    first = 0
    for source in sources:
        moves.append((source, weights_ref.at[pl.ds(first, source.shape[0]), :]))
        first += source.shape[0]
    copies = [pltpu.make_async_copy(*move, arrived.at[n]) for n, move in enumerate(moves)]
    for copy in copies:
        copy.start()
    copies[0].wait()
    copies[1].wait()
    tokens = tokens_ref.shape[0]
    values = tokens_ref[...].astype(F32)
    scale = lax.rsqrt(jnp.mean(values * values, axis=-1, keepdims=True) + EPS)
    normed = (values * scale * gain_ref[...]).astype(BF16)
    _, slot = routing(own_ref[0], picks_ref[...], max(8, len(out_refs)))
    for k, out_ref in enumerate(out_refs):
        place = iota((out_ref.shape[0], tokens), 0)
        chosen = (slot[k : k + 1, :] == place).astype(F32).astype(BF16)
        out_ref[...] = jnp.dot(chosen, normed, preferred_element_type=F32).astype(BF16)
    for copy in copies[2:]:
        copy.wait()


def pack(own, tokens, gain, picks, weights, experts, capacity):
    width, hidden = weights[0].shape
    smem = pl.BlockSpec(memory_space=pltpu.SMEM)
    vmem = pl.BlockSpec(memory_space=pltpu.VMEM)
    hbm = pl.BlockSpec(memory_space=pltpu.HBM)
    shapes = [(capacity, width)] * experts + [(3 * width, hidden)]
    there = [pltpu.with_memory_space_constraint(array, pltpu.HBM) for array in (tokens, picks, *weights)]
    return pl.pallas_call(
        pack_kernel,
        out_shape=[jax.ShapeDtypeStruct(shape, BF16) for shape in shapes],
        in_specs=[smem, hbm, vmem, hbm] + [hbm] * 3,
        out_specs=[vmem] * len(shapes),
        scratch_shapes=[
            pltpu.VMEM(tokens.shape, BF16),
            pltpu.VMEM(picks.shape, jnp.int32),
            pltpu.SemaphoreType.DMA((4 + width // hidden,)),
        ],
        compiler_params=pltpu.CompilerParams(vmem_limit_bytes=VMEM_LIMIT),
        cost_estimate=COST,
        name="pack",
    )(own, there[0], gain, *there[1:])


def expert_kernel(first, near_ref, far_ref, *refs):
    *weight_refs, mine_ref, theirs_ref, rows = refs
    count = far_ref.shape[0]
    rows[:count, :] = near_ref[first : first + count, :]
    rows[count:, :] = far_ref[...]
    width = rows.shape[1]
    size = weight_refs[0].shape[1]
    hidden = []
    for ref in weight_refs:
        gate = jnp.dot(rows[...], ref[:width, :], preferred_element_type=F32)
        up = jnp.dot(rows[...], ref[width : 2 * width, :], preferred_element_type=F32)
        hidden.append((jax.nn.silu(gate) * up).astype(BF16))
    for start in range(0, width, size):
        part = sum(
            jnp.dot(value, ref[pl.ds(2 * width + start, size), :], preferred_element_type=F32)
            for value, ref in zip(hidden, weight_refs)
        ).astype(BF16)
        mine_ref[:, start : start + size] = part[:count]
        theirs_ref[:, start : start + size] = part[count:]


def expert_block(near, first, far, weights):
    count, width = far.shape
    vmem = pl.BlockSpec(memory_space=pltpu.VMEM)
    return pl.pallas_call(
        functools.partial(expert_kernel, first),
        out_shape=[jax.ShapeDtypeStruct((count, width), BF16)] * 2,
        in_specs=[vmem] * (2 + len(weights)),
        out_specs=[vmem] * 2,
        scratch_shapes=[pltpu.VMEM((2 * count, width), BF16)],
        compiler_params=pltpu.CompilerParams(vmem_limit_bytes=VMEM_LIMIT),
        cost_estimate=COST,
        name="expert_block",
    )(near, far, *weights)


def score_kernel(capacity, own_ref, tokens_ref, gain_ref, picks_ref, gates_ref, target_ref, rest_ref, seg_ref, *refs):
    *block_refs, out_ref, stacked, stream = refs
    tokens, width = tokens_ref.shape
    experts = stacked.shape[0] // capacity
    first = 0
    for ref in block_refs:
        stacked[first : first + ref.shape[0], :] = ref[...]
        first += ref.shape[0]
    hit, slot = routing(own_ref[0], picks_ref[...], max(8, experts))
    weight = sum(jnp.where(hit[k], gates_ref[k : k + 1, :], 0.0) for k in range(TOPK))
    place = iota((capacity, tokens), 0)
    parts = [
        jnp.where(slot[k : k + 1, :] == place, weight[k : k + 1, :], 0.0) for k in range(experts)
    ]
    spread = jnp.concatenate(parts, axis=0)
    coarse = spread.astype(BF16)
    fine = (spread - coarse.astype(F32)).astype(BF16)
    chunk = width // 7 if width % 7 == 0 else width
    over_rows = (((0,), (0,)), ((), ()))
    squares = jnp.zeros((tokens, 1), F32)
    for start in range(0, width, chunk):
        cols = slice(start, start + chunk)
        rows = stacked[:, cols]
        moe = lax.dot_general(coarse, rows, over_rows, preferred_element_type=F32)
        moe = moe + lax.dot_general(fine, rows, over_rows, preferred_element_type=F32)
        value = tokens_ref[:, cols].astype(F32) + moe
        stream[:, cols] = value
        squares = squares + jnp.sum(value * value, axis=-1, keepdims=True)
    scale = lax.rsqrt(squares / width + EPS)
    logit = jnp.zeros((tokens, 1), F32)
    for start in range(0, width, chunk):
        cols = slice(start, start + chunk)
        final = (stream[:, cols] * scale * gain_ref[:, cols]).astype(BF16).astype(F32)
        logit = logit + jnp.sum(final * target_ref[:, cols].astype(F32), axis=-1, keepdims=True)
    turn = iota((tokens, tokens), 0) == iota((tokens, tokens), 1)
    logit = jnp.sum(jnp.where(turn, logit, 0.0), axis=0, keepdims=True)
    gap = rest_ref[...] - logit
    token_logp = -(jnp.maximum(gap, 0.0) + jnp.log1p(jnp.exp(-jnp.abs(gap))))
    sequences = out_ref.shape[1]
    inside = iota((sequences, tokens), 0) == seg_ref[...]
    sums = jnp.sum(jnp.where(inside, token_logp, 0.0), axis=1, keepdims=True)
    turn = iota((sequences, sequences), 0) == iota((sequences, sequences), 1)
    sums = jnp.sum(jnp.where(turn, sums, 0.0), axis=0, keepdims=True)
    out_ref[...] = jnp.broadcast_to(sums, out_ref.shape)


def score(own, tokens, gain, picks, gates, target, rest, seg, blocks, capacity, outs):
    rows, width = tokens.shape
    slots = sum(block.shape[0] for block in blocks)
    smem = pl.BlockSpec(memory_space=pltpu.SMEM)
    vmem = pl.BlockSpec(memory_space=pltpu.VMEM)
    return pl.pallas_call(
        functools.partial(score_kernel, capacity),
        out_shape=jax.ShapeDtypeStruct(outs, F32),
        in_specs=[smem] + [vmem] * (7 + len(blocks)),
        out_specs=vmem,
        scratch_shapes=[
            pltpu.VMEM((slots, width), BF16),
            pltpu.VMEM((rows, width), F32),
        ],
        compiler_params=pltpu.CompilerParams(vmem_limit_bytes=VMEM_LIMIT),
        cost_estimate=COST,
        name="score",
    )(own, tokens, gain, picks, gates, target, rest, seg, *blocks)


class Order:
    def __init__(self, token):
        self.token = token

    def mark(self, *values):
        *values, self.token = lax.optimization_barrier((*values, self.token))
        return values

    def mark_one(self, value):
        return self.mark(value)[0]

    def late(self, value):
        return lax.optimization_barrier((value, self.token))[0]


def cut_kernel(whole_ref, *refs):
    first = 0
    for ref in refs:
        ref[...] = whole_ref[first : first + ref.shape[0], :]
        first += ref.shape[0]


def cut(whole, pieces):
    vmem = pl.BlockSpec(memory_space=pltpu.VMEM)
    return pl.pallas_call(
        cut_kernel,
        out_shape=[jax.ShapeDtypeStruct((count, whole.shape[1]), BF16) for _, count in pieces],
        in_specs=[vmem],
        out_specs=[vmem] * len(pieces),
        compiler_params=pltpu.CompilerParams(vmem_limit_bytes=VMEM_LIMIT),
        cost_estimate=COST,
        name="cut",
    )(whole)


def total_kernel(count, *refs):
    *refs, out_ref = refs
    for side in (refs[:count], refs[count:]):
        first = 0
        for ref in side:
            rows = slice(first, first + ref.shape[0])
            if side[0] is refs[0]:
                out_ref[rows, :] = ref[...]
            else:
                out_ref[rows, :] = (out_ref[rows, :].astype(F32) + ref[...].astype(F32)).astype(BF16)
            first += ref.shape[0]


def total(ours, others):
    rows = sum(piece.shape[0] for piece in ours)
    vmem = pl.BlockSpec(memory_space=pltpu.VMEM)
    return pl.pallas_call(
        functools.partial(total_kernel, len(ours)),
        out_shape=jax.ShapeDtypeStruct((rows, ours[0].shape[1]), BF16),
        in_specs=[vmem] * (len(ours) + len(others)),
        out_specs=vmem,
        compiler_params=pltpu.CompilerParams(vmem_limit_bytes=VMEM_LIMIT),
        cost_estimate=COST,
        name="total",
    )(*ours, *others)


def per_device(
    tokens,
    norm_gain,
    final_gain,
    gate_weight,
    up_weight,
    down_weight,
    picks,
    gates,
    target_rows,
    rest_lse,
    segment_ids,
    ref_logps,
):
    tok_rows = tokens.shape[0]
    spread = FFE // HID_DEV
    devices = lax.axis_size("expert")
    experts = devices // spread
    capacity = (tok_rows * TOPK * 5 // (experts * 4) + 3) // 4 * 4
    capacity = (capacity + 15) // 16 * 16
    own = (lax.axis_index("expert") // spread).astype(jnp.int32).reshape(1)
    picks_t = picks.T
    core, side = 1, 2
    cut_at = capacity * 5 // 8 // 16 * 16
    pieces = [(0, cut_at), (cut_at, capacity - cut_at)] if cut_at else [(0, capacity)]
    weights = (gate_weight, up_weight, down_weight)
    *near, staged = pack(own, tokens, norm_gain[None, :], picks_t, weights, experts, capacity)
    weights = [staged, swap(staged, core)]
    order = Order(own)
    far, mine, theirs, back = {}, {}, {}, {}

    def leave(k):
        near[k] = swap(order.late(near[k]), k * spread)

    def arrive(k):
        near[k] = order.mark_one(near[k])

    def share(k):
        far[k] = [swap(order.late(piece), side) for piece in order.mark(*cut(near[k], pieces))]

    def work(k):
        mine[k], theirs[k] = [], []
        for (first, _), piece in zip(pieces, far[k]):
            there = order.mark_one(piece)
            if first == 0 and k == 2:
                theirs[0] = order.mark(*theirs[0])
            part, other = order.mark(*expert_block(order.late(near[k]), first, there, weights))
            mine[k].append(part)
            theirs[k].append(swap(other, side))

    def work_whole(k):
        rows = (order.late(near[k]), 0, order.late(far[k]))
        mine[k], theirs[k] = order.mark(*expert_block(*rows, weights))

    def home(k):
        theirs[k] = order.mark(*theirs[k])
        back[k] = order.mark_one(total(mine[k], theirs[k]))

    def leave_back(k):
        back[k] = swap(order.late(back[k]), k * spread)

    def arrive_back(k):
        back[k] = order.mark_one(back[k])

    far[0], far[1] = swap(near[0], side), swap(near[1], side)
    leave(1)
    leave(2)
    far[0], weights[1] = order.mark(far[0], weights[1])
    work_whole(0)
    theirs[0] = [swap(theirs[0], side)]
    mine[0] = [mine[0]]
    arrive(2)
    arrive(1)
    far[1] = order.mark_one(far[1])
    for k in range(3, experts + 1):
        share(k - 1)
        if k < experts:
            leave(k)
        if k == 3:
            far[1] = swap(order.late(far[1]), spread)
        if k > 3:
            home(k - 2)
            leave_back(k - 2)
        if k == experts:
            far[1] = order.mark_one(far[1])
            work_whole(1)
            theirs[1] = [swap(piece, spread) for piece in order.mark(*cut(theirs[1], pieces))]
        work(k - 1)
        if k < experts:
            arrive(k)
        if k > 3:
            arrive_back(k - 2)
    theirs[1] = order.mark(*theirs[1])
    home(experts - 1)
    leave_back(experts - 1)
    mine[1] = [swap(order.late(mine[1]), spread)]
    theirs[1] = [swap(order.late(piece), side) for piece in theirs[1]]
    arrive_back(experts - 1)
    home(0)
    mine[1] = order.mark(*mine[1])
    home(1)
    blocks = [back[k] for k in range(experts)]
    local = score(
        own,
        tokens,
        final_gain[None, :],
        picks_t,
        gates.T,
        target_rows,
        rest_lse[None, :],
        segment_ids[None, :],
        blocks,
        capacity,
        (devices, ref_logps.shape[0]),
    )
    gathered = lax.all_to_all(local, "expert", split_axis=0, concat_axis=0, tiled=True)
    sequence_logps = jnp.sum(gathered, axis=0)
    margin = sequence_logps[0::2] - ref_logps[0::2] - (sequence_logps[1::2] - ref_logps[1::2])
    pair_loss = -jax.nn.log_sigmoid(BETA * margin)
    return (sequence_logps, pair_loss)


def solution(mesh):
    placed = (
        P(("group", "expert"), None),
        P(),
        P(),
        P(None, "expert"),
        P(None, "expert"),
        P("expert", None),
        P(("group", "expert"), None),
        P(("group", "expert"), None),
        P(("group", "expert"), None),
        P(("group", "expert")),
        P(("group", "expert")),
        P("group"),
    )
    return jax.shard_map(
        per_device, mesh=mesh, in_specs=placed, out_specs=(P("group"), P("group")), check_vma=False
    )
```

```python
import functools

import jax
import jax.numpy as jnp
from jax import lax
from jax.experimental import pallas as pl
from jax.experimental.pallas import tpu as pltpu
from jax.sharding import PartitionSpec as P

FFE = 2048
HID_DEV = 512
TOPK = 2

EPS = 1e-06
BETA = 0.01

F32 = jnp.float32
BF16 = jnp.bfloat16
VMEM_LIMIT = 10 * 1024 * 1024
COST = pl.CostEstimate(flops=1024, bytes_accessed=1024, transcendentals=0)


def swap(value, mask):
    pairs = [(source, source ^ mask) for source in range(lax.axis_size("expert"))]
    return lax.ppermute(value, "expert", pairs)


def iota(shape, dim):
    return lax.broadcasted_iota(jnp.int32, shape, dim)


def routing(own, picks, rows):
    tokens = picks.shape[1]
    expert = jnp.bitwise_xor(own, iota((rows, tokens), 0))
    hit = [picks[k : k + 1, :] == expert for k in range(TOPK)]
    member = hit[0] | hit[1]
    earlier = (iota((tokens, tokens), 0) < iota((tokens, tokens), 1)).astype(BF16)
    slot = jnp.dot(member.astype(F32).astype(BF16), earlier, preferred_element_type=F32)
    slot = jnp.where(member, slot.astype(jnp.int32), -1)
    return hit, slot


def pack_kernel(chunks, own_ref, tokens_hbm, gain_ref, picks_hbm, gate_hbm, up_hbm, down_hbm, *refs):
    *out_refs, weights_ref, tokens_ref, picks_ref, arrived = refs
    width, hidden = gate_hbm.shape
    moves = [(tokens_hbm, tokens_ref), (picks_hbm, picks_ref)]
    sources = [gate_hbm, up_hbm]
    sources += [down_hbm.at[:, pl.ds(first, hidden)] for first in range(0, width, hidden)]
    first = 0
    for source in sources:
        moves.append((source, weights_ref.at[pl.ds(first, source.shape[0]), :]))
        first += source.shape[0]
    copies = [pltpu.make_async_copy(*move, arrived.at[n]) for n, move in enumerate(moves)]
    for copy in copies:
        copy.start()
    copies[0].wait()
    copies[1].wait()
    tokens = tokens_ref.shape[0]
    values = tokens_ref[...].astype(F32)
    scale = lax.rsqrt(jnp.mean(values * values, axis=-1, keepdims=True) + EPS)
    normed = (values * scale * gain_ref[...]).astype(BF16)
    _, slot = routing(own_ref[0], picks_ref[...], max(8, 1 + chunks[-1][0]))
    for (k, first, count), out_ref in zip(chunks, out_refs):
        place = first + iota((count, tokens), 0)
        chosen = (slot[k : k + 1, :] == place).astype(F32).astype(BF16)
        out_ref[...] = jnp.dot(chosen, normed, preferred_element_type=F32).astype(BF16)
    for copy in copies[2:]:
        copy.wait()


def pack(own, tokens, gain, picks, weights, chunks):
    width, hidden = weights[0].shape
    smem = pl.BlockSpec(memory_space=pltpu.SMEM)
    vmem = pl.BlockSpec(memory_space=pltpu.VMEM)
    hbm = pl.BlockSpec(memory_space=pltpu.HBM)
    shapes = [(count, width) for _, _, count in chunks] + [(3 * width, hidden)]
    there = [pltpu.with_memory_space_constraint(array, pltpu.HBM) for array in (tokens, picks, *weights)]
    return pl.pallas_call(
        functools.partial(pack_kernel, chunks),
        out_shape=[jax.ShapeDtypeStruct(shape, BF16) for shape in shapes],
        in_specs=[smem, hbm, vmem, hbm] + [hbm] * 3,
        out_specs=[vmem] * len(shapes),
        scratch_shapes=[
            pltpu.VMEM(tokens.shape, BF16),
            pltpu.VMEM(picks.shape, jnp.int32),
            pltpu.SemaphoreType.DMA((4 + width // hidden,)),
        ],
        compiler_params=pltpu.CompilerParams(vmem_limit_bytes=VMEM_LIMIT),
        cost_estimate=COST,
        name="pack",
    )(own, there[0], gain, *there[1:])


def expert_kernel(near_ref, far_ref, *refs):
    *weight_refs, mine_ref, theirs_ref, rows = refs
    count = far_ref.shape[0]
    rows[:count, :] = near_ref[...]
    rows[count:, :] = far_ref[...]
    width = rows.shape[1]
    size = weight_refs[0].shape[1]
    hidden = []
    for ref in weight_refs:
        gate = jnp.dot(rows[...], ref[:width, :], preferred_element_type=F32)
        up = jnp.dot(rows[...], ref[width : 2 * width, :], preferred_element_type=F32)
        hidden.append((jax.nn.silu(gate) * up).astype(BF16))
    for start in range(0, width, size):
        part = sum(
            jnp.dot(value, ref[pl.ds(2 * width + start, size), :], preferred_element_type=F32)
            for value, ref in zip(hidden, weight_refs)
        ).astype(BF16)
        mine_ref[:, start : start + size] = part[:count]
        theirs_ref[:, start : start + size] = part[count:]


def expert_block(near, far, weights):
    count, width = far.shape
    vmem = pl.BlockSpec(memory_space=pltpu.VMEM)
    return pl.pallas_call(
        expert_kernel,
        out_shape=[jax.ShapeDtypeStruct((count, width), BF16)] * 2,
        in_specs=[vmem] * (2 + len(weights)),
        out_specs=[vmem] * 2,
        scratch_shapes=[pltpu.VMEM((2 * count, width), BF16)],
        compiler_params=pltpu.CompilerParams(vmem_limit_bytes=VMEM_LIMIT),
        cost_estimate=COST,
        name="expert_block",
    )(near, far, *weights)


def score_kernel(capacity, own_ref, tokens_ref, gain_ref, picks_ref, gates_ref, target_ref, rest_ref, seg_ref, *refs):
    *block_refs, out_ref, stacked, stream = refs
    tokens, width = tokens_ref.shape
    experts = stacked.shape[0] // capacity
    first = 0
    for ref in block_refs:
        stacked[first : first + ref.shape[0], :] = ref[...]
        first += ref.shape[0]
    hit, slot = routing(own_ref[0], picks_ref[...], max(8, experts))
    weight = sum(jnp.where(hit[k], gates_ref[k : k + 1, :], 0.0) for k in range(TOPK))
    place = iota((capacity, tokens), 0)
    parts = [
        jnp.where(slot[k : k + 1, :] == place, weight[k : k + 1, :], 0.0) for k in range(experts)
    ]
    spread = jnp.concatenate(parts, axis=0)
    coarse = spread.astype(BF16)
    fine = (spread - coarse.astype(F32)).astype(BF16)
    chunk = width // 7 if width % 7 == 0 else width
    over_rows = (((0,), (0,)), ((), ()))
    squares = jnp.zeros((tokens, 1), F32)
    for start in range(0, width, chunk):
        cols = slice(start, start + chunk)
        rows = stacked[:, cols]
        moe = lax.dot_general(coarse, rows, over_rows, preferred_element_type=F32)
        moe = moe + lax.dot_general(fine, rows, over_rows, preferred_element_type=F32)
        value = tokens_ref[:, cols].astype(F32) + moe
        stream[:, cols] = value
        squares = squares + jnp.sum(value * value, axis=-1, keepdims=True)
    scale = lax.rsqrt(squares / width + EPS)
    logit = jnp.zeros((tokens, 1), F32)
    for start in range(0, width, chunk):
        cols = slice(start, start + chunk)
        final = (stream[:, cols] * scale * gain_ref[:, cols]).astype(BF16).astype(F32)
        logit = logit + jnp.sum(final * target_ref[:, cols].astype(F32), axis=-1, keepdims=True)
    turn = iota((tokens, tokens), 0) == iota((tokens, tokens), 1)
    logit = jnp.sum(jnp.where(turn, logit, 0.0), axis=0, keepdims=True)
    gap = rest_ref[...] - logit
    token_logp = -(jnp.maximum(gap, 0.0) + jnp.log1p(jnp.exp(-jnp.abs(gap))))
    sequences = out_ref.shape[1]
    inside = iota((sequences, tokens), 0) == seg_ref[...]
    sums = jnp.sum(jnp.where(inside, token_logp, 0.0), axis=1, keepdims=True)
    turn = iota((sequences, sequences), 0) == iota((sequences, sequences), 1)
    sums = jnp.sum(jnp.where(turn, sums, 0.0), axis=0, keepdims=True)
    out_ref[...] = jnp.broadcast_to(sums, out_ref.shape)


def score(own, tokens, gain, picks, gates, target, rest, seg, blocks, capacity, outs):
    rows, width = tokens.shape
    slots = sum(block.shape[0] for block in blocks)
    smem = pl.BlockSpec(memory_space=pltpu.SMEM)
    vmem = pl.BlockSpec(memory_space=pltpu.VMEM)
    return pl.pallas_call(
        functools.partial(score_kernel, capacity),
        out_shape=jax.ShapeDtypeStruct(outs, F32),
        in_specs=[smem] + [vmem] * (7 + len(blocks)),
        out_specs=vmem,
        scratch_shapes=[
            pltpu.VMEM((slots, width), BF16),
            pltpu.VMEM((rows, width), F32),
        ],
        compiler_params=pltpu.CompilerParams(vmem_limit_bytes=VMEM_LIMIT),
        cost_estimate=COST,
        name="score",
    )(own, tokens, gain, picks, gates, target, rest, seg, *blocks)


class Order:
    def __init__(self, token):
        self.token = token

    def mark(self, *values):
        *values, self.token = lax.optimization_barrier((*values, self.token))
        return values

    def mark_one(self, value):
        return self.mark(value)[0]

    def late(self, value):
        return lax.optimization_barrier((value, self.token))[0]


def cut_kernel(whole_ref, *refs):
    first = 0
    for ref in refs:
        ref[...] = whole_ref[first : first + ref.shape[0], :]
        first += ref.shape[0]


def cut(whole, pieces):
    vmem = pl.BlockSpec(memory_space=pltpu.VMEM)
    return pl.pallas_call(
        cut_kernel,
        out_shape=[jax.ShapeDtypeStruct((count, whole.shape[1]), BF16) for _, count in pieces],
        in_specs=[vmem],
        out_specs=[vmem] * len(pieces),
        compiler_params=pltpu.CompilerParams(vmem_limit_bytes=VMEM_LIMIT),
        cost_estimate=COST,
        name="cut",
    )(whole)


def total_kernel(count, *refs):
    *refs, out_ref = refs
    for side in (refs[:count], refs[count:]):
        first = 0
        for ref in side:
            rows = slice(first, first + ref.shape[0])
            if side[0] is refs[0]:
                out_ref[rows, :] = ref[...]
            else:
                out_ref[rows, :] = (out_ref[rows, :].astype(F32) + ref[...].astype(F32)).astype(BF16)
            first += ref.shape[0]


def total(ours, others):
    rows = sum(piece.shape[0] for piece in ours)
    vmem = pl.BlockSpec(memory_space=pltpu.VMEM)
    return pl.pallas_call(
        functools.partial(total_kernel, len(ours)),
        out_shape=jax.ShapeDtypeStruct((rows, ours[0].shape[1]), BF16),
        in_specs=[vmem] * (len(ours) + len(others)),
        out_specs=vmem,
        compiler_params=pltpu.CompilerParams(vmem_limit_bytes=VMEM_LIMIT),
        cost_estimate=COST,
        name="total",
    )(*ours, *others)


def per_device(
    tokens,
    norm_gain,
    final_gain,
    gate_weight,
    up_weight,
    down_weight,
    picks,
    gates,
    target_rows,
    rest_lse,
    segment_ids,
    ref_logps,
):
    tok_rows = tokens.shape[0]
    spread = FFE // HID_DEV
    devices = lax.axis_size("expert")
    experts = devices // spread
    capacity = (tok_rows * TOPK * 5 // (experts * 4) + 3) // 4 * 4
    capacity = (capacity + 15) // 16 * 16
    own = (lax.axis_index("expert") // spread).astype(jnp.int32).reshape(1)
    picks_t = picks.T
    core, side = 1, 2
    cut_at = capacity * 5 // 8 // 16 * 16
    pieces = [(0, cut_at), (cut_at, capacity - cut_at)] if cut_at else [(0, capacity)]
    chunks = [(0, 0, capacity), (1, 0, capacity)]
    chunks += [(k, first, count) for k in range(2, experts) for first, count in pieces]
    travel = [(k, i) for k in range(2, experts) for i in range(len(pieces))]
    weights = (gate_weight, up_weight, down_weight)
    *packed, staged = pack(own, tokens, norm_gain[None, :], picks_t, weights, tuple(chunks))
    near = dict(zip([0, 1, *travel], packed))
    weights = [staged, swap(staged, core)]
    order = Order(own)
    far, mine, theirs, back = {}, {}, {}, {}

    def leave(piece):
        near[piece] = swap(order.late(near[piece]), piece[0] * spread)

    def arrive(piece):
        near[piece] = order.mark_one(near[piece])

    def share(piece):
        far[piece] = swap(order.late(near[piece]), side)

    def work(piece):
        there = order.mark_one(far[piece])
        rows = (order.late(near[piece]), there)
        mine[piece], theirs[piece] = order.mark(*expert_block(*rows, weights))

    def cross(piece):
        theirs[piece] = swap(theirs[piece], side)

    def home(k, parts):
        others = order.mark(*(theirs[part] for part in parts))
        back[k] = order.mark_one(total([mine[part] for part in parts], others))

    def leave_back(k):
        back[k] = swap(order.late(back[k]), k * spread)

    def arrive_back(k):
        back[k] = order.mark_one(back[k])

    def parts_of(k):
        return [(k, i) for i in range(len(pieces))]

    far[0], far[1] = swap(near[0], side), swap(near[1], side)
    near[1] = swap(near[1], spread)
    leave(travel[0])
    far[0] = order.mark_one(far[0])
    for n, piece in enumerate(travel):
        k, i = piece
        arrive(piece)
        if n + 1 < len(travel):
            leave(travel[n + 1])
        if k > 2 and i == len(pieces) - 1:
            if k > 3:
                arrive_back(k - 2)
            leave_back(k - 1)
        share(piece)
        if n == 0:
            weights[1] = order.mark_one(weights[1])
            work(0)
        if n == 1:
            far[1] = swap(order.late(far[1]), spread)
        if k > 2 and i == 0:
            home(k - 1, parts_of(k - 1))
        if n == len(travel) - 1:
            work(1)
            theirs[1] = [swap(part, spread) for part in order.mark(*cut(theirs[1], pieces))]
        work(piece)
        cross(piece)
        if n == 0:
            far[1], near[1] = order.mark(far[1], near[1])
        if n == len(travel) - 2:
            far[1] = order.mark_one(far[1])
    home(experts - 1, parts_of(experts - 1))
    arrive_back(experts - 2)
    leave_back(experts - 1)
    theirs[0] = swap(order.late(theirs[0]), side)
    mine[1] = swap(order.late(mine[1]), spread)
    theirs[1] = [swap(part, side) for part in order.mark(*theirs[1])]
    arrive_back(experts - 1)
    home(0, [0])
    mine[1] = order.mark_one(mine[1])
    others = order.mark(*theirs[1])
    back[1] = total([mine[1]], others)
    blocks = [back[k] for k in range(experts)]
    local = score(
        own,
        tokens,
        final_gain[None, :],
        picks_t,
        gates.T,
        target_rows,
        rest_lse[None, :],
        segment_ids[None, :],
        blocks,
        capacity,
        (devices, ref_logps.shape[0]),
    )
    gathered = lax.all_to_all(local, "expert", split_axis=0, concat_axis=0, tiled=True)
    sequence_logps = jnp.sum(gathered, axis=0)
    margin = sequence_logps[0::2] - ref_logps[0::2] - (sequence_logps[1::2] - ref_logps[1::2])
    pair_loss = -jax.nn.log_sigmoid(BETA * margin)
    return (sequence_logps, pair_loss)


def solution(mesh):
    placed = (
        P(("group", "expert"), None),
        P(),
        P(),
        P(None, "expert"),
        P(None, "expert"),
        P("expert", None),
        P(("group", "expert"), None),
        P(("group", "expert"), None),
        P(("group", "expert"), None),
        P(("group", "expert")),
        P(("group", "expert")),
        P("group"),
    )
    return jax.shard_map(
        per_device, mesh=mesh, in_specs=placed, out_specs=(P("group"), P("group")), check_vma=False
    )
```

```python
import functools

import jax
import jax.numpy as jnp
from jax import lax
from jax.experimental import pallas as pl
from jax.experimental.pallas import tpu as pltpu
from jax.sharding import PartitionSpec as P

FFE = 2048
HID_DEV = 512
TOPK = 2

EPS = 1e-06
BETA = 0.01

F32 = jnp.float32
BF16 = jnp.bfloat16
VMEM_LIMIT = 10 * 1024 * 1024
COST = pl.CostEstimate(flops=1024, bytes_accessed=1024, transcendentals=0)


def swap(value, mask):
    pairs = [(source, source ^ mask) for source in range(lax.axis_size("expert"))]
    return lax.ppermute(value, "expert", pairs)


def iota(shape, dim):
    return lax.broadcasted_iota(jnp.int32, shape, dim)


def routing(own, picks, rows):
    tokens = picks.shape[1]
    expert = jnp.bitwise_xor(own, iota((rows, tokens), 0))
    hit = [picks[k : k + 1, :] == expert for k in range(TOPK)]
    member = hit[0] | hit[1]
    earlier = (iota((tokens, tokens), 0) < iota((tokens, tokens), 1)).astype(BF16)
    slot = jnp.dot(member.astype(F32).astype(BF16), earlier, preferred_element_type=F32)
    slot = jnp.where(member, slot.astype(jnp.int32), -1)
    return hit, slot


def pack_kernel(chunks, own_ref, tokens_hbm, gain_ref, picks_hbm, *refs):
    *out_refs, tokens_ref, picks_ref, arrived = refs
    moves = [(tokens_hbm, tokens_ref), (picks_hbm, picks_ref)]
    copies = [pltpu.make_async_copy(*move, arrived.at[n]) for n, move in enumerate(moves)]
    for copy in copies:
        copy.start()
    for copy in copies:
        copy.wait()
    tokens = tokens_ref.shape[0]
    values = tokens_ref[...].astype(F32)
    scale = lax.rsqrt(jnp.mean(values * values, axis=-1, keepdims=True) + EPS)
    normed = (values * scale * gain_ref[...]).astype(BF16)
    _, slot = routing(own_ref[0], picks_ref[...], max(8, 1 + chunks[-1][-1]))
    for blocks, out_ref in zip(chunks, out_refs):
        count = out_ref.shape[0] // len(blocks)
        place = iota((count, tokens), 0)
        for n, k in enumerate(blocks):
            chosen = (slot[k : k + 1, :] == place).astype(F32).astype(BF16)
            rows = jnp.dot(chosen, normed, preferred_element_type=F32).astype(BF16)
            out_ref[n * count : (n + 1) * count, :] = rows


def in_hbm(*arrays):
    return [pltpu.with_memory_space_constraint(array, pltpu.HBM) for array in arrays]


def pack(own, tokens, gain, picks, chunks, capacity):
    width = tokens.shape[1]
    smem = pl.BlockSpec(memory_space=pltpu.SMEM)
    vmem = pl.BlockSpec(memory_space=pltpu.VMEM)
    hbm = pl.BlockSpec(memory_space=pltpu.HBM)
    tokens, picks = in_hbm(tokens, picks)
    return pl.pallas_call(
        functools.partial(pack_kernel, chunks),
        out_shape=[jax.ShapeDtypeStruct((len(blocks) * capacity, width), BF16) for blocks in chunks],
        in_specs=[smem, hbm, vmem, hbm],
        out_specs=[vmem] * len(chunks),
        scratch_shapes=[
            pltpu.VMEM(tokens.shape, BF16),
            pltpu.VMEM(picks.shape, jnp.int32),
            pltpu.SemaphoreType.DMA((2,)),
        ],
        compiler_params=pltpu.CompilerParams(vmem_limit_bytes=VMEM_LIMIT),
        cost_estimate=COST,
        name="pack",
    )(own, tokens, gain, picks)


def stage_kernel(count, *refs):
    sources, there, arrived = refs[:count], refs[count:-1], refs[-1]
    copies = [pltpu.make_async_copy(*move, arrived.at[n]) for n, move in enumerate(zip(sources, there))]
    for copy in copies:
        copy.start()
    for copy in copies:
        copy.wait()


def stage(arrays, memory):
    vmem = pl.BlockSpec(memory_space=pltpu.VMEM)
    there = pl.BlockSpec(memory_space=memory)
    return pl.pallas_call(
        functools.partial(stage_kernel, len(arrays)),
        out_shape=[pltpu.VMEM(array.shape, array.dtype) for array in arrays],
        in_specs=[there] * len(arrays),
        out_specs=[vmem] * len(arrays),
        scratch_shapes=[pltpu.SemaphoreType.DMA((len(arrays),))],
        compiler_params=pltpu.CompilerParams(vmem_limit_bytes=VMEM_LIMIT),
        cost_estimate=COST,
        name="stage",
    )(*arrays)


def expert_kernel(near_first, far_first, near_ref, far_ref, *refs):
    *weight_refs, mine_ref, theirs_ref, rows = refs
    count, width = mine_ref.shape
    rows[:count, :] = near_ref[near_first : near_first + count, :]
    rows[count:, :] = far_ref[far_first : far_first + count, :]
    size = weight_refs[0].shape[1]
    slices = [weight_refs[n : n + 3] for n in range(0, len(weight_refs), 3)]
    hidden = []
    for gate_ref, up_ref, _ in slices:
        gate = jnp.dot(rows[...], gate_ref[...], preferred_element_type=F32)
        up = jnp.dot(rows[...], up_ref[...], preferred_element_type=F32)
        hidden.append((jax.nn.silu(gate) * up).astype(BF16))
    for start in range(0, width, size):
        cols = slice(start, start + size)
        part = sum(
            jnp.dot(value, down_ref[:, cols], preferred_element_type=F32)
            for value, (_, _, down_ref) in zip(hidden, slices)
        ).astype(BF16)
        mine_ref[:, cols] = part[:count]
        theirs_ref[:, cols] = part[count:]


def expert_block(near, far, weights, count, near_first=0, far_first=0):
    width = far.shape[1]
    vmem = pl.BlockSpec(memory_space=pltpu.VMEM)
    return pl.pallas_call(
        functools.partial(expert_kernel, near_first, far_first),
        out_shape=[jax.ShapeDtypeStruct((count, width), BF16)] * 2,
        in_specs=[vmem] * (2 + len(weights)),
        out_specs=[vmem] * 2,
        scratch_shapes=[pltpu.VMEM((2 * count, width), BF16)],
        compiler_params=pltpu.CompilerParams(vmem_limit_bytes=VMEM_LIMIT),
        cost_estimate=COST,
        name="expert_block",
    )(near, far, *weights)


def score_kernel(capacity, own_ref, tokens_ref, gain_ref, picks_ref, gates_ref, target_ref, rest_ref, seg_ref, *refs):
    *block_refs, out_ref, stacked, stream = refs
    tokens, width = tokens_ref.shape
    experts = stacked.shape[0] // capacity
    first = 0
    for ref in block_refs:
        stacked[first : first + ref.shape[0], :] = ref[...]
        first += ref.shape[0]
    hit, slot = routing(own_ref[0], picks_ref[...], max(8, experts))
    weight = sum(jnp.where(hit[k], gates_ref[k : k + 1, :], 0.0) for k in range(TOPK))
    place = iota((capacity, tokens), 0)
    parts = [
        jnp.where(slot[k : k + 1, :] == place, weight[k : k + 1, :], 0.0) for k in range(experts)
    ]
    spread = jnp.concatenate(parts, axis=0)
    coarse = spread.astype(BF16)
    fine = (spread - coarse.astype(F32)).astype(BF16)
    chunk = width // 7 if width % 7 == 0 else width
    over_rows = (((0,), (0,)), ((), ()))
    squares = jnp.zeros((tokens, 1), F32)
    for start in range(0, width, chunk):
        cols = slice(start, start + chunk)
        rows = stacked[:, cols]
        moe = lax.dot_general(coarse, rows, over_rows, preferred_element_type=F32)
        moe = moe + lax.dot_general(fine, rows, over_rows, preferred_element_type=F32)
        value = tokens_ref[:, cols].astype(F32) + moe
        stream[:, cols] = value
        squares = squares + jnp.sum(value * value, axis=-1, keepdims=True)
    scale = lax.rsqrt(squares / width + EPS)
    logit = jnp.zeros((tokens, 1), F32)
    for start in range(0, width, chunk):
        cols = slice(start, start + chunk)
        final = (stream[:, cols] * scale * gain_ref[:, cols]).astype(BF16).astype(F32)
        logit = logit + jnp.sum(final * target_ref[:, cols].astype(F32), axis=-1, keepdims=True)
    turn = iota((tokens, tokens), 0) == iota((tokens, tokens), 1)
    logit = jnp.sum(jnp.where(turn, logit, 0.0), axis=0, keepdims=True)
    gap = rest_ref[...] - logit
    token_logp = -(jnp.maximum(gap, 0.0) + jnp.log1p(jnp.exp(-jnp.abs(gap))))
    sequences = out_ref.shape[1]
    inside = iota((sequences, tokens), 0) == seg_ref[...]
    sums = jnp.sum(jnp.where(inside, token_logp, 0.0), axis=1, keepdims=True)
    turn = iota((sequences, sequences), 0) == iota((sequences, sequences), 1)
    sums = jnp.sum(jnp.where(turn, sums, 0.0), axis=0, keepdims=True)
    out_ref[...] = jnp.broadcast_to(sums, out_ref.shape)


def score(own, tokens, gain, picks, gates, target, rest, seg, blocks, capacity, outs):
    rows, width = tokens.shape
    slots = sum(block.shape[0] for block in blocks)
    smem = pl.BlockSpec(memory_space=pltpu.SMEM)
    vmem = pl.BlockSpec(memory_space=pltpu.VMEM)
    return pl.pallas_call(
        functools.partial(score_kernel, capacity),
        out_shape=jax.ShapeDtypeStruct(outs, F32),
        in_specs=[smem] + [vmem] * (7 + len(blocks)),
        out_specs=vmem,
        scratch_shapes=[
            pltpu.VMEM((slots, width), BF16),
            pltpu.VMEM((rows, width), F32),
        ],
        compiler_params=pltpu.CompilerParams(vmem_limit_bytes=VMEM_LIMIT),
        cost_estimate=COST,
        name="score",
    )(own, tokens, gain, picks, gates, target, rest, seg, *blocks)


class Order:
    def __init__(self, token):
        self.token = token

    def mark(self, *values):
        *values, self.token = lax.optimization_barrier((*values, self.token))
        return values

    def mark_one(self, value):
        return self.mark(value)[0]

    def late(self, value):
        return lax.optimization_barrier((value, self.token))[0]


def cut_kernel(pieces, whole_ref, *refs):
    for (first, count), ref in zip(pieces, refs):
        ref[...] = whole_ref[first : first + count, :]


def cut(whole, pieces):
    vmem = pl.BlockSpec(memory_space=pltpu.VMEM)
    return pl.pallas_call(
        functools.partial(cut_kernel, pieces),
        out_shape=[jax.ShapeDtypeStruct((count, whole.shape[1]), BF16) for _, count in pieces],
        in_specs=[vmem],
        out_specs=[vmem] * len(pieces),
        compiler_params=pltpu.CompilerParams(vmem_limit_bytes=VMEM_LIMIT),
        cost_estimate=COST,
        name="cut",
    )(whole)


def total_kernel(count, *refs):
    *refs, out_ref = refs
    for side in (refs[:count], refs[count:]):
        first = 0
        for ref in side:
            rows = slice(first, first + ref.shape[0])
            if side[0] is refs[0]:
                out_ref[rows, :] = ref[...]
            else:
                out_ref[rows, :] = (out_ref[rows, :].astype(F32) + ref[...].astype(F32)).astype(BF16)
            first += ref.shape[0]


def total(ours, others):
    rows = sum(piece.shape[0] for piece in ours)
    vmem = pl.BlockSpec(memory_space=pltpu.VMEM)
    return pl.pallas_call(
        functools.partial(total_kernel, len(ours)),
        out_shape=jax.ShapeDtypeStruct((rows, ours[0].shape[1]), BF16),
        in_specs=[vmem] * (len(ours) + len(others)),
        out_specs=vmem,
        compiler_params=pltpu.CompilerParams(vmem_limit_bytes=VMEM_LIMIT),
        cost_estimate=COST,
        name="total",
    )(*ours, *others)


def per_device(
    tokens,
    norm_gain,
    final_gain,
    gate_weight,
    up_weight,
    down_weight,
    picks,
    gates,
    target_rows,
    rest_lse,
    segment_ids,
    ref_logps,
):
    tok_rows = tokens.shape[0]
    spread = FFE // HID_DEV
    devices = lax.axis_size("expert")
    experts = devices // spread
    capacity = (tok_rows * TOPK * 5 // (experts * 4) + 3) // 4 * 4
    capacity = (capacity + 15) // 16 * 16
    own = (lax.axis_index("expert") // spread).astype(jnp.int32).reshape(1)
    picks_t = picks.T
    core, side = 1, 2
    cut_at = capacity * 5 // 8 // 16 * 16
    pieces = ((0, cut_at), (cut_at, capacity - cut_at)) if cut_at else ((0, capacity),)
    weights = [gate_weight, up_weight, down_weight]
    swapped = [swap(weight, core) for weight in weights]
    chunks = ((0, 1), (1,)) + tuple((k,) for k in range(2, experts))
    both, *near = pack(own, tokens, norm_gain[None, :], picks_t, chunks, capacity)
    near = [both, *near]
    order = Order(own)
    far, mine, theirs, back = {}, {}, {}, {}

    def leave(k):
        near[k] = swap(order.late(near[k]), k * spread)

    def arrive(k):
        near[k] = order.mark_one(near[k])

    def share(k):
        far[k] = [swap(order.late(piece), side) for piece in order.mark(*cut(near[k], pieces))]

    def work(k):
        mine[k], theirs[k] = [], []
        for (first, count), piece in zip(pieces, far[k]):
            there = order.mark_one(piece)
            rows = (order.late(near[k]), there)
            part, other = order.mark(*expert_block(*rows, weights, count, near_first=first))
            mine[k].append(part)
            theirs[k].append(swap(other, side))

    def home(k):
        theirs[k] = order.mark(*theirs[k])
        back[k] = order.mark_one(total(mine[k], theirs[k]))

    def leave_back(k):
        back[k] = swap(order.late(back[k]), k * spread)

    def arrive_back(k):
        back[k] = order.mark_one(back[k])

    both_far = swap(both, side)
    leave(2)
    weights = order.mark(*stage(in_hbm(*(order.late(weight) for weight in weights)), pltpu.HBM))
    weights += order.mark(*stage(order.mark(*swapped), pl.ANY))
    arrive(2)
    for k in range(3, experts + 1):
        share(k - 1)
        if k < experts:
            leave(k)
        if k == 3:
            leave(1)
            both_far = order.mark_one(both_far)
            far[1] = swap(order.mark_one(cut(both_far, ((capacity, capacity),))[0]), spread)
            mine[0], theirs[0] = order.mark(*expert_block(both, both_far, weights, capacity))
        if k > 3:
            home(k - 2)
            leave_back(k - 2)
        if k == experts:
            mine[1], theirs[1] = order.mark(*expert_block(near[1], far[1], weights, capacity))
            theirs[1] = [swap(piece, spread) for piece in order.mark(*cut(theirs[1], pieces))]
            mine[1] = swap(mine[1], spread)
        work(k - 1)
        if k < experts:
            arrive(k)
        if k == 3:
            near[1], far[1] = order.mark(near[1], far[1])
        if k > 3:
            arrive_back(k - 2)
    home(experts - 1)
    leave_back(experts - 1)
    mine[1], *theirs[1] = order.mark(mine[1], *theirs[1])
    mine[1] = [mine[1]]
    theirs[1] = [swap(order.late(piece), side) for piece in theirs[1]]
    mine[0], theirs[0] = [mine[0]], [swap(order.late(theirs[0]), side)]
    arrive_back(experts - 1)
    home(0)
    home(1)
    blocks = [back[k] for k in range(experts)]
    local = score(
        own,
        tokens,
        final_gain[None, :],
        picks_t,
        gates.T,
        target_rows,
        rest_lse[None, :],
        segment_ids[None, :],
        blocks,
        capacity,
        (devices, ref_logps.shape[0]),
    )
    gathered = lax.all_to_all(local, "expert", split_axis=0, concat_axis=0, tiled=True)
    sequence_logps = jnp.sum(gathered, axis=0)
    margin = sequence_logps[0::2] - ref_logps[0::2] - (sequence_logps[1::2] - ref_logps[1::2])
    pair_loss = -jax.nn.log_sigmoid(BETA * margin)
    return (sequence_logps, pair_loss)


def solution(mesh):
    placed = (
        P(("group", "expert"), None),
        P(),
        P(),
        P(None, "expert"),
        P(None, "expert"),
        P("expert", None),
        P(("group", "expert"), None),
        P(("group", "expert"), None),
        P(("group", "expert"), None),
        P(("group", "expert")),
        P(("group", "expert")),
        P("group"),
    )
    return jax.shard_map(
        per_device, mesh=mesh, in_specs=placed, out_specs=(P("group"), P("group")), check_vma=False
    )
```

```python
import functools

import jax
import jax.numpy as jnp
from jax import lax
from jax.experimental import pallas as pl
from jax.experimental.pallas import tpu as pltpu
from jax.sharding import PartitionSpec as P

FFE = 2048
HID_DEV = 512
TOPK = 2

EPS = 1e-06
BETA = 0.01

F32 = jnp.float32
BF16 = jnp.bfloat16
VMEM_LIMIT = 10 * 1024 * 1024
COST = pl.CostEstimate(flops=1024, bytes_accessed=1024, transcendentals=0)


def swap(value, mask):
    pairs = [(source, source ^ mask) for source in range(lax.axis_size("expert"))]
    return lax.ppermute(value, "expert", pairs)


def iota(shape, dim):
    return lax.broadcasted_iota(jnp.int32, shape, dim)


def routing(own, picks, rows):
    tokens = picks.shape[1]
    expert = jnp.bitwise_xor(own, iota((rows, tokens), 0))
    hit = [picks[k : k + 1, :] == expert for k in range(TOPK)]
    member = hit[0] | hit[1]
    earlier = (iota((tokens, tokens), 0) < iota((tokens, tokens), 1)).astype(BF16)
    slot = jnp.dot(member.astype(F32).astype(BF16), earlier, preferred_element_type=F32)
    slot = jnp.where(member, slot.astype(jnp.int32), -1)
    return hit, slot


def pack_kernel(own_ref, tokens_hbm, gain_ref, picks_hbm, gate_hbm, up_hbm, down_hbm, *refs):
    *out_refs, weights_ref, tokens_ref, picks_ref, arrived = refs
    width, hidden = gate_hbm.shape
    moves = [(tokens_hbm, tokens_ref), (picks_hbm, picks_ref)]
    sources = [gate_hbm, up_hbm]
    sources += [down_hbm.at[:, pl.ds(first, hidden)] for first in range(0, width, hidden)]
    first = 0
    for source in sources:
        moves.append((source, weights_ref.at[pl.ds(first, source.shape[0]), :]))
        first += source.shape[0]
    copies = [pltpu.make_async_copy(*move, arrived.at[n]) for n, move in enumerate(moves)]
    for copy in copies:
        copy.start()
    copies[0].wait()
    copies[1].wait()
    tokens = tokens_ref.shape[0]
    values = tokens_ref[...].astype(F32)
    scale = lax.rsqrt(jnp.mean(values * values, axis=-1, keepdims=True) + EPS)
    normed = (values * scale * gain_ref[...]).astype(BF16)
    _, slot = routing(own_ref[0], picks_ref[...], max(8, len(out_refs)))
    for k, out_ref in enumerate(out_refs):
        place = iota((out_ref.shape[0], tokens), 0)
        chosen = (slot[k : k + 1, :] == place).astype(F32).astype(BF16)
        out_ref[...] = jnp.dot(chosen, normed, preferred_element_type=F32).astype(BF16)
    for copy in copies[2:]:
        copy.wait()


def pack(own, tokens, gain, picks, weights, experts, capacity):
    width, hidden = weights[0].shape
    smem = pl.BlockSpec(memory_space=pltpu.SMEM)
    vmem = pl.BlockSpec(memory_space=pltpu.VMEM)
    hbm = pl.BlockSpec(memory_space=pltpu.HBM)
    shapes = [(capacity, width)] * experts + [(3 * width, hidden)]
    there = [pltpu.with_memory_space_constraint(array, pltpu.HBM) for array in (tokens, picks, *weights)]
    return pl.pallas_call(
        pack_kernel,
        out_shape=[jax.ShapeDtypeStruct(shape, BF16) for shape in shapes],
        in_specs=[smem, hbm, vmem, hbm] + [hbm] * 3,
        out_specs=[vmem] * len(shapes),
        scratch_shapes=[
            pltpu.VMEM(tokens.shape, BF16),
            pltpu.VMEM(picks.shape, jnp.int32),
            pltpu.SemaphoreType.DMA((4 + width // hidden,)),
        ],
        compiler_params=pltpu.CompilerParams(vmem_limit_bytes=VMEM_LIMIT),
        cost_estimate=COST,
        name="pack",
    )(own, there[0], gain, *there[1:])


def expert_kernel(first, near_ref, far_ref, *refs):
    *weight_refs, mine_ref, theirs_ref, rows = refs
    count = far_ref.shape[0]
    rows[:count, :] = near_ref[first : first + count, :]
    rows[count:, :] = far_ref[...]
    width = rows.shape[1]
    size = weight_refs[0].shape[1]
    hidden = []
    for ref in weight_refs:
        gate = jnp.dot(rows[...], ref[:width, :], preferred_element_type=F32)
        up = jnp.dot(rows[...], ref[width : 2 * width, :], preferred_element_type=F32)
        hidden.append((jax.nn.silu(gate) * up).astype(BF16))
    for start in range(0, width, size):
        part = sum(
            jnp.dot(value, ref[pl.ds(2 * width + start, size), :], preferred_element_type=F32)
            for value, ref in zip(hidden, weight_refs)
        ).astype(BF16)
        mine_ref[:, start : start + size] = part[:count]
        theirs_ref[:, start : start + size] = part[count:]


def expert_block(near, first, far, weights):
    count, width = far.shape
    vmem = pl.BlockSpec(memory_space=pltpu.VMEM)
    return pl.pallas_call(
        functools.partial(expert_kernel, first),
        out_shape=[jax.ShapeDtypeStruct((count, width), BF16)] * 2,
        in_specs=[vmem] * (2 + len(weights)),
        out_specs=[vmem] * 2,
        scratch_shapes=[pltpu.VMEM((2 * count, width), BF16)],
        compiler_params=pltpu.CompilerParams(vmem_limit_bytes=VMEM_LIMIT),
        cost_estimate=COST,
        name="expert_block",
    )(near, far, *weights)


def score_kernel(capacity, own_ref, tokens_ref, gain_ref, picks_ref, gates_ref, target_ref, rest_ref, seg_ref, *refs):
    *block_refs, out_ref, stacked, stream = refs
    tokens, width = tokens_ref.shape
    experts = stacked.shape[0] // capacity
    first = 0
    for ref in block_refs:
        stacked[first : first + ref.shape[0], :] = ref[...]
        first += ref.shape[0]
    hit, slot = routing(own_ref[0], picks_ref[...], max(8, experts))
    weight = sum(jnp.where(hit[k], gates_ref[k : k + 1, :], 0.0) for k in range(TOPK))
    place = iota((capacity, tokens), 0)
    parts = [
        jnp.where(slot[k : k + 1, :] == place, weight[k : k + 1, :], 0.0) for k in range(experts)
    ]
    spread = jnp.concatenate(parts, axis=0)
    coarse = spread.astype(BF16)
    fine = (spread - coarse.astype(F32)).astype(BF16)
    chunk = width // 7 if width % 7 == 0 else width
    over_rows = (((0,), (0,)), ((), ()))
    squares = jnp.zeros((tokens, 1), F32)
    for start in range(0, width, chunk):
        cols = slice(start, start + chunk)
        rows = stacked[:, cols]
        moe = lax.dot_general(coarse, rows, over_rows, preferred_element_type=F32)
        moe = moe + lax.dot_general(fine, rows, over_rows, preferred_element_type=F32)
        value = tokens_ref[:, cols].astype(F32) + moe
        stream[:, cols] = value
        squares = squares + jnp.sum(value * value, axis=-1, keepdims=True)
    scale = lax.rsqrt(squares / width + EPS)
    logit = jnp.zeros((tokens, 1), F32)
    for start in range(0, width, chunk):
        cols = slice(start, start + chunk)
        final = (stream[:, cols] * scale * gain_ref[:, cols]).astype(BF16).astype(F32)
        logit = logit + jnp.sum(final * target_ref[:, cols].astype(F32), axis=-1, keepdims=True)
    turn = iota((tokens, tokens), 0) == iota((tokens, tokens), 1)
    logit = jnp.sum(jnp.where(turn, logit, 0.0), axis=0, keepdims=True)
    gap = rest_ref[...] - logit
    token_logp = -(jnp.maximum(gap, 0.0) + jnp.log1p(jnp.exp(-jnp.abs(gap))))
    sequences = out_ref.shape[1]
    inside = iota((sequences, tokens), 0) == seg_ref[...]
    sums = jnp.sum(jnp.where(inside, token_logp, 0.0), axis=1, keepdims=True)
    turn = iota((sequences, sequences), 0) == iota((sequences, sequences), 1)
    sums = jnp.sum(jnp.where(turn, sums, 0.0), axis=0, keepdims=True)
    out_ref[...] = jnp.broadcast_to(sums, out_ref.shape)


def score(own, tokens, gain, picks, gates, target, rest, seg, blocks, capacity, outs):
    rows, width = tokens.shape
    slots = sum(block.shape[0] for block in blocks)
    smem = pl.BlockSpec(memory_space=pltpu.SMEM)
    vmem = pl.BlockSpec(memory_space=pltpu.VMEM)
    return pl.pallas_call(
        functools.partial(score_kernel, capacity),
        out_shape=jax.ShapeDtypeStruct(outs, F32),
        in_specs=[smem] + [vmem] * (7 + len(blocks)),
        out_specs=vmem,
        scratch_shapes=[
            pltpu.VMEM((slots, width), BF16),
            pltpu.VMEM((rows, width), F32),
        ],
        compiler_params=pltpu.CompilerParams(vmem_limit_bytes=VMEM_LIMIT),
        cost_estimate=COST,
        name="score",
    )(own, tokens, gain, picks, gates, target, rest, seg, *blocks)


class Order:
    def __init__(self, token):
        self.token = token

    def mark(self, *values):
        *values, self.token = lax.optimization_barrier((*values, self.token))
        return values

    def mark_one(self, value):
        return self.mark(value)[0]

    def late(self, value):
        return lax.optimization_barrier((value, self.token))[0]


def cut_kernel(whole_ref, *refs):
    first = 0
    for ref in refs:
        ref[...] = whole_ref[first : first + ref.shape[0], :]
        first += ref.shape[0]


def cut(whole, pieces):
    vmem = pl.BlockSpec(memory_space=pltpu.VMEM)
    return pl.pallas_call(
        cut_kernel,
        out_shape=[jax.ShapeDtypeStruct((count, whole.shape[1]), BF16) for _, count in pieces],
        in_specs=[vmem],
        out_specs=[vmem] * len(pieces),
        compiler_params=pltpu.CompilerParams(vmem_limit_bytes=VMEM_LIMIT),
        cost_estimate=COST,
        name="cut",
    )(whole)


def total_kernel(count, *refs):
    *refs, out_ref = refs
    for side in (refs[:count], refs[count:]):
        first = 0
        for ref in side:
            rows = slice(first, first + ref.shape[0])
            if side[0] is refs[0]:
                out_ref[rows, :] = ref[...]
            else:
                out_ref[rows, :] = (out_ref[rows, :].astype(F32) + ref[...].astype(F32)).astype(BF16)
            first += ref.shape[0]


def total(ours, others):
    rows = sum(piece.shape[0] for piece in ours)
    vmem = pl.BlockSpec(memory_space=pltpu.VMEM)
    return pl.pallas_call(
        functools.partial(total_kernel, len(ours)),
        out_shape=jax.ShapeDtypeStruct((rows, ours[0].shape[1]), BF16),
        in_specs=[vmem] * (len(ours) + len(others)),
        out_specs=vmem,
        compiler_params=pltpu.CompilerParams(vmem_limit_bytes=VMEM_LIMIT),
        cost_estimate=COST,
        name="total",
    )(*ours, *others)


def per_device(
    tokens,
    norm_gain,
    final_gain,
    gate_weight,
    up_weight,
    down_weight,
    picks,
    gates,
    target_rows,
    rest_lse,
    segment_ids,
    ref_logps,
):
    tok_rows = tokens.shape[0]
    spread = FFE // HID_DEV
    devices = lax.axis_size("expert")
    experts = devices // spread
    capacity = (tok_rows * TOPK * 5 // (experts * 4) + 3) // 4 * 4
    capacity = (capacity + 15) // 16 * 16
    own = (lax.axis_index("expert") // spread).astype(jnp.int32).reshape(1)
    picks_t = picks.T
    core, side = 1, 2
    cut_at = capacity * 5 // 8 // 16 * 16
    pieces = [(0, cut_at), (cut_at, capacity - cut_at)] if cut_at else [(0, capacity)]
    weights = (gate_weight, up_weight, down_weight)
    *near, staged = pack(own, tokens, norm_gain[None, :], picks_t, weights, experts, capacity)
    weights = [staged, swap(staged, core)]
    order = Order(own)
    far, mine, theirs, back = {}, {}, {}, {}

    def leave(k):
        near[k] = swap(order.late(near[k]), k * spread)

    def arrive(k):
        near[k] = order.mark_one(near[k])

    def share(k):
        far[k] = [swap(order.late(piece), side) for piece in order.mark(*cut(near[k], pieces))]

    def work(k):
        mine[k], theirs[k] = [], []
        for (first, _), piece in zip(pieces, far[k]):
            there = order.mark_one(piece)
            part, other = order.mark(*expert_block(order.late(near[k]), first, there, weights))
            mine[k].append(part)
            theirs[k].append(swap(other, side))

    def work_whole(k):
        rows = (order.late(near[k]), 0, order.late(far[k]))
        mine[k], theirs[k] = order.mark(*expert_block(*rows, weights))

    def home(k):
        theirs[k] = order.mark(*theirs[k])
        back[k] = order.mark_one(total(mine[k], theirs[k]))

    def leave_back(k):
        back[k] = swap(order.late(back[k]), k * spread)

    def arrive_back(k):
        back[k] = order.mark_one(back[k])

    leave(2)
    far[0], far[1] = swap(near[0], side), swap(near[1], side)
    leave(1)
    arrive(2)
    far[0] = order.mark_one(far[0])
    far[1] = order.mark_one(far[1])
    arrive(1)
    for k in range(3, experts + 1):
        share(k - 1)
        if k < experts:
            leave(k)
        if k == 3:
            far[1] = swap(order.late(far[1]), spread)
        if k > 3:
            home(k - 2)
            leave_back(k - 2)
        if k == experts:
            far[1] = order.mark_one(far[1])
            work_whole(1)
            theirs[1] = swap(theirs[1], spread)
        work(k - 1)
        if k == experts:
            work_whole(0)
        if k < experts:
            arrive(k)
        if k > 3:
            arrive_back(k - 2)
    home(experts - 1)
    leave_back(experts - 1)
    mine[0], theirs[0] = [mine[0]], [swap(order.late(theirs[0]), side)]
    mine[1] = [swap(order.late(mine[1]), spread)]
    theirs[1] = order.mark(*cut(order.mark_one(theirs[1]), pieces))
    theirs[1] = [swap(order.late(piece), side) for piece in theirs[1]]
    order = Order(own)
    arrive_back(experts - 1)
    theirs[0] = order.mark(*theirs[0])
    mine[1] = order.mark(*mine[1])
    own = order.token
    back[0], back[1] = total(mine[0], theirs[0]), total(mine[1], theirs[1])
    blocks = [back[k] for k in range(experts)]
    local = score(
        own,
        tokens,
        final_gain[None, :],
        picks_t,
        gates.T,
        target_rows,
        rest_lse[None, :],
        segment_ids[None, :],
        blocks,
        capacity,
        (devices, ref_logps.shape[0]),
    )
    gathered = lax.all_to_all(local, "expert", split_axis=0, concat_axis=0, tiled=True)
    sequence_logps = jnp.sum(gathered, axis=0)
    margin = sequence_logps[0::2] - ref_logps[0::2] - (sequence_logps[1::2] - ref_logps[1::2])
    pair_loss = -jax.nn.log_sigmoid(BETA * margin)
    return (sequence_logps, pair_loss)


def solution(mesh):
    placed = (
        P(("group", "expert"), None),
        P(),
        P(),
        P(None, "expert"),
        P(None, "expert"),
        P("expert", None),
        P(("group", "expert"), None),
        P(("group", "expert"), None),
        P(("group", "expert"), None),
        P(("group", "expert")),
        P(("group", "expert")),
        P("group"),
    )
    return jax.shard_map(
        per_device, mesh=mesh, in_specs=placed, out_specs=(P("group"), P("group")), check_vma=False
    )
```

```python
import functools

import jax
import jax.numpy as jnp
from jax import lax
from jax.experimental import pallas as pl
from jax.experimental.pallas import tpu as pltpu
from jax.sharding import PartitionSpec as P

FFE = 2048
HID_DEV = 512
TOPK = 2

EPS = 1e-06
BETA = 0.01

F32 = jnp.float32
BF16 = jnp.bfloat16
VMEM_LIMIT = 10 * 1024 * 1024
COST = pl.CostEstimate(flops=1024, bytes_accessed=1024, transcendentals=0)


def swap(value, mask):
    pairs = [(source, source ^ mask) for source in range(lax.axis_size("expert"))]
    return lax.ppermute(value, "expert", pairs)


def iota(shape, dim):
    return lax.broadcasted_iota(jnp.int32, shape, dim)


def routing(own, picks, rows):
    tokens = picks.shape[1]
    expert = jnp.bitwise_xor(own, iota((rows, tokens), 0))
    hit = [picks[k : k + 1, :] == expert for k in range(TOPK)]
    member = hit[0] | hit[1]
    earlier = (iota((tokens, tokens), 0) < iota((tokens, tokens), 1)).astype(BF16)
    slot = jnp.dot(member.astype(F32).astype(BF16), earlier, preferred_element_type=F32)
    slot = jnp.where(member, slot.astype(jnp.int32), -1)
    return hit, slot


def pack_kernel(own_ref, tokens_hbm, gain_hbm, picks_hbm, gate_hbm, up_hbm, down_hbm, *refs):
    *out_refs, weights_ref, tokens_ref, gain_ref, picks_ref, arrived = refs
    width, hidden = gate_hbm.shape
    moves = [(tokens_hbm, tokens_ref), (gain_hbm, gain_ref), (picks_hbm, picks_ref)]
    sources = [gate_hbm, up_hbm]
    sources += [down_hbm.at[:, pl.ds(first, hidden)] for first in range(0, width, hidden)]
    first = 0
    for source in sources:
        moves.append((source, weights_ref.at[pl.ds(first, source.shape[0]), :]))
        first += source.shape[0]
    copies = [pltpu.make_async_copy(*move, arrived.at[n]) for n, move in enumerate(moves)]
    for copy in copies:
        copy.start()
    for copy in copies[:3]:
        copy.wait()
    tokens = tokens_ref.shape[0]
    values = tokens_ref[...].astype(F32)
    scale = lax.rsqrt(jnp.mean(values * values, axis=-1, keepdims=True) + EPS)
    normed = (values * scale * gain_ref[...][None, :]).astype(BF16)
    _, slot = routing(own_ref[0], picks_ref[...], max(8, len(out_refs)))
    for k, out_ref in enumerate(out_refs):
        place = iota((out_ref.shape[0], tokens), 0)
        chosen = (slot[k : k + 1, :] == place).astype(F32).astype(BF16)
        out_ref[...] = jnp.dot(chosen, normed, preferred_element_type=F32).astype(BF16)
    for copy in copies[3:]:
        copy.wait()


def pack(own, tokens, gain, picks, weights, experts, capacity):
    width, hidden = weights[0].shape
    smem = pl.BlockSpec(memory_space=pltpu.SMEM)
    vmem = pl.BlockSpec(memory_space=pltpu.VMEM)
    hbm = pl.BlockSpec(memory_space=pltpu.HBM)
    shapes = [(capacity, width)] * experts + [(3 * width, hidden)]
    there = [pltpu.with_memory_space_constraint(array, pltpu.HBM) for array in (tokens, gain, picks, *weights)]
    return pl.pallas_call(
        pack_kernel,
        out_shape=[jax.ShapeDtypeStruct(shape, BF16) for shape in shapes],
        in_specs=[smem] + [hbm] * 6,
        out_specs=[vmem] * len(shapes),
        scratch_shapes=[
            pltpu.VMEM(tokens.shape, BF16),
            pltpu.VMEM(gain.shape, F32),
            pltpu.VMEM(picks.shape, jnp.int32),
            pltpu.SemaphoreType.DMA((5 + width // hidden,)),
        ],
        compiler_params=pltpu.CompilerParams(vmem_limit_bytes=VMEM_LIMIT),
        cost_estimate=COST,
        name="pack",
    )(own, *there)


def expert_kernel(first, near_ref, far_ref, *refs):
    *weight_refs, mine_ref, theirs_ref, rows = refs
    count = far_ref.shape[0]
    rows[:count, :] = near_ref[first : first + count, :]
    rows[count:, :] = far_ref[...]
    width = rows.shape[1]
    size = weight_refs[0].shape[1]
    hidden = []
    for ref in weight_refs:
        gate = jnp.dot(rows[...], ref[:width, :], preferred_element_type=F32)
        up = jnp.dot(rows[...], ref[width : 2 * width, :], preferred_element_type=F32)
        hidden.append((jax.nn.silu(gate) * up).astype(BF16))
    for start in range(0, width, size):
        part = sum(
            jnp.dot(value, ref[pl.ds(2 * width + start, size), :], preferred_element_type=F32)
            for value, ref in zip(hidden, weight_refs)
        ).astype(BF16)
        mine_ref[:, start : start + size] = part[:count]
        theirs_ref[:, start : start + size] = part[count:]


def expert_block(near, first, far, weights):
    count, width = far.shape
    vmem = pl.BlockSpec(memory_space=pltpu.VMEM)
    return pl.pallas_call(
        functools.partial(expert_kernel, first),
        out_shape=[jax.ShapeDtypeStruct((count, width), BF16)] * 2,
        in_specs=[vmem] * (2 + len(weights)),
        out_specs=[vmem] * 2,
        scratch_shapes=[pltpu.VMEM((2 * count, width), BF16)],
        compiler_params=pltpu.CompilerParams(vmem_limit_bytes=VMEM_LIMIT),
        cost_estimate=COST,
        name="expert_block",
    )(near, far, *weights)


def score_kernel(capacity, own_ref, tokens_ref, gain_ref, picks_ref, gates_ref, target_ref, rest_ref, seg_ref, *refs):
    *block_refs, out_ref, stacked, stream = refs
    tokens, width = tokens_ref.shape
    experts = stacked.shape[0] // capacity
    first = 0
    for ref in block_refs:
        stacked[first : first + ref.shape[0], :] = ref[...]
        first += ref.shape[0]
    hit, slot = routing(own_ref[0], picks_ref[...], max(8, experts))
    weight = sum(jnp.where(hit[k], gates_ref[k : k + 1, :], 0.0) for k in range(TOPK))
    place = iota((capacity, tokens), 0)
    parts = [
        jnp.where(slot[k : k + 1, :] == place, weight[k : k + 1, :], 0.0) for k in range(experts)
    ]
    spread = jnp.concatenate(parts, axis=0)
    coarse = spread.astype(BF16)
    fine = (spread - coarse.astype(F32)).astype(BF16)
    chunk = width // 7 if width % 7 == 0 else width
    over_rows = (((0,), (0,)), ((), ()))
    squares = jnp.zeros((tokens, 1), F32)
    for start in range(0, width, chunk):
        cols = slice(start, start + chunk)
        rows = stacked[:, cols]
        moe = lax.dot_general(coarse, rows, over_rows, preferred_element_type=F32)
        moe = moe + lax.dot_general(fine, rows, over_rows, preferred_element_type=F32)
        value = tokens_ref[:, cols].astype(F32) + moe
        stream[:, cols] = value
        squares = squares + jnp.sum(value * value, axis=-1, keepdims=True)
    scale = lax.rsqrt(squares / width + EPS)
    logit = jnp.zeros((tokens, 1), F32)
    for start in range(0, width, chunk):
        cols = slice(start, start + chunk)
        final = (stream[:, cols] * scale * gain_ref[cols][None, :]).astype(BF16).astype(F32)
        logit = logit + jnp.sum(final * target_ref[:, cols].astype(F32), axis=-1, keepdims=True)
    turn = iota((tokens, tokens), 0) == iota((tokens, tokens), 1)
    logit = jnp.sum(jnp.where(turn, logit, 0.0), axis=0, keepdims=True)
    gap = rest_ref[...] - logit
    token_logp = -(jnp.maximum(gap, 0.0) + jnp.log1p(jnp.exp(-jnp.abs(gap))))
    sequences = out_ref.shape[1]
    inside = iota((sequences, tokens), 0) == seg_ref[...]
    sums = jnp.sum(jnp.where(inside, token_logp, 0.0), axis=1, keepdims=True)
    turn = iota((sequences, sequences), 0) == iota((sequences, sequences), 1)
    sums = jnp.sum(jnp.where(turn, sums, 0.0), axis=0, keepdims=True)
    out_ref[...] = jnp.broadcast_to(sums, out_ref.shape)


def score(own, tokens, gain, picks, gates, target, rest, seg, blocks, capacity, outs):
    rows, width = tokens.shape
    slots = sum(block.shape[0] for block in blocks)
    smem = pl.BlockSpec(memory_space=pltpu.SMEM)
    vmem = pl.BlockSpec(memory_space=pltpu.VMEM)
    return pl.pallas_call(
        functools.partial(score_kernel, capacity),
        out_shape=jax.ShapeDtypeStruct(outs, F32),
        in_specs=[smem] + [vmem] * (7 + len(blocks)),
        out_specs=vmem,
        scratch_shapes=[
            pltpu.VMEM((slots, width), BF16),
            pltpu.VMEM((rows, width), F32),
        ],
        compiler_params=pltpu.CompilerParams(vmem_limit_bytes=VMEM_LIMIT),
        cost_estimate=COST,
        name="score",
    )(own, tokens, gain, picks, gates, target, rest, seg, *blocks)


class Order:
    def __init__(self, token):
        self.token = token

    def mark(self, *values):
        *values, self.token = lax.optimization_barrier((*values, self.token))
        return values

    def mark_one(self, value):
        return self.mark(value)[0]

    def late(self, value):
        return lax.optimization_barrier((value, self.token))[0]


def cut_kernel(whole_ref, *refs):
    first = 0
    for ref in refs:
        ref[...] = whole_ref[first : first + ref.shape[0], :]
        first += ref.shape[0]


def cut(whole, pieces):
    vmem = pl.BlockSpec(memory_space=pltpu.VMEM)
    return pl.pallas_call(
        cut_kernel,
        out_shape=[jax.ShapeDtypeStruct((count, whole.shape[1]), BF16) for _, count in pieces],
        in_specs=[vmem],
        out_specs=[vmem] * len(pieces),
        compiler_params=pltpu.CompilerParams(vmem_limit_bytes=VMEM_LIMIT),
        cost_estimate=COST,
        name="cut",
    )(whole)


def total_kernel(count, *refs):
    *refs, out_ref = refs
    for side in (refs[:count], refs[count:]):
        first = 0
        for ref in side:
            rows = slice(first, first + ref.shape[0])
            if side[0] is refs[0]:
                out_ref[rows, :] = ref[...]
            else:
                out_ref[rows, :] = (out_ref[rows, :].astype(F32) + ref[...].astype(F32)).astype(BF16)
            first += ref.shape[0]


def total(ours, others):
    rows = sum(piece.shape[0] for piece in ours)
    vmem = pl.BlockSpec(memory_space=pltpu.VMEM)
    return pl.pallas_call(
        functools.partial(total_kernel, len(ours)),
        out_shape=jax.ShapeDtypeStruct((rows, ours[0].shape[1]), BF16),
        in_specs=[vmem] * (len(ours) + len(others)),
        out_specs=vmem,
        compiler_params=pltpu.CompilerParams(vmem_limit_bytes=VMEM_LIMIT),
        cost_estimate=COST,
        name="total",
    )(*ours, *others)


def per_device(
    tokens,
    norm_gain,
    final_gain,
    gate_weight,
    up_weight,
    down_weight,
    picks,
    gates,
    target_rows,
    rest_lse,
    segment_ids,
    ref_logps,
):
    tok_rows = tokens.shape[0]
    spread = FFE // HID_DEV
    devices = lax.axis_size("expert")
    experts = devices // spread
    capacity = (tok_rows * TOPK * 5 // (experts * 4) + 3) // 4 * 4
    capacity = (capacity + 15) // 16 * 16
    own = (lax.axis_index("expert") // spread).astype(jnp.int32).reshape(1)
    picks_t = picks.T
    core, side = 1, 2
    cut_at = capacity * 5 // 8 // 16 * 16
    pieces = [(0, cut_at), (cut_at, capacity - cut_at)] if cut_at else [(0, capacity)]
    weights = (gate_weight, up_weight, down_weight)
    *near, staged = pack(own, tokens, norm_gain, picks_t, weights, experts, capacity)
    weights = [staged, swap(staged, core)]
    order = Order(own)
    far, mine, theirs, back = {}, {}, {}, {}

    def leave(k):
        near[k] = swap(order.late(near[k]), k * spread)

    def arrive(k):
        near[k] = order.mark_one(near[k])

    def share(k):
        far[k] = [swap(order.late(piece), side) for piece in order.mark(*cut(near[k], pieces))]

    def work(k):
        mine[k], theirs[k] = [], []
        for (first, _), piece in zip(pieces, far[k]):
            there = order.mark_one(piece)
            part, other = order.mark(*expert_block(order.late(near[k]), first, there, weights))
            mine[k].append(part)
            theirs[k].append(swap(other, side))

    def work_whole(k):
        rows = (order.late(near[k]), 0, order.late(far[k]))
        mine[k], theirs[k] = order.mark(*expert_block(*rows, weights))

    def home(k):
        theirs[k] = order.mark(*theirs[k])
        back[k] = order.mark_one(total(mine[k], theirs[k]))

    def leave_back(k):
        back[k] = swap(order.late(back[k]), k * spread)

    def arrive_back(k):
        back[k] = order.mark_one(back[k])

    leave(2)
    far[0], far[1] = swap(near[0], side), swap(near[1], side)
    leave(1)
    arrive(2)
    far[0] = order.mark_one(far[0])
    far[1] = order.mark_one(far[1])
    arrive(1)
    last = (capacity - 16, 16)
    for k in range(3, experts + 1):
        if k > 3:
            near[k - 1], *theirs[k - 2] = lax.optimization_barrier((near[k - 1], *theirs[k - 2]))
        share(k - 1)
        if k < experts:
            leave(k)
        if k == 3:
            far[1] = swap(order.late(far[1]), spread)
        if k > 3:
            if k == experts:
                far[1], *theirs[k - 2] = lax.optimization_barrier((far[1], *theirs[k - 2]))
            home(k - 2)
            leave_back(k - 2)
        if k == experts:
            work_whole(1)
            theirs[1] = swap(theirs[1], spread)
        work(k - 1)
        if k == experts:
            work_whole(0)
        if k < experts:
            arrive(k)
        if k > 3:
            arrive_back(k - 2)
    home(experts - 1)
    leave_back(experts - 1)
    mine[0], theirs[0] = [mine[0]], [swap(order.late(theirs[0]), side)]
    mine[1] = [swap(order.late(mine[1]), spread)]
    theirs[1] = order.mark(*cut(order.mark_one(theirs[1]), [(0, last[0]), last]))
    theirs[1] = [swap(order.late(piece), side) for piece in theirs[1]]
    order = Order(own)
    arrive_back(experts - 1)
    theirs[0] = order.mark(*theirs[0])
    mine[1] = order.mark(*mine[1])
    own = order.token
    back[0], back[1] = total(mine[0], theirs[0]), total(mine[1], theirs[1])
    blocks = [back[k] for k in range(experts)]
    local = score(
        own,
        tokens,
        final_gain,
        picks_t,
        gates.T,
        target_rows,
        rest_lse[None, :],
        segment_ids[None, :],
        blocks,
        capacity,
        (devices, ref_logps.shape[0]),
    )
    gathered = lax.all_to_all(local, "expert", split_axis=0, concat_axis=0, tiled=True)
    sequence_logps = jnp.sum(gathered, axis=0)
    margin = sequence_logps[0::2] - ref_logps[0::2] - (sequence_logps[1::2] - ref_logps[1::2])
    pair_loss = -jax.nn.log_sigmoid(BETA * margin)
    return (sequence_logps, pair_loss)


def solution(mesh):
    placed = (
        P(("group", "expert"), None),
        P(),
        P(),
        P(None, "expert"),
        P(None, "expert"),
        P("expert", None),
        P(("group", "expert"), None),
        P(("group", "expert"), None),
        P(("group", "expert"), None),
        P(("group", "expert")),
        P(("group", "expert")),
        P("group"),
    )
    return jax.shard_map(
        per_device, mesh=mesh, in_specs=placed, out_specs=(P("group"), P("group")), check_vma=False
    )
```

```python
import functools

import jax
import jax.numpy as jnp
from jax import lax
from jax.experimental import pallas as pl
from jax.experimental.pallas import tpu as pltpu
from jax.sharding import PartitionSpec as P

FFE = 2048
HID_DEV = 512
TOPK = 2

EPS = 1e-06
BETA = 0.01

F32 = jnp.float32
BF16 = jnp.bfloat16
VMEM_LIMIT = 10 * 1024 * 1024
COST = pl.CostEstimate(flops=1024, bytes_accessed=1024, transcendentals=0)


def swap(value, mask):
    pairs = [(source, source ^ mask) for source in range(lax.axis_size("expert"))]
    return lax.ppermute(value, "expert", pairs)


def iota(shape, dim):
    return lax.broadcasted_iota(jnp.int32, shape, dim)


def routing(own, picks, rows):
    tokens = picks.shape[1]
    expert = jnp.bitwise_xor(own, iota((rows, tokens), 0))
    hit = [picks[k : k + 1, :] == expert for k in range(TOPK)]
    member = hit[0] | hit[1]
    earlier = (iota((tokens, tokens), 0) < iota((tokens, tokens), 1)).astype(BF16)
    slot = jnp.dot(member.astype(F32).astype(BF16), earlier, preferred_element_type=F32)
    slot = jnp.where(member, slot.astype(jnp.int32), -1)
    return hit, slot


def pack_kernel(own_ref, tokens_hbm, gain_hbm, picks_hbm, gate_hbm, up_hbm, down_hbm, *refs):
    *out_refs, weights_ref, tokens_ref, gain_ref, picks_ref, arrived = refs
    width, hidden = gate_hbm.shape
    moves = [(tokens_hbm, tokens_ref), (gain_hbm, gain_ref), (picks_hbm, picks_ref)]
    sources = [gate_hbm, up_hbm]
    sources += [down_hbm.at[:, pl.ds(first, hidden)] for first in range(0, width, hidden)]
    first = 0
    for source in sources:
        moves.append((source, weights_ref.at[pl.ds(first, source.shape[0]), :]))
        first += source.shape[0]
    copies = [pltpu.make_async_copy(*move, arrived.at[n]) for n, move in enumerate(moves)]
    for copy in copies:
        copy.start()
    for copy in copies[:3]:
        copy.wait()
    tokens = tokens_ref.shape[0]
    values = tokens_ref[...].astype(F32)
    scale = lax.rsqrt(jnp.mean(values * values, axis=-1, keepdims=True) + EPS)
    normed = (values * scale * gain_ref[...][None, :]).astype(BF16)
    _, slot = routing(own_ref[0], picks_ref[...], max(8, len(out_refs)))
    for k, out_ref in enumerate(out_refs):
        place = iota((out_ref.shape[0], tokens), 0)
        chosen = (slot[k : k + 1, :] == place).astype(F32).astype(BF16)
        out_ref[...] = jnp.dot(chosen, normed, preferred_element_type=F32).astype(BF16)
    for copy in copies[3:]:
        copy.wait()


def pack(own, tokens, gain, picks, weights, experts, capacity):
    width, hidden = weights[0].shape
    smem = pl.BlockSpec(memory_space=pltpu.SMEM)
    vmem = pl.BlockSpec(memory_space=pltpu.VMEM)
    hbm = pl.BlockSpec(memory_space=pltpu.HBM)
    shapes = [(capacity, width)] * experts + [(3 * width, hidden)]
    there = [pltpu.with_memory_space_constraint(array, pltpu.HBM) for array in (tokens, gain, picks, *weights)]
    return pl.pallas_call(
        pack_kernel,
        out_shape=[jax.ShapeDtypeStruct(shape, BF16) for shape in shapes],
        in_specs=[smem] + [hbm] * 6,
        out_specs=[vmem] * len(shapes),
        scratch_shapes=[
            pltpu.VMEM(tokens.shape, BF16),
            pltpu.VMEM(gain.shape, F32),
            pltpu.VMEM(picks.shape, jnp.int32),
            pltpu.SemaphoreType.DMA((5 + width // hidden,)),
        ],
        compiler_params=pltpu.CompilerParams(vmem_limit_bytes=VMEM_LIMIT),
        cost_estimate=COST,
        name="pack",
    )(own, *there)


def expert_kernel(first, near_ref, far_ref, *refs):
    *refs, rows = refs
    weight_refs, out_refs = refs[:2], refs[2:]
    count = far_ref.shape[0]
    rows[:count, :] = near_ref[first : first + count, :]
    rows[count:, :] = far_ref[...]
    width = rows.shape[1]
    size = weight_refs[0].shape[1]
    hidden = []
    for ref in weight_refs:
        gate = jnp.dot(rows[...], ref[:width, :], preferred_element_type=F32)
        up = jnp.dot(rows[...], ref[width : 2 * width, :], preferred_element_type=F32)
        hidden.append((jax.nn.silu(gate) * up).astype(BF16))
    for start in range(0, width, size):
        part = sum(
            jnp.dot(value, ref[pl.ds(2 * width + start, size), :], preferred_element_type=F32)
            for value, ref in zip(hidden, weight_refs)
        ).astype(BF16)
        done = 0
        for ref in out_refs:
            ref[:, start : start + size] = part[done : done + ref.shape[0]]
            done += ref.shape[0]


def expert_block(near, first, far, weights, joined=False):
    count, width = far.shape
    outs = [2 * count] if joined else [count, count]
    vmem = pl.BlockSpec(memory_space=pltpu.VMEM)
    return pl.pallas_call(
        functools.partial(expert_kernel, first),
        out_shape=[jax.ShapeDtypeStruct((rows, width), BF16) for rows in outs],
        in_specs=[vmem] * (2 + len(weights)),
        out_specs=[vmem] * len(outs),
        scratch_shapes=[pltpu.VMEM((2 * count, width), BF16)],
        compiler_params=pltpu.CompilerParams(vmem_limit_bytes=VMEM_LIMIT),
        cost_estimate=COST,
        name="expert_block",
    )(near, far, *weights)


def score_kernel(capacity, own_ref, tokens_ref, gain_ref, picks_ref, gates_ref, target_ref, rest_ref, seg_ref, *refs):
    *block_refs, out_ref, stacked, stream = refs
    tokens, width = tokens_ref.shape
    experts = stacked.shape[0] // capacity
    first = 0
    for ref in block_refs:
        stacked[first : first + ref.shape[0], :] = ref[...]
        first += ref.shape[0]
    hit, slot = routing(own_ref[0], picks_ref[...], max(8, experts))
    weight = sum(jnp.where(hit[k], gates_ref[k : k + 1, :], 0.0) for k in range(TOPK))
    place = iota((capacity, tokens), 0)
    parts = [
        jnp.where(slot[k : k + 1, :] == place, weight[k : k + 1, :], 0.0) for k in range(experts)
    ]
    spread = jnp.concatenate(parts, axis=0)
    coarse = spread.astype(BF16)
    fine = (spread - coarse.astype(F32)).astype(BF16)
    chunk = width // 7 if width % 7 == 0 else width
    over_rows = (((0,), (0,)), ((), ()))
    squares = jnp.zeros((tokens, 1), F32)
    for start in range(0, width, chunk):
        cols = slice(start, start + chunk)
        rows = stacked[:, cols]
        moe = lax.dot_general(coarse, rows, over_rows, preferred_element_type=F32)
        moe = moe + lax.dot_general(fine, rows, over_rows, preferred_element_type=F32)
        value = tokens_ref[:, cols].astype(F32) + moe
        stream[:, cols] = value
        squares = squares + jnp.sum(value * value, axis=-1, keepdims=True)
    scale = lax.rsqrt(squares / width + EPS)
    logit = jnp.zeros((tokens, 1), F32)
    for start in range(0, width, chunk):
        cols = slice(start, start + chunk)
        final = (stream[:, cols] * scale * gain_ref[cols][None, :]).astype(BF16).astype(F32)
        logit = logit + jnp.sum(final * target_ref[:, cols].astype(F32), axis=-1, keepdims=True)
    turn = iota((tokens, tokens), 0) == iota((tokens, tokens), 1)
    logit = jnp.sum(jnp.where(turn, logit, 0.0), axis=0, keepdims=True)
    gap = rest_ref[...] - logit
    token_logp = -(jnp.maximum(gap, 0.0) + jnp.log1p(jnp.exp(-jnp.abs(gap))))
    sequences = out_ref.shape[1]
    inside = iota((sequences, tokens), 0) == seg_ref[...]
    sums = jnp.sum(jnp.where(inside, token_logp, 0.0), axis=1, keepdims=True)
    turn = iota((sequences, sequences), 0) == iota((sequences, sequences), 1)
    sums = jnp.sum(jnp.where(turn, sums, 0.0), axis=0, keepdims=True)
    out_ref[...] = jnp.broadcast_to(sums, out_ref.shape)


def score(own, tokens, gain, picks, gates, target, rest, seg, blocks, capacity, outs):
    rows, width = tokens.shape
    slots = sum(block.shape[0] for block in blocks)
    smem = pl.BlockSpec(memory_space=pltpu.SMEM)
    vmem = pl.BlockSpec(memory_space=pltpu.VMEM)
    return pl.pallas_call(
        functools.partial(score_kernel, capacity),
        out_shape=jax.ShapeDtypeStruct(outs, F32),
        in_specs=[smem] + [vmem] * (7 + len(blocks)),
        out_specs=vmem,
        scratch_shapes=[
            pltpu.VMEM((slots, width), BF16),
            pltpu.VMEM((rows, width), F32),
        ],
        compiler_params=pltpu.CompilerParams(vmem_limit_bytes=VMEM_LIMIT),
        cost_estimate=COST,
        name="score",
    )(own, tokens, gain, picks, gates, target, rest, seg, *blocks)


class Order:
    def __init__(self, token):
        self.token = token

    def mark(self, *values):
        *values, self.token = lax.optimization_barrier((*values, self.token))
        return values

    def mark_one(self, value):
        return self.mark(value)[0]

    def late(self, value):
        return lax.optimization_barrier((value, self.token))[0]


def cut_kernel(pieces, whole_ref, *refs):
    for (first, count), ref in zip(pieces, refs):
        ref[...] = whole_ref[first : first + count, :]


def cut(whole, pieces):
    vmem = pl.BlockSpec(memory_space=pltpu.VMEM)
    return pl.pallas_call(
        functools.partial(cut_kernel, tuple(pieces)),
        out_shape=[jax.ShapeDtypeStruct((count, whole.shape[1]), BF16) for _, count in pieces],
        in_specs=[vmem],
        out_specs=[vmem] * len(pieces),
        compiler_params=pltpu.CompilerParams(vmem_limit_bytes=VMEM_LIMIT),
        cost_estimate=COST,
        name="cut",
    )(whole)


def total_kernel(count, *refs):
    *refs, out_ref = refs
    for n, side in enumerate((refs[:count], refs[count:])):
        first = 0
        for ref in side:
            rows = min(ref.shape[0], out_ref.shape[0] - first)
            there = slice(first, first + rows)
            value = ref[:rows, :]
            if n:
                value = (out_ref[there, :].astype(F32) + value.astype(F32)).astype(BF16)
            out_ref[there, :] = value
            first += rows


def total(ours, others):
    rows = sum(piece.shape[0] for piece in others)
    vmem = pl.BlockSpec(memory_space=pltpu.VMEM)
    return pl.pallas_call(
        functools.partial(total_kernel, len(ours)),
        out_shape=jax.ShapeDtypeStruct((rows, ours[0].shape[1]), BF16),
        in_specs=[vmem] * (len(ours) + len(others)),
        out_specs=vmem,
        compiler_params=pltpu.CompilerParams(vmem_limit_bytes=VMEM_LIMIT),
        cost_estimate=COST,
        name="total",
    )(*ours, *others)


def per_device(
    tokens,
    norm_gain,
    final_gain,
    gate_weight,
    up_weight,
    down_weight,
    picks,
    gates,
    target_rows,
    rest_lse,
    segment_ids,
    ref_logps,
):
    tok_rows = tokens.shape[0]
    spread = FFE // HID_DEV
    devices = lax.axis_size("expert")
    experts = devices // spread
    capacity = (tok_rows * TOPK * 5 // (experts * 4) + 3) // 4 * 4
    capacity = (capacity + 15) // 16 * 16
    own = (lax.axis_index("expert") // spread).astype(jnp.int32).reshape(1)
    picks_t = picks.T
    core, side = 1, 2
    cut_at = capacity * 5 // 8 // 16 * 16
    pieces = [(0, cut_at), (cut_at, capacity - cut_at)] if cut_at else [(0, capacity)]
    weights = (gate_weight, up_weight, down_weight)
    *near, staged = pack(own, tokens, norm_gain, picks_t, weights, experts, capacity)
    weights = [staged, swap(staged, core)]
    order = Order(own)
    far, mine, theirs, back = {}, {}, {}, {}

    def leave(k):
        near[k] = swap(order.late(near[k]), k * spread)

    def arrive(k):
        near[k] = order.mark_one(near[k])

    def share(k):
        far[k] = [swap(order.late(piece), side) for piece in order.mark(*cut(near[k], pieces))]

    def work(k):
        mine[k], theirs[k] = [], []
        for (first, _), piece in zip(pieces, far[k]):
            there = order.mark_one(piece)
            part, other = order.mark(*expert_block(order.late(near[k]), first, there, weights))
            mine[k].append(part)
            theirs[k].append(swap(other, side))

    def work_whole(k):
        rows = (order.late(near[k]), 0, order.late(far[k]))
        mine[k], theirs[k] = order.mark(*expert_block(*rows, weights))

    def home(k):
        theirs[k] = order.mark(*theirs[k])
        back[k] = order.mark_one(total(mine[k], theirs[k]))

    def leave_back(k):
        back[k] = swap(order.late(back[k]), k * spread)

    def arrive_back(k):
        back[k] = order.mark_one(back[k])

    leave(2)
    far[0], far[1] = swap(near[0], side), swap(near[1], side)
    leave(1)
    arrive(2)
    far[0] = order.mark_one(far[0])
    far[1] = order.mark_one(far[1])
    arrive(1)
    for k in range(3, experts + 1):
        if k > 3:
            near[k - 1], *theirs[k - 2] = lax.optimization_barrier((near[k - 1], *theirs[k - 2]))
        share(k - 1)
        if k < experts:
            leave(k)
        if k == 3:
            far[1] = swap(order.late(far[1]), spread)
        if k > 3:
            home(k - 2)
            leave_back(k - 2)
        work(k - 1)
        if k == 3:
            (joined,) = order.mark(*expert_block(order.late(near[1]), 0, order.late(far[1]), weights, joined=True))
            mine[1] = [swap(joined, spread)]
        if k == experts:
            work_whole(0)
        if k < experts:
            arrive(k)
        if k > 3:
            arrive_back(k - 2)
    home(experts - 1)
    leave_back(experts - 1)
    mine[0], theirs[0] = [mine[0]], [swap(order.late(theirs[0]), side)]
    mine[1] = order.mark(*mine[1])
    thirds = [(first, min(32, 2 * capacity - first)) for first in range(capacity, 2 * capacity, 32)]
    theirs[1] = order.mark(*cut(mine[1][0], thirds))
    theirs[1] = [swap(order.late(piece), side) for piece in theirs[1]]
    order = Order(own)
    arrive_back(experts - 1)
    theirs[0] = order.mark(*theirs[0])
    theirs[1] = order.mark(*theirs[1])
    own = order.token
    back[0], back[1] = total(mine[0], theirs[0]), total(mine[1], theirs[1])
    blocks = [back[k] for k in range(experts)]
    local = score(
        own,
        tokens,
        final_gain,
        picks_t,
        gates.T,
        target_rows,
        rest_lse[None, :],
        segment_ids[None, :],
        blocks,
        capacity,
        (devices, ref_logps.shape[0]),
    )
    gathered = lax.all_to_all(local, "expert", split_axis=0, concat_axis=0, tiled=True)
    sequence_logps = jnp.sum(gathered, axis=0)
    margin = sequence_logps[0::2] - ref_logps[0::2] - (sequence_logps[1::2] - ref_logps[1::2])
    pair_loss = -jax.nn.log_sigmoid(BETA * margin)
    return (sequence_logps, pair_loss)


def solution(mesh):
    placed = (
        P(("group", "expert"), None),
        P(),
        P(),
        P(None, "expert"),
        P(None, "expert"),
        P("expert", None),
        P(("group", "expert"), None),
        P(("group", "expert"), None),
        P(("group", "expert"), None),
        P(("group", "expert")),
        P(("group", "expert")),
        P("group"),
    )
    return jax.shard_map(
        per_device, mesh=mesh, in_specs=placed, out_specs=(P("group"), P("group")), check_vma=False
    )
```

```python
import functools

import jax
import jax.numpy as jnp
from jax import lax
from jax.experimental import pallas as pl
from jax.experimental.pallas import tpu as pltpu
from jax.sharding import PartitionSpec as P

FFE = 2048
HID_DEV = 512
TOPK = 2

EPS = 1e-06
BETA = 0.01

F32 = jnp.float32
BF16 = jnp.bfloat16
VMEM_LIMIT = 10 * 1024 * 1024
COST = pl.CostEstimate(flops=1024, bytes_accessed=1024, transcendentals=0)


def swap(value, mask):
    pairs = [(source, source ^ mask) for source in range(lax.axis_size("expert"))]
    return lax.ppermute(value, "expert", pairs)


def iota(shape, dim):
    return lax.broadcasted_iota(jnp.int32, shape, dim)


def routing(own, picks, rows):
    tokens = picks.shape[1]
    expert = jnp.bitwise_xor(own, iota((rows, tokens), 0))
    hit = [picks[k : k + 1, :] == expert for k in range(TOPK)]
    member = hit[0] | hit[1]
    earlier = (iota((tokens, tokens), 0) < iota((tokens, tokens), 1)).astype(BF16)
    slot = jnp.dot(member.astype(F32).astype(BF16), earlier, preferred_element_type=F32)
    slot = jnp.where(member, slot.astype(jnp.int32), -1)
    return hit, slot


def pack_kernel(own_ref, tokens_hbm, gain_hbm, picks_hbm, gate_hbm, up_hbm, down_hbm, *refs):
    *out_refs, weights_ref, tokens_ref, gain_ref, picks_ref, arrived = refs
    width, hidden = gate_hbm.shape
    moves = [(tokens_hbm, tokens_ref), (gain_hbm, gain_ref), (picks_hbm, picks_ref)]
    sources = [gate_hbm, up_hbm]
    sources += [down_hbm.at[:, pl.ds(first, hidden)] for first in range(0, width, hidden)]
    first = 0
    for source in sources:
        moves.append((source, weights_ref.at[pl.ds(first, source.shape[0]), :]))
        first += source.shape[0]
    copies = [pltpu.make_async_copy(*move, arrived.at[n]) for n, move in enumerate(moves)]
    for copy in copies:
        copy.start()
    for copy in copies[:3]:
        copy.wait()
    tokens = tokens_ref.shape[0]
    values = tokens_ref[...].astype(F32)
    scale = lax.rsqrt(jnp.mean(values * values, axis=-1, keepdims=True) + EPS)
    normed = (values * scale * gain_ref[...][None, :]).astype(BF16)
    _, slot = routing(own_ref[0], picks_ref[...], max(8, len(out_refs)))
    for k, out_ref in enumerate(out_refs):
        place = iota((out_ref.shape[0], tokens), 0)
        chosen = (slot[k : k + 1, :] == place).astype(F32).astype(BF16)
        out_ref[...] = jnp.dot(chosen, normed, preferred_element_type=F32).astype(BF16)
    for copy in copies[3:]:
        copy.wait()


def pack(own, tokens, gain, picks, weights, experts, capacity):
    width, hidden = weights[0].shape
    smem = pl.BlockSpec(memory_space=pltpu.SMEM)
    vmem = pl.BlockSpec(memory_space=pltpu.VMEM)
    hbm = pl.BlockSpec(memory_space=pltpu.HBM)
    shapes = [(capacity, width)] * experts + [(3 * width, hidden)]
    there = [pltpu.with_memory_space_constraint(array, pltpu.HBM) for array in (tokens, gain, picks, *weights)]
    return pl.pallas_call(
        pack_kernel,
        out_shape=[jax.ShapeDtypeStruct(shape, BF16) for shape in shapes],
        in_specs=[smem] + [hbm] * 6,
        out_specs=[vmem] * len(shapes),
        scratch_shapes=[
            pltpu.VMEM(tokens.shape, BF16),
            pltpu.VMEM(gain.shape, F32),
            pltpu.VMEM(picks.shape, jnp.int32),
            pltpu.SemaphoreType.DMA((5 + width // hidden,)),
        ],
        compiler_params=pltpu.CompilerParams(vmem_limit_bytes=VMEM_LIMIT),
        cost_estimate=COST,
        name="pack",
    )(own, *there)


def expert_kernel(first, near_ref, far_ref, *refs):
    *weight_refs, mine_ref, theirs_ref, rows = refs
    count = far_ref.shape[0]
    rows[:count, :] = near_ref[first : first + count, :]
    rows[count:, :] = far_ref[...]
    width = rows.shape[1]
    size = weight_refs[0].shape[1]
    hidden = []
    for ref in weight_refs:
        gate = jnp.dot(rows[...], ref[:width, :], preferred_element_type=F32)
        up = jnp.dot(rows[...], ref[width : 2 * width, :], preferred_element_type=F32)
        hidden.append((jax.nn.silu(gate) * up).astype(BF16))
    for start in range(0, width, size):
        part = sum(
            jnp.dot(value, ref[pl.ds(2 * width + start, size), :], preferred_element_type=F32)
            for value, ref in zip(hidden, weight_refs)
        ).astype(BF16)
        mine_ref[:, start : start + size] = part[:count]
        theirs_ref[:, start : start + size] = part[count:]


def expert_block(near, first, far, weights):
    count, width = far.shape
    vmem = pl.BlockSpec(memory_space=pltpu.VMEM)
    return pl.pallas_call(
        functools.partial(expert_kernel, first),
        out_shape=[jax.ShapeDtypeStruct((count, width), BF16)] * 2,
        in_specs=[vmem] * (2 + len(weights)),
        out_specs=[vmem] * 2,
        scratch_shapes=[pltpu.VMEM((2 * count, width), BF16)],
        compiler_params=pltpu.CompilerParams(vmem_limit_bytes=VMEM_LIMIT),
        cost_estimate=COST,
        name="expert_block",
    )(near, far, *weights)


def score_kernel(capacity, own_ref, tokens_ref, gain_ref, picks_ref, gates_ref, target_ref, rest_ref, seg_ref, *refs):
    *block_refs, out_ref, stacked, stream = refs
    tokens, width = tokens_ref.shape
    experts = stacked.shape[0] // capacity
    first = 0
    for ref in block_refs:
        stacked[first : first + ref.shape[0], :] = ref[...]
        first += ref.shape[0]
    hit, slot = routing(own_ref[0], picks_ref[...], max(8, experts))
    weight = sum(jnp.where(hit[k], gates_ref[k : k + 1, :], 0.0) for k in range(TOPK))
    place = iota((capacity, tokens), 0)
    parts = [
        jnp.where(slot[k : k + 1, :] == place, weight[k : k + 1, :], 0.0) for k in range(experts)
    ]
    spread = jnp.concatenate(parts, axis=0)
    coarse = spread.astype(BF16)
    fine = (spread - coarse.astype(F32)).astype(BF16)
    chunk = width // 7 if width % 7 == 0 else width
    over_rows = (((0,), (0,)), ((), ()))
    squares = jnp.zeros((tokens, 1), F32)
    for start in range(0, width, chunk):
        cols = slice(start, start + chunk)
        rows = stacked[:, cols]
        moe = lax.dot_general(coarse, rows, over_rows, preferred_element_type=F32)
        moe = moe + lax.dot_general(fine, rows, over_rows, preferred_element_type=F32)
        value = tokens_ref[:, cols].astype(F32) + moe
        stream[:, cols] = value
        squares = squares + jnp.sum(value * value, axis=-1, keepdims=True)
    scale = lax.rsqrt(squares / width + EPS)
    logit = jnp.zeros((tokens, 1), F32)
    for start in range(0, width, chunk):
        cols = slice(start, start + chunk)
        final = (stream[:, cols] * scale * gain_ref[cols][None, :]).astype(BF16).astype(F32)
        logit = logit + jnp.sum(final * target_ref[:, cols].astype(F32), axis=-1, keepdims=True)
    turn = iota((tokens, tokens), 0) == iota((tokens, tokens), 1)
    logit = jnp.sum(jnp.where(turn, logit, 0.0), axis=0, keepdims=True)
    gap = rest_ref[...] - logit
    token_logp = -(jnp.maximum(gap, 0.0) + jnp.log1p(jnp.exp(-jnp.abs(gap))))
    sequences = out_ref.shape[1]
    inside = iota((sequences, tokens), 0) == seg_ref[...]
    sums = jnp.sum(jnp.where(inside, token_logp, 0.0), axis=1, keepdims=True)
    turn = iota((sequences, sequences), 0) == iota((sequences, sequences), 1)
    sums = jnp.sum(jnp.where(turn, sums, 0.0), axis=0, keepdims=True)
    out_ref[...] = jnp.broadcast_to(sums, out_ref.shape)


def score(own, tokens, gain, picks, gates, target, rest, seg, blocks, capacity, outs):
    rows, width = tokens.shape
    slots = sum(block.shape[0] for block in blocks)
    smem = pl.BlockSpec(memory_space=pltpu.SMEM)
    vmem = pl.BlockSpec(memory_space=pltpu.VMEM)
    return pl.pallas_call(
        functools.partial(score_kernel, capacity),
        out_shape=jax.ShapeDtypeStruct(outs, F32),
        in_specs=[smem] + [vmem] * (7 + len(blocks)),
        out_specs=vmem,
        scratch_shapes=[
            pltpu.VMEM((slots, width), BF16),
            pltpu.VMEM((rows, width), F32),
        ],
        compiler_params=pltpu.CompilerParams(vmem_limit_bytes=VMEM_LIMIT),
        cost_estimate=COST,
        name="score",
    )(own, tokens, gain, picks, gates, target, rest, seg, *blocks)


class Order:
    def __init__(self, token):
        self.token = token

    def mark(self, *values):
        *values, self.token = lax.optimization_barrier((*values, self.token))
        return values

    def mark_one(self, value):
        return self.mark(value)[0]

    def late(self, value):
        return lax.optimization_barrier((value, self.token))[0]


def cut_kernel(whole_ref, *refs):
    first = 0
    for ref in refs:
        ref[...] = whole_ref[first : first + ref.shape[0], :]
        first += ref.shape[0]


def cut(whole, pieces):
    vmem = pl.BlockSpec(memory_space=pltpu.VMEM)
    return pl.pallas_call(
        cut_kernel,
        out_shape=[jax.ShapeDtypeStruct((count, whole.shape[1]), BF16) for _, count in pieces],
        in_specs=[vmem],
        out_specs=[vmem] * len(pieces),
        compiler_params=pltpu.CompilerParams(vmem_limit_bytes=VMEM_LIMIT),
        cost_estimate=COST,
        name="cut",
    )(whole)


def total_kernel(count, *refs):
    *refs, out_ref = refs
    for side in (refs[:count], refs[count:]):
        first = 0
        for ref in side:
            rows = slice(first, first + ref.shape[0])
            if side[0] is refs[0]:
                out_ref[rows, :] = ref[...]
            else:
                out_ref[rows, :] = (out_ref[rows, :].astype(F32) + ref[...].astype(F32)).astype(BF16)
            first += ref.shape[0]


def total(ours, others):
    rows = sum(piece.shape[0] for piece in ours)
    vmem = pl.BlockSpec(memory_space=pltpu.VMEM)
    return pl.pallas_call(
        functools.partial(total_kernel, len(ours)),
        out_shape=jax.ShapeDtypeStruct((rows, ours[0].shape[1]), BF16),
        in_specs=[vmem] * (len(ours) + len(others)),
        out_specs=vmem,
        compiler_params=pltpu.CompilerParams(vmem_limit_bytes=VMEM_LIMIT),
        cost_estimate=COST,
        name="total",
    )(*ours, *others)


def per_device(
    tokens,
    norm_gain,
    final_gain,
    gate_weight,
    up_weight,
    down_weight,
    picks,
    gates,
    target_rows,
    rest_lse,
    segment_ids,
    ref_logps,
):
    tok_rows = tokens.shape[0]
    spread = FFE // HID_DEV
    devices = lax.axis_size("expert")
    experts = devices // spread
    capacity = (tok_rows * TOPK * 5 // (experts * 4) + 3) // 4 * 4
    capacity = (capacity + 15) // 16 * 16
    own = (lax.axis_index("expert") // spread).astype(jnp.int32).reshape(1)
    picks_t = picks.T
    core, side = 1, 2
    cut_at = capacity * 5 // 8 // 16 * 16
    pieces = [(0, cut_at), (cut_at, capacity - cut_at)] if cut_at else [(0, capacity)]
    weights = (gate_weight, up_weight, down_weight)
    *near, staged = pack(own, tokens, norm_gain, picks_t, weights, experts, capacity)
    weights = [staged, swap(staged, core)]
    order = Order(own)
    far, mine, theirs, back = {}, {}, {}, {}

    def leave(k):
        near[k] = swap(order.late(near[k]), k * spread)

    def arrive(k):
        near[k] = order.mark_one(near[k])

    def share(k):
        far[k] = [swap(order.late(piece), side) for piece in order.mark(*cut(near[k], pieces))]

    def work(k):
        mine[k], theirs[k] = [], []
        for (first, _), piece in zip(pieces, far[k]):
            there = order.mark_one(piece)
            part, other = order.mark(*expert_block(order.late(near[k]), first, there, weights))
            mine[k].append(part)
            theirs[k].append(swap(other, side))

    def work_whole(k):
        rows = (order.late(near[k]), 0, order.late(far[k]))
        mine[k], theirs[k] = order.mark(*expert_block(*rows, weights))

    def home(k):
        theirs[k] = order.mark(*theirs[k])
        back[k] = order.mark_one(total(mine[k], theirs[k]))

    def leave_back(k):
        back[k] = swap(order.late(back[k]), k * spread)

    def arrive_back(k):
        back[k] = order.mark_one(back[k])

    leave(2)
    far[0], far[1] = swap(near[0], side), swap(near[1], side)
    leave(1)
    weights[1] = order.mark_one(weights[1])
    arrive(2)
    far[0] = order.mark_one(far[0])
    last = (capacity - 16, 16)
    for k in range(3, experts + 1):
        if k > 3:
            near[k - 1], *theirs[k - 2] = lax.optimization_barrier((near[k - 1], *theirs[k - 2]))
        share(k - 1)
        if k < experts:
            leave(k)
        if k == 3:
            far[1] = order.mark_one(far[1])
            arrive(1)
            far[1] = swap(order.late(far[1]), spread)
        if k > 3:
            if k == experts:
                far[1], *theirs[k - 2] = lax.optimization_barrier((far[1], *theirs[k - 2]))
            home(k - 2)
            leave_back(k - 2)
        if k == experts:
            work_whole(1)
            theirs[1] = swap(theirs[1], spread)
        work(k - 1)
        if k == experts:
            work_whole(0)
        if k < experts:
            arrive(k)
        if k > 3:
            arrive_back(k - 2)
    home(experts - 1)
    leave_back(experts - 1)
    mine[0], theirs[0] = [mine[0]], [swap(order.late(theirs[0]), side)]
    mine[1] = [swap(order.late(mine[1]), spread)]
    theirs[1] = order.mark(*cut(order.mark_one(theirs[1]), [(0, last[0]), last]))
    theirs[1] = [swap(order.late(piece), side) for piece in theirs[1]]
    order = Order(own)
    arrive_back(experts - 1)
    theirs[0] = order.mark(*theirs[0])
    mine[1] = order.mark(*mine[1])
    own = order.token
    back[0], back[1] = total(mine[0], theirs[0]), total(mine[1], theirs[1])
    blocks = [back[k] for k in range(experts)]
    local = score(
        own,
        tokens,
        final_gain,
        picks_t,
        gates.T,
        target_rows,
        rest_lse[None, :],
        segment_ids[None, :],
        blocks,
        capacity,
        (devices, ref_logps.shape[0]),
    )
    gathered = lax.all_to_all(local, "expert", split_axis=0, concat_axis=0, tiled=True)
    sequence_logps = jnp.sum(gathered, axis=0)
    margin = sequence_logps[0::2] - ref_logps[0::2] - (sequence_logps[1::2] - ref_logps[1::2])
    pair_loss = -jax.nn.log_sigmoid(BETA * margin)
    return (sequence_logps, pair_loss)


def solution(mesh):
    placed = (
        P(("group", "expert"), None),
        P(),
        P(),
        P(None, "expert"),
        P(None, "expert"),
        P("expert", None),
        P(("group", "expert"), None),
        P(("group", "expert"), None),
        P(("group", "expert"), None),
        P(("group", "expert")),
        P(("group", "expert")),
        P("group"),
    )
    return jax.shard_map(
        per_device, mesh=mesh, in_specs=placed, out_specs=(P("group"), P("group")), check_vma=False
    )
```

```python
import functools

import jax
import jax.numpy as jnp
from jax import lax
from jax.experimental import pallas as pl
from jax.experimental.pallas import tpu as pltpu
from jax.sharding import PartitionSpec as P

FFE = 2048
HID_DEV = 512
TOPK = 2

EPS = 1e-06
BETA = 0.01

F32 = jnp.float32
BF16 = jnp.bfloat16
VMEM_LIMIT = 10 * 1024 * 1024
COST = pl.CostEstimate(flops=1024, bytes_accessed=1024, transcendentals=0)


def swap(value, mask):
    pairs = [(source, source ^ mask) for source in range(lax.axis_size("expert"))]
    return lax.ppermute(value, "expert", pairs)


def iota(shape, dim):
    return lax.broadcasted_iota(jnp.int32, shape, dim)


def routing(own, picks, rows):
    tokens = picks.shape[1]
    expert = jnp.bitwise_xor(own, iota((rows, tokens), 0))
    hit = [picks[k : k + 1, :] == expert for k in range(TOPK)]
    member = hit[0] | hit[1]
    earlier = (iota((tokens, tokens), 0) < iota((tokens, tokens), 1)).astype(BF16)
    slot = jnp.dot(member.astype(F32).astype(BF16), earlier, preferred_element_type=F32)
    slot = jnp.where(member, slot.astype(jnp.int32), -1)
    return hit, slot


def pack_kernel(own_ref, tokens_hbm, gain_hbm, picks_hbm, gate_hbm, up_hbm, down_hbm, *refs):
    *out_refs, weights_ref, tokens_ref, gain_ref, picks_ref, arrived = refs
    width, hidden = gate_hbm.shape
    moves = [(tokens_hbm, tokens_ref), (gain_hbm, gain_ref), (picks_hbm, picks_ref)]
    sources = [gate_hbm, up_hbm]
    sources += [down_hbm.at[:, pl.ds(first, hidden)] for first in range(0, width, hidden)]
    first = 0
    for source in sources:
        moves.append((source, weights_ref.at[pl.ds(first, source.shape[0]), :]))
        first += source.shape[0]
    copies = [pltpu.make_async_copy(*move, arrived.at[n]) for n, move in enumerate(moves)]
    for copy in copies:
        copy.start()
    for copy in copies[:3]:
        copy.wait()
    tokens = tokens_ref.shape[0]
    values = tokens_ref[...].astype(F32)
    scale = lax.rsqrt(jnp.mean(values * values, axis=-1, keepdims=True) + EPS)
    normed = (values * scale * gain_ref[...][None, :]).astype(BF16)
    _, slot = routing(own_ref[0], picks_ref[...], max(8, len(out_refs)))
    for k, out_ref in enumerate(out_refs):
        place = iota((out_ref.shape[0], tokens), 0)
        chosen = (slot[k : k + 1, :] == place).astype(F32).astype(BF16)
        out_ref[...] = jnp.dot(chosen, normed, preferred_element_type=F32).astype(BF16)
    for copy in copies[3:]:
        copy.wait()


def pack(own, tokens, gain, picks, weights, experts, capacity):
    width, hidden = weights[0].shape
    smem = pl.BlockSpec(memory_space=pltpu.SMEM)
    vmem = pl.BlockSpec(memory_space=pltpu.VMEM)
    hbm = pl.BlockSpec(memory_space=pltpu.HBM)
    shapes = [(capacity, width)] * experts + [(3 * width, hidden)]
    there = [pltpu.with_memory_space_constraint(array, pltpu.HBM) for array in (tokens, gain, picks, *weights)]
    return pl.pallas_call(
        pack_kernel,
        out_shape=[jax.ShapeDtypeStruct(shape, BF16) for shape in shapes],
        in_specs=[smem] + [hbm] * 6,
        out_specs=[vmem] * len(shapes),
        scratch_shapes=[
            pltpu.VMEM(tokens.shape, BF16),
            pltpu.VMEM(gain.shape, F32),
            pltpu.VMEM(picks.shape, jnp.int32),
            pltpu.SemaphoreType.DMA((5 + width // hidden,)),
        ],
        compiler_params=pltpu.CompilerParams(vmem_limit_bytes=VMEM_LIMIT),
        cost_estimate=COST,
        name="pack",
    )(own, *there)


def expert_kernel(first, near_ref, far_ref, *refs):
    *weight_refs, mine_ref, theirs_ref, rows = refs
    count = far_ref.shape[0]
    rows[:count, :] = near_ref[first : first + count, :]
    rows[count:, :] = far_ref[...]
    width = rows.shape[1]
    size = weight_refs[0].shape[1]
    hidden = []
    for ref in weight_refs:
        gate = jnp.dot(rows[...], ref[:width, :], preferred_element_type=F32)
        up = jnp.dot(rows[...], ref[width : 2 * width, :], preferred_element_type=F32)
        hidden.append((jax.nn.silu(gate) * up).astype(BF16))
    for start in range(0, width, size):
        part = sum(
            jnp.dot(value, ref[pl.ds(2 * width + start, size), :], preferred_element_type=F32)
            for value, ref in zip(hidden, weight_refs)
        ).astype(BF16)
        mine_ref[:, start : start + size] = part[:count]
        theirs_ref[:, start : start + size] = part[count:]


def expert_block(near, first, far, weights):
    count, width = far.shape
    vmem = pl.BlockSpec(memory_space=pltpu.VMEM)
    return pl.pallas_call(
        functools.partial(expert_kernel, first),
        out_shape=[jax.ShapeDtypeStruct((count, width), BF16)] * 2,
        in_specs=[vmem] * (2 + len(weights)),
        out_specs=[vmem] * 2,
        scratch_shapes=[pltpu.VMEM((2 * count, width), BF16)],
        compiler_params=pltpu.CompilerParams(vmem_limit_bytes=VMEM_LIMIT),
        cost_estimate=COST,
        name="expert_block",
    )(near, far, *weights)


def score_kernel(capacity, own_ref, tokens_ref, gain_ref, picks_ref, gates_ref, target_ref, rest_ref, seg_ref, *refs):
    *block_refs, out_ref, stacked, stream = refs
    tokens, width = tokens_ref.shape
    experts = stacked.shape[0] // capacity
    first = 0
    for ref in block_refs:
        stacked[first : first + ref.shape[0], :] = ref[...]
        first += ref.shape[0]
    hit, slot = routing(own_ref[0], picks_ref[...], max(8, experts))
    weight = sum(jnp.where(hit[k], gates_ref[k : k + 1, :], 0.0) for k in range(TOPK))
    place = iota((capacity, tokens), 0)
    parts = [
        jnp.where(slot[k : k + 1, :] == place, weight[k : k + 1, :], 0.0) for k in range(experts)
    ]
    spread = jnp.concatenate(parts, axis=0)
    coarse = spread.astype(BF16)
    fine = (spread - coarse.astype(F32)).astype(BF16)
    halves = jnp.concatenate([coarse, fine], axis=1)
    chunk = width // 7 if width % 7 == 0 else width
    over_rows = (((0,), (0,)), ((), ()))
    squares = jnp.zeros((tokens, 1), F32)
    for start in range(0, width, chunk):
        cols = slice(start, start + chunk)
        rows = stacked[:, cols]
        moe = lax.dot_general(halves, rows, over_rows, preferred_element_type=F32)
        value = tokens_ref[:, cols].astype(F32) + (moe[:tokens] + moe[tokens:])
        stream[:, cols] = value
        squares = squares + jnp.sum(value * value, axis=-1, keepdims=True)
    scale = lax.rsqrt(squares / width + EPS)
    logit = jnp.zeros((tokens, 1), F32)
    for start in range(0, width, chunk):
        cols = slice(start, start + chunk)
        final = (stream[:, cols] * scale * gain_ref[cols][None, :]).astype(BF16).astype(F32)
        logit = logit + jnp.sum(final * target_ref[:, cols].astype(F32), axis=-1, keepdims=True)
    turn = iota((tokens, tokens), 0) == iota((tokens, tokens), 1)
    logit = jnp.sum(jnp.where(turn, logit, 0.0), axis=0, keepdims=True)
    gap = rest_ref[...] - logit
    token_logp = -(jnp.maximum(gap, 0.0) + jnp.log1p(jnp.exp(-jnp.abs(gap))))
    sequences = out_ref.shape[1]
    inside = iota((sequences, tokens), 0) == seg_ref[...]
    sums = jnp.sum(jnp.where(inside, token_logp, 0.0), axis=1, keepdims=True)
    turn = iota((sequences, sequences), 0) == iota((sequences, sequences), 1)
    sums = jnp.sum(jnp.where(turn, sums, 0.0), axis=0, keepdims=True)
    out_ref[...] = jnp.broadcast_to(sums, out_ref.shape)


def score(own, tokens, gain, picks, gates, target, rest, seg, blocks, capacity, outs):
    rows, width = tokens.shape
    slots = sum(block.shape[0] for block in blocks)
    smem = pl.BlockSpec(memory_space=pltpu.SMEM)
    vmem = pl.BlockSpec(memory_space=pltpu.VMEM)
    return pl.pallas_call(
        functools.partial(score_kernel, capacity),
        out_shape=jax.ShapeDtypeStruct(outs, F32),
        in_specs=[smem] + [vmem] * (7 + len(blocks)),
        out_specs=vmem,
        scratch_shapes=[
            pltpu.VMEM((slots, width), BF16),
            pltpu.VMEM((rows, width), F32),
        ],
        compiler_params=pltpu.CompilerParams(vmem_limit_bytes=VMEM_LIMIT),
        cost_estimate=COST,
        name="score",
    )(own, tokens, gain, picks, gates, target, rest, seg, *blocks)


class Order:
    def __init__(self, token):
        self.token = token

    def mark(self, *values):
        *values, self.token = lax.optimization_barrier((*values, self.token))
        return values

    def mark_one(self, value):
        return self.mark(value)[0]

    def late(self, value):
        return lax.optimization_barrier((value, self.token))[0]


def cut_kernel(whole_ref, *refs):
    first = 0
    for ref in refs:
        ref[...] = whole_ref[first : first + ref.shape[0], :]
        first += ref.shape[0]


def cut(whole, pieces):
    vmem = pl.BlockSpec(memory_space=pltpu.VMEM)
    return pl.pallas_call(
        cut_kernel,
        out_shape=[jax.ShapeDtypeStruct((count, whole.shape[1]), BF16) for _, count in pieces],
        in_specs=[vmem],
        out_specs=[vmem] * len(pieces),
        compiler_params=pltpu.CompilerParams(vmem_limit_bytes=VMEM_LIMIT),
        cost_estimate=COST,
        name="cut",
    )(whole)


def total_kernel(count, *refs):
    *refs, out_ref = refs
    for side in (refs[:count], refs[count:]):
        first = 0
        for ref in side:
            rows = slice(first, first + ref.shape[0])
            if side[0] is refs[0]:
                out_ref[rows, :] = ref[...]
            else:
                out_ref[rows, :] = (out_ref[rows, :].astype(F32) + ref[...].astype(F32)).astype(BF16)
            first += ref.shape[0]


def total(ours, others):
    rows = sum(piece.shape[0] for piece in ours)
    vmem = pl.BlockSpec(memory_space=pltpu.VMEM)
    return pl.pallas_call(
        functools.partial(total_kernel, len(ours)),
        out_shape=jax.ShapeDtypeStruct((rows, ours[0].shape[1]), BF16),
        in_specs=[vmem] * (len(ours) + len(others)),
        out_specs=vmem,
        compiler_params=pltpu.CompilerParams(vmem_limit_bytes=VMEM_LIMIT),
        cost_estimate=COST,
        name="total",
    )(*ours, *others)


def per_device(
    tokens,
    norm_gain,
    final_gain,
    gate_weight,
    up_weight,
    down_weight,
    picks,
    gates,
    target_rows,
    rest_lse,
    segment_ids,
    ref_logps,
):
    tok_rows = tokens.shape[0]
    spread = FFE // HID_DEV
    devices = lax.axis_size("expert")
    experts = devices // spread
    capacity = (tok_rows * TOPK * 5 // (experts * 4) + 3) // 4 * 4
    capacity = (capacity + 15) // 16 * 16
    own = (lax.axis_index("expert") // spread).astype(jnp.int32).reshape(1)
    picks_t = picks.T
    core, side = 1, 2
    cut_at = capacity * 5 // 8 // 16 * 16
    pieces = [(0, cut_at), (cut_at, capacity - cut_at)] if cut_at else [(0, capacity)]
    weights = (gate_weight, up_weight, down_weight)
    *near, staged = pack(own, tokens, norm_gain, picks_t, weights, experts, capacity)
    weights = [staged, swap(staged, core)]
    order = Order(own)
    far, mine, theirs, back = {}, {}, {}, {}

    def leave(k):
        near[k] = swap(order.late(near[k]), k * spread)

    def arrive(k):
        near[k] = order.mark_one(near[k])

    def share(k):
        far[k] = [swap(order.late(piece), side) for piece in order.mark(*cut(near[k], pieces))]

    def work(k):
        mine[k], theirs[k] = [], []
        for (first, _), piece in zip(pieces, far[k]):
            there = order.mark_one(piece)
            part, other = order.mark(*expert_block(order.late(near[k]), first, there, weights))
            mine[k].append(part)
            theirs[k].append(swap(other, side))

    def work_whole(k):
        rows = (order.late(near[k]), 0, order.late(far[k]))
        mine[k], theirs[k] = order.mark(*expert_block(*rows, weights))

    def home(k):
        theirs[k] = order.mark(*theirs[k])
        back[k] = order.mark_one(total(mine[k], theirs[k]))

    def leave_back(k):
        back[k] = swap(order.late(back[k]), k * spread)

    def arrive_back(k):
        back[k] = order.mark_one(back[k])

    leave(2)
    far[0], far[1] = swap(near[0], side), swap(near[1], side)
    leave(1)
    weights[1] = order.mark_one(weights[1])
    arrive(2)
    far[0] = order.mark_one(far[0])
    last = (capacity - 16, 16)
    for k in range(3, experts + 1):
        if k > 3:
            held = (far[1], near[k - 1], *theirs[k - 2])
            far[1], near[k - 1], *theirs[k - 2] = lax.optimization_barrier(held)
        share(k - 1)
        if k < experts:
            leave(k)
        if k == 3:
            far[1] = order.mark_one(far[1])
            arrive(1)
            far[1] = swap(order.late(far[1]), spread)
        if k > 3:
            home(k - 2)
            leave_back(k - 2)
        if k == experts:
            work_whole(1)
            theirs[1] = swap(theirs[1], spread)
        work(k - 1)
        if k == experts:
            work_whole(0)
        if k < experts:
            arrive(k)
        if k > 3:
            arrive_back(k - 2)
    home(experts - 1)
    leave_back(experts - 1)
    mine[0], theirs[0] = [mine[0]], [swap(order.late(theirs[0]), side)]
    mine[1] = [swap(order.late(mine[1]), spread)]
    theirs[1] = order.mark(*cut(order.mark_one(theirs[1]), [(0, last[0]), last]))
    theirs[1] = [swap(order.late(piece), side) for piece in theirs[1]]
    order = Order(own)
    arrive_back(experts - 1)
    theirs[0] = order.mark(*theirs[0])
    mine[1] = order.mark(*mine[1])
    own = order.token
    back[0], back[1] = total(mine[0], theirs[0]), total(mine[1], theirs[1])
    blocks = [back[k] for k in range(experts)]
    local = score(
        own,
        tokens,
        final_gain,
        picks_t,
        gates.T,
        target_rows,
        rest_lse[None, :],
        segment_ids[None, :],
        blocks,
        capacity,
        (devices, ref_logps.shape[0]),
    )
    gathered = lax.all_to_all(local, "expert", split_axis=0, concat_axis=0, tiled=True)
    sequence_logps = jnp.sum(gathered, axis=0)
    margin = sequence_logps[0::2] - ref_logps[0::2] - (sequence_logps[1::2] - ref_logps[1::2])
    pair_loss = -jax.nn.log_sigmoid(BETA * margin)
    return (sequence_logps, pair_loss)


def solution(mesh):
    placed = (
        P(("group", "expert"), None),
        P(),
        P(),
        P(None, "expert"),
        P(None, "expert"),
        P("expert", None),
        P(("group", "expert"), None),
        P(("group", "expert"), None),
        P(("group", "expert"), None),
        P(("group", "expert")),
        P(("group", "expert")),
        P("group"),
    )
    return jax.shard_map(
        per_device, mesh=mesh, in_specs=placed, out_specs=(P("group"), P("group")), check_vma=False
    )
```

```python
import functools

import jax
import jax.numpy as jnp
from jax import lax
from jax.experimental import pallas as pl
from jax.experimental.pallas import tpu as pltpu
from jax.sharding import PartitionSpec as P

FFE = 2048
HID_DEV = 512
TOPK = 2

EPS = 1e-06
BETA = 0.01

F32 = jnp.float32
BF16 = jnp.bfloat16
VMEM_LIMIT = 10 * 1024 * 1024
COST = pl.CostEstimate(flops=1024, bytes_accessed=1024, transcendentals=0)


def swap(value, mask):
    pairs = [(source, source ^ mask) for source in range(lax.axis_size("expert"))]
    return lax.ppermute(value, "expert", pairs)


def iota(shape, dim):
    return lax.broadcasted_iota(jnp.int32, shape, dim)


def routing(own, picks, rows):
    tokens = picks.shape[1]
    expert = jnp.bitwise_xor(own, iota((rows, tokens), 0))
    hit = [picks[k : k + 1, :] == expert for k in range(TOPK)]
    member = hit[0] | hit[1]
    earlier = (iota((tokens, tokens), 0) < iota((tokens, tokens), 1)).astype(BF16)
    slot = jnp.dot(member.astype(F32).astype(BF16), earlier, preferred_element_type=F32)
    slot = jnp.where(member, slot.astype(jnp.int32), -1)
    return hit, slot


def pack_kernel(own_ref, tokens_hbm, gain_hbm, picks_hbm, gate_hbm, up_hbm, down_hbm, *refs):
    *out_refs, weights_ref, tokens_ref, gain_ref, picks_ref, arrived = refs
    width, hidden = gate_hbm.shape
    moves = [(tokens_hbm, tokens_ref), (gain_hbm, gain_ref), (picks_hbm, picks_ref)]
    sources = [gate_hbm, up_hbm]
    sources += [down_hbm.at[:, pl.ds(first, hidden)] for first in range(0, width, hidden)]
    first = 0
    for source in sources:
        moves.append((source, weights_ref.at[pl.ds(first, source.shape[0]), :]))
        first += source.shape[0]
    copies = [pltpu.make_async_copy(*move, arrived.at[n]) for n, move in enumerate(moves)]
    for copy in copies:
        copy.start()
    for copy in copies[:3]:
        copy.wait()
    tokens = tokens_ref.shape[0]
    values = tokens_ref[...].astype(F32)
    scale = lax.rsqrt(jnp.mean(values * values, axis=-1, keepdims=True) + EPS)
    normed = (values * scale * gain_ref[...][None, :]).astype(BF16)
    _, slot = routing(own_ref[0], picks_ref[...], max(8, len(out_refs)))
    for k, out_ref in enumerate(out_refs):
        place = iota((out_ref.shape[0], tokens), 0)
        chosen = (slot[k : k + 1, :] == place).astype(F32).astype(BF16)
        out_ref[...] = jnp.dot(chosen, normed, preferred_element_type=F32).astype(BF16)
    for copy in copies[3:]:
        copy.wait()


def pack(own, tokens, gain, picks, weights, experts, capacity):
    width, hidden = weights[0].shape
    smem = pl.BlockSpec(memory_space=pltpu.SMEM)
    vmem = pl.BlockSpec(memory_space=pltpu.VMEM)
    hbm = pl.BlockSpec(memory_space=pltpu.HBM)
    shapes = [(capacity, width)] * experts + [(3 * width, hidden)]
    there = [pltpu.with_memory_space_constraint(array, pltpu.HBM) for array in (tokens, gain, picks, *weights)]
    return pl.pallas_call(
        pack_kernel,
        out_shape=[jax.ShapeDtypeStruct(shape, BF16) for shape in shapes],
        in_specs=[smem] + [hbm] * 6,
        out_specs=[vmem] * len(shapes),
        scratch_shapes=[
            pltpu.VMEM(tokens.shape, BF16),
            pltpu.VMEM(gain.shape, F32),
            pltpu.VMEM(picks.shape, jnp.int32),
            pltpu.SemaphoreType.DMA((5 + width // hidden,)),
        ],
        compiler_params=pltpu.CompilerParams(vmem_limit_bytes=VMEM_LIMIT),
        cost_estimate=COST,
        name="pack",
    )(own, *there)


def expert_kernel(first, near_ref, far_ref, *refs):
    *weight_refs, mine_ref, theirs_ref, rows = refs
    count = far_ref.shape[0]
    rows[:count, :] = near_ref[first : first + count, :]
    rows[count:, :] = far_ref[...]
    width = rows.shape[1]
    size = weight_refs[0].shape[1]
    hidden = []
    for ref in weight_refs:
        gate = jnp.dot(rows[...], ref[:width, :], preferred_element_type=F32)
        up = jnp.dot(rows[...], ref[width : 2 * width, :], preferred_element_type=F32)
        hidden.append((jax.nn.silu(gate) * up).astype(BF16))
    for start in range(0, width, size):
        part = sum(
            jnp.dot(value, ref[pl.ds(2 * width + start, size), :], preferred_element_type=F32)
            for value, ref in zip(hidden, weight_refs)
        ).astype(BF16)
        mine_ref[:, start : start + size] = part[:count]
        theirs_ref[:, start : start + size] = part[count:]


def expert_block(near, first, far, weights):
    count, width = far.shape
    vmem = pl.BlockSpec(memory_space=pltpu.VMEM)
    return pl.pallas_call(
        functools.partial(expert_kernel, first),
        out_shape=[jax.ShapeDtypeStruct((count, width), BF16)] * 2,
        in_specs=[vmem] * (2 + len(weights)),
        out_specs=[vmem] * 2,
        scratch_shapes=[pltpu.VMEM((2 * count, width), BF16)],
        compiler_params=pltpu.CompilerParams(vmem_limit_bytes=VMEM_LIMIT),
        cost_estimate=COST,
        name="expert_block",
    )(near, far, *weights)


def score_kernel(capacity, own_ref, tokens_ref, gain_ref, picks_ref, gates_ref, target_ref, rest_ref, seg_ref, *refs):
    *block_refs, out_ref, stacked, stream = refs
    tokens, width = tokens_ref.shape
    experts = stacked.shape[0] // capacity
    first = 0
    for ref in block_refs:
        stacked[first : first + ref.shape[0], :] = ref[...]
        first += ref.shape[0]
    hit, slot = routing(own_ref[0], picks_ref[...], max(8, experts))
    weight = sum(jnp.where(hit[k], gates_ref[k : k + 1, :], 0.0) for k in range(TOPK))
    place = iota((capacity, tokens), 0)
    parts = [
        jnp.where(slot[k : k + 1, :] == place, weight[k : k + 1, :], 0.0) for k in range(experts)
    ]
    spread = jnp.concatenate(parts, axis=0)
    coarse = spread.astype(BF16)
    fine = (spread - coarse.astype(F32)).astype(BF16)
    chunk = width // 7 if width % 7 == 0 else width
    over_rows = (((0,), (0,)), ((), ()))
    squares = jnp.zeros((tokens, 1), F32)
    for start in range(0, width, chunk):
        cols = slice(start, start + chunk)
        rows = stacked[:, cols]
        moe = lax.dot_general(coarse, rows, over_rows, preferred_element_type=F32)
        moe = moe + lax.dot_general(fine, rows, over_rows, preferred_element_type=F32)
        value = tokens_ref[:, cols].astype(F32) + moe
        stream[:, cols] = value
        squares = squares + jnp.sum(value * value, axis=-1, keepdims=True)
    scale = lax.rsqrt(squares / width + EPS)
    logit = jnp.zeros((tokens, 1), F32)
    for start in range(0, width, chunk):
        cols = slice(start, start + chunk)
        final = (stream[:, cols] * scale * gain_ref[cols][None, :]).astype(BF16).astype(F32)
        logit = logit + jnp.sum(final * target_ref[:, cols].astype(F32), axis=-1, keepdims=True)
    turn = iota((tokens, tokens), 0) == iota((tokens, tokens), 1)
    logit = jnp.sum(jnp.where(turn, logit, 0.0), axis=0, keepdims=True)
    gap = rest_ref[...] - logit
    token_logp = -(jnp.maximum(gap, 0.0) + jnp.log1p(jnp.exp(-jnp.abs(gap))))
    sequences = out_ref.shape[1]
    inside = iota((sequences, tokens), 0) == seg_ref[...]
    sums = jnp.sum(jnp.where(inside, token_logp, 0.0), axis=1, keepdims=True)
    turn = iota((sequences, sequences), 0) == iota((sequences, sequences), 1)
    sums = jnp.sum(jnp.where(turn, sums, 0.0), axis=0, keepdims=True)
    out_ref[...] = jnp.broadcast_to(sums, out_ref.shape)


def score(own, tokens, gain, picks, gates, target, rest, seg, blocks, capacity, outs):
    rows, width = tokens.shape
    slots = sum(block.shape[0] for block in blocks)
    smem = pl.BlockSpec(memory_space=pltpu.SMEM)
    vmem = pl.BlockSpec(memory_space=pltpu.VMEM)
    return pl.pallas_call(
        functools.partial(score_kernel, capacity),
        out_shape=jax.ShapeDtypeStruct(outs, F32),
        in_specs=[smem] + [vmem] * (7 + len(blocks)),
        out_specs=vmem,
        scratch_shapes=[
            pltpu.VMEM((slots, width), BF16),
            pltpu.VMEM((rows, width), F32),
        ],
        compiler_params=pltpu.CompilerParams(vmem_limit_bytes=VMEM_LIMIT),
        cost_estimate=COST,
        name="score",
    )(own, tokens, gain, picks, gates, target, rest, seg, *blocks)


class Order:
    def __init__(self, token):
        self.token = token

    def mark(self, *values):
        *values, self.token = lax.optimization_barrier((*values, self.token))
        return values

    def mark_one(self, value):
        return self.mark(value)[0]

    def late(self, value):
        return lax.optimization_barrier((value, self.token))[0]


def cut_kernel(whole_ref, *refs):
    first = 0
    for ref in refs:
        ref[...] = whole_ref[first : first + ref.shape[0], :]
        first += ref.shape[0]


def cut(whole, pieces):
    vmem = pl.BlockSpec(memory_space=pltpu.VMEM)
    return pl.pallas_call(
        cut_kernel,
        out_shape=[jax.ShapeDtypeStruct((count, whole.shape[1]), BF16) for _, count in pieces],
        in_specs=[vmem],
        out_specs=[vmem] * len(pieces),
        compiler_params=pltpu.CompilerParams(vmem_limit_bytes=VMEM_LIMIT),
        cost_estimate=COST,
        name="cut",
    )(whole)


def total_kernel(count, *refs):
    *refs, out_ref = refs
    for side in (refs[:count], refs[count:]):
        first = 0
        for ref in side:
            rows = slice(first, first + ref.shape[0])
            if side[0] is refs[0]:
                out_ref[rows, :] = ref[...]
            else:
                out_ref[rows, :] = (out_ref[rows, :].astype(F32) + ref[...].astype(F32)).astype(BF16)
            first += ref.shape[0]


def total(ours, others):
    rows = sum(piece.shape[0] for piece in ours)
    vmem = pl.BlockSpec(memory_space=pltpu.VMEM)
    return pl.pallas_call(
        functools.partial(total_kernel, len(ours)),
        out_shape=jax.ShapeDtypeStruct((rows, ours[0].shape[1]), BF16),
        in_specs=[vmem] * (len(ours) + len(others)),
        out_specs=vmem,
        compiler_params=pltpu.CompilerParams(vmem_limit_bytes=VMEM_LIMIT),
        cost_estimate=COST,
        name="total",
    )(*ours, *others)


def per_device(
    tokens,
    norm_gain,
    final_gain,
    gate_weight,
    up_weight,
    down_weight,
    picks,
    gates,
    target_rows,
    rest_lse,
    segment_ids,
    ref_logps,
):
    tok_rows = tokens.shape[0]
    spread = FFE // HID_DEV
    devices = lax.axis_size("expert")
    experts = devices // spread
    capacity = (tok_rows * TOPK * 5 // (experts * 4) + 3) // 4 * 4
    capacity = (capacity + 15) // 16 * 16
    own = (lax.axis_index("expert") // spread).astype(jnp.int32).reshape(1)
    picks_t = picks.T
    core, side = 1, 2
    cut_at = capacity * 5 // 8 // 16 * 16
    pieces = [(0, cut_at), (cut_at, capacity - cut_at)] if cut_at else [(0, capacity)]
    weights = (gate_weight, up_weight, down_weight)
    *near, staged = pack(own, tokens, norm_gain, picks_t, weights, experts, capacity)
    weights = [staged, swap(staged, core)]
    order = Order(own)
    far, mine, theirs, back = {}, {}, {}, {}

    def leave(k):
        near[k] = swap(order.late(near[k]), k * spread)

    def arrive(k):
        near[k] = order.mark_one(near[k])

    def share(k):
        far[k] = [swap(order.late(piece), side) for piece in order.mark(*cut(near[k], pieces))]

    def work(k):
        mine[k], theirs[k] = [], []
        for (first, _), piece in zip(pieces, far[k]):
            there = order.mark_one(piece)
            part, other = order.mark(*expert_block(order.late(near[k]), first, there, weights))
            mine[k].append(part)
            theirs[k].append(swap(other, side))

    def work_whole(k):
        rows = (order.late(near[k]), 0, order.late(far[k]))
        mine[k], theirs[k] = order.mark(*expert_block(*rows, weights))

    def home(k):
        theirs[k] = order.mark(*theirs[k])
        back[k] = order.mark_one(total(mine[k], theirs[k]))

    def leave_back(k):
        back[k] = swap(order.late(back[k]), k * spread)

    def arrive_back(k):
        back[k] = order.mark_one(back[k])

    leave(2)
    far[0], far[1] = swap(near[0], side), swap(near[1], side)
    leave(1)
    weights[1] = order.mark_one(weights[1])
    arrive(2)
    far[0] = order.mark_one(far[0])
    last = (capacity - 16, 16)
    for k in range(3, experts + 1):
        if k > 3:
            near[k - 1], *theirs[k - 2] = lax.optimization_barrier((near[k - 1], *theirs[k - 2]))
        share(k - 1)
        if k < experts:
            leave(k)
        if k == 3:
            far[1] = order.mark_one(far[1])
            arrive(1)
            far[1] = swap(order.late(far[1]), spread)
        if k > 3:
            if k == experts:
                far[1], *theirs[k - 2] = lax.optimization_barrier((far[1], *theirs[k - 2]))
            home(k - 2)
            leave_back(k - 2)
        if k == experts:
            work_whole(1)
            theirs[1] = swap(theirs[1], spread)
        work(k - 1)
        if k == experts:
            work_whole(0)
        if k < experts:
            arrive(k)
        if k > 3:
            arrive_back(k - 2)
    home(experts - 1)
    leave_back(experts - 1)
    mine[0], theirs[0] = [mine[0]], [swap(order.late(theirs[0]), side)]
    mine[1] = [swap(order.late(mine[1]), spread)]
    theirs[1] = order.mark(*cut(order.mark_one(theirs[1]), [(0, last[0]), last]))
    theirs[1] = [swap(order.late(piece), side) for piece in theirs[1]]
    order = Order(own)
    arrive_back(experts - 1)
    theirs[0] = order.mark(*theirs[0])
    mine[1] = order.mark(*mine[1])
    own = order.token
    back[0], back[1] = total(mine[0], theirs[0]), total(mine[1], theirs[1])
    blocks = [back[k] for k in range(experts)]
    local = score(
        own,
        tokens,
        final_gain,
        picks_t,
        gates.T,
        target_rows,
        rest_lse[None, :],
        segment_ids[None, :],
        blocks,
        capacity,
        (devices // 2, ref_logps.shape[0]),
    )
    local = local + swap(local, core)
    cores = [list(range(first, devices, 2)) for first in range(2)]
    gathered = lax.all_to_all(
        local, "expert", split_axis=0, concat_axis=0, axis_index_groups=cores, tiled=True
    )
    sequence_logps = jnp.sum(gathered, axis=0)
    margin = sequence_logps[0::2] - ref_logps[0::2] - (sequence_logps[1::2] - ref_logps[1::2])
    pair_loss = -jax.nn.log_sigmoid(BETA * margin)
    return (sequence_logps, pair_loss)


def solution(mesh):
    placed = (
        P(("group", "expert"), None),
        P(),
        P(),
        P(None, "expert"),
        P(None, "expert"),
        P("expert", None),
        P(("group", "expert"), None),
        P(("group", "expert"), None),
        P(("group", "expert"), None),
        P(("group", "expert")),
        P(("group", "expert")),
        P("group"),
    )
    return jax.shard_map(
        per_device, mesh=mesh, in_specs=placed, out_specs=(P("group"), P("group")), check_vma=False
    )
```

```python
import functools

import jax
import jax.numpy as jnp
from jax import lax
from jax.experimental import pallas as pl
from jax.experimental.pallas import tpu as pltpu
from jax.sharding import PartitionSpec as P

FFE = 2048
HID_DEV = 512
TOPK = 2

EPS = 1e-06
BETA = 0.01

F32 = jnp.float32
BF16 = jnp.bfloat16
VMEM_LIMIT = 10 * 1024 * 1024
COST = pl.CostEstimate(flops=1024, bytes_accessed=1024, transcendentals=0)


def swap(value, mask):
    pairs = [(source, source ^ mask) for source in range(lax.axis_size("expert"))]
    return lax.ppermute(value, "expert", pairs)


def iota(shape, dim):
    return lax.broadcasted_iota(jnp.int32, shape, dim)


def routing(own, picks, rows):
    tokens = picks.shape[1]
    expert = jnp.bitwise_xor(own, iota((rows, tokens), 0))
    hit = [picks[k : k + 1, :] == expert for k in range(TOPK)]
    member = hit[0] | hit[1]
    earlier = (iota((tokens, tokens), 0) < iota((tokens, tokens), 1)).astype(BF16)
    slot = jnp.dot(member.astype(F32).astype(BF16), earlier, preferred_element_type=F32)
    slot = jnp.where(member, slot.astype(jnp.int32), -1)
    return hit, slot


def pack_kernel(own_ref, tokens_hbm, gain_hbm, picks_hbm, gate_hbm, up_hbm, down_hbm, *refs):
    *out_refs, weights_ref, tokens_ref, gain_ref, picks_ref, arrived = refs
    width, hidden = gate_hbm.shape
    moves = [(tokens_hbm, tokens_ref), (gain_hbm, gain_ref), (picks_hbm, picks_ref)]
    sources = [gate_hbm, up_hbm]
    sources += [down_hbm.at[:, pl.ds(first, hidden)] for first in range(0, width, hidden)]
    first = 0
    for source in sources:
        moves.append((source, weights_ref.at[pl.ds(first, source.shape[0]), :]))
        first += source.shape[0]
    copies = [pltpu.make_async_copy(*move, arrived.at[n]) for n, move in enumerate(moves)]
    for copy in copies:
        copy.start()
    for copy in copies[:3]:
        copy.wait()
    tokens = tokens_ref.shape[0]
    values = tokens_ref[...].astype(F32)
    scale = lax.rsqrt(jnp.mean(values * values, axis=-1, keepdims=True) + EPS)
    normed = (values * scale * gain_ref[...][None, :]).astype(BF16)
    _, slot = routing(own_ref[0], picks_ref[...], max(8, len(out_refs)))
    for k, out_ref in enumerate(out_refs):
        place = iota((out_ref.shape[0], tokens), 0)
        chosen = (slot[k : k + 1, :] == place).astype(F32).astype(BF16)
        out_ref[...] = jnp.dot(chosen, normed, preferred_element_type=F32).astype(BF16)
    for copy in copies[3:]:
        copy.wait()


def pack(own, tokens, gain, picks, weights, experts, capacity):
    width, hidden = weights[0].shape
    smem = pl.BlockSpec(memory_space=pltpu.SMEM)
    vmem = pl.BlockSpec(memory_space=pltpu.VMEM)
    hbm = pl.BlockSpec(memory_space=pltpu.HBM)
    shapes = [(capacity, width)] * experts + [(3 * width, hidden)]
    there = [pltpu.with_memory_space_constraint(array, pltpu.HBM) for array in (tokens, gain, picks, *weights)]
    return pl.pallas_call(
        pack_kernel,
        out_shape=[jax.ShapeDtypeStruct(shape, BF16) for shape in shapes],
        in_specs=[smem] + [hbm] * 6,
        out_specs=[vmem] * len(shapes),
        scratch_shapes=[
            pltpu.VMEM(tokens.shape, BF16),
            pltpu.VMEM(gain.shape, F32),
            pltpu.VMEM(picks.shape, jnp.int32),
            pltpu.SemaphoreType.DMA((5 + width // hidden,)),
        ],
        compiler_params=pltpu.CompilerParams(vmem_limit_bytes=VMEM_LIMIT),
        cost_estimate=COST,
        name="pack",
    )(own, *there)


def expert_kernel(first, near_ref, far_ref, *refs):
    *weight_refs, mine_ref, theirs_ref, rows = refs
    count = far_ref.shape[0]
    rows[:count, :] = near_ref[first : first + count, :]
    rows[count:, :] = far_ref[...]
    width = rows.shape[1]
    size = weight_refs[0].shape[1]
    hidden = []
    for ref in weight_refs:
        gate = jnp.dot(rows[...], ref[:width, :], preferred_element_type=F32)
        up = jnp.dot(rows[...], ref[width : 2 * width, :], preferred_element_type=F32)
        hidden.append((jax.nn.silu(gate) * up).astype(BF16))
    for start in range(0, width, size):
        part = sum(
            jnp.dot(value, ref[pl.ds(2 * width + start, size), :], preferred_element_type=F32)
            for value, ref in zip(hidden, weight_refs)
        ).astype(BF16)
        mine_ref[:, start : start + size] = part[:count]
        theirs_ref[:, start : start + size] = part[count:]


def expert_block(near, first, far, weights):
    count, width = far.shape
    vmem = pl.BlockSpec(memory_space=pltpu.VMEM)
    return pl.pallas_call(
        functools.partial(expert_kernel, first),
        out_shape=[jax.ShapeDtypeStruct((count, width), BF16)] * 2,
        in_specs=[vmem] * (2 + len(weights)),
        out_specs=[vmem] * 2,
        scratch_shapes=[pltpu.VMEM((2 * count, width), BF16)],
        compiler_params=pltpu.CompilerParams(vmem_limit_bytes=VMEM_LIMIT),
        cost_estimate=COST,
        name="expert_block",
    )(near, far, *weights)


def score_kernel(capacity, own_ref, tokens_ref, gain_ref, picks_ref, gates_ref, target_ref, rest_ref, seg_ref, *refs):
    *block_refs, out_ref, stacked, stream = refs
    tokens, width = tokens_ref.shape
    experts = stacked.shape[0] // capacity
    first = 0
    for ref in block_refs:
        stacked[first : first + ref.shape[0], :] = ref[...]
        first += ref.shape[0]
    hit, slot = routing(own_ref[0], picks_ref[...], max(8, experts))
    weight = sum(jnp.where(hit[k], gates_ref[k : k + 1, :], 0.0) for k in range(TOPK))
    place = iota((capacity, tokens), 0)
    parts = [
        jnp.where(slot[k : k + 1, :] == place, weight[k : k + 1, :], 0.0) for k in range(experts)
    ]
    spread = jnp.concatenate(parts, axis=0)
    coarse = spread.astype(BF16)
    fine = (spread - coarse.astype(F32)).astype(BF16)
    chunk = width // 7 if width % 7 == 0 else width
    over_rows = (((0,), (0,)), ((), ()))
    squares = jnp.zeros((tokens, 1), F32)
    for start in range(0, width, chunk):
        cols = slice(start, start + chunk)
        rows = stacked[:, cols]
        moe = lax.dot_general(coarse, rows, over_rows, preferred_element_type=F32)
        moe = moe + lax.dot_general(fine, rows, over_rows, preferred_element_type=F32)
        value = tokens_ref[:, cols].astype(F32) + moe
        stream[:, cols] = value
        squares = squares + jnp.sum(value * value, axis=-1, keepdims=True)
    scale = lax.rsqrt(squares / width + EPS)
    logit = jnp.zeros((tokens, 1), F32)
    for start in range(0, width, chunk):
        cols = slice(start, start + chunk)
        final = (stream[:, cols] * scale * gain_ref[cols][None, :]).astype(BF16).astype(F32)
        logit = logit + jnp.sum(final * target_ref[:, cols].astype(F32), axis=-1, keepdims=True)
    turn = iota((tokens, tokens), 0) == iota((tokens, tokens), 1)
    logit = jnp.sum(jnp.where(turn, logit, 0.0), axis=0, keepdims=True)
    gap = rest_ref[...] - logit
    token_logp = -(jnp.maximum(gap, 0.0) + jnp.log1p(jnp.exp(-jnp.abs(gap))))
    sequences = out_ref.shape[1]
    inside = iota((sequences, tokens), 0) == seg_ref[...]
    sums = jnp.sum(jnp.where(inside, token_logp, 0.0), axis=1, keepdims=True)
    turn = iota((sequences, sequences), 0) == iota((sequences, sequences), 1)
    sums = jnp.sum(jnp.where(turn, sums, 0.0), axis=0, keepdims=True)
    out_ref[...] = jnp.broadcast_to(sums, out_ref.shape)


def score(own, tokens, gain, picks, gates, target, rest, seg, blocks, capacity, outs):
    rows, width = tokens.shape
    slots = sum(block.shape[0] for block in blocks)
    smem = pl.BlockSpec(memory_space=pltpu.SMEM)
    vmem = pl.BlockSpec(memory_space=pltpu.VMEM)
    return pl.pallas_call(
        functools.partial(score_kernel, capacity),
        out_shape=jax.ShapeDtypeStruct(outs, F32),
        in_specs=[smem] + [vmem] * (7 + len(blocks)),
        out_specs=vmem,
        scratch_shapes=[
            pltpu.VMEM((slots, width), BF16),
            pltpu.VMEM((rows, width), F32),
        ],
        compiler_params=pltpu.CompilerParams(vmem_limit_bytes=VMEM_LIMIT),
        cost_estimate=COST,
        name="score",
    )(own, tokens, gain, picks, gates, target, rest, seg, *blocks)


class Order:
    def __init__(self, token):
        self.token = token

    def mark(self, *values):
        *values, self.token = lax.optimization_barrier((*values, self.token))
        return values

    def mark_one(self, value):
        return self.mark(value)[0]

    def late(self, value):
        return lax.optimization_barrier((value, self.token))[0]


def cut_kernel(whole_ref, *refs):
    first = 0
    for ref in refs:
        ref[...] = whole_ref[first : first + ref.shape[0], :]
        first += ref.shape[0]


def cut(whole, pieces):
    vmem = pl.BlockSpec(memory_space=pltpu.VMEM)
    return pl.pallas_call(
        cut_kernel,
        out_shape=[jax.ShapeDtypeStruct((count, whole.shape[1]), BF16) for _, count in pieces],
        in_specs=[vmem],
        out_specs=[vmem] * len(pieces),
        compiler_params=pltpu.CompilerParams(vmem_limit_bytes=VMEM_LIMIT),
        cost_estimate=COST,
        name="cut",
    )(whole)


def join_kernel(*refs):
    *refs, out_ref = refs
    first = 0
    for ref in refs:
        out_ref[first : first + ref.shape[0], :] = ref[...]
        first += ref.shape[0]


def join(arrays):
    vmem = pl.BlockSpec(memory_space=pltpu.VMEM)
    rows = sum(array.shape[0] for array in arrays)
    return pl.pallas_call(
        join_kernel,
        out_shape=jax.ShapeDtypeStruct((rows, arrays[0].shape[1]), BF16),
        in_specs=[vmem] * len(arrays),
        out_specs=vmem,
        compiler_params=pltpu.CompilerParams(vmem_limit_bytes=VMEM_LIMIT),
        cost_estimate=COST,
        name="join",
    )(*arrays)


def total_kernel(count, *refs):
    *refs, out_ref = refs
    for side in (refs[:count], refs[count:]):
        first = 0
        for ref in side:
            rows = slice(first, first + ref.shape[0])
            if side[0] is refs[0]:
                out_ref[rows, :] = ref[...]
            else:
                out_ref[rows, :] = (out_ref[rows, :].astype(F32) + ref[...].astype(F32)).astype(BF16)
            first += ref.shape[0]


def total(ours, others):
    rows = sum(piece.shape[0] for piece in ours)
    vmem = pl.BlockSpec(memory_space=pltpu.VMEM)
    return pl.pallas_call(
        functools.partial(total_kernel, len(ours)),
        out_shape=jax.ShapeDtypeStruct((rows, ours[0].shape[1]), BF16),
        in_specs=[vmem] * (len(ours) + len(others)),
        out_specs=vmem,
        compiler_params=pltpu.CompilerParams(vmem_limit_bytes=VMEM_LIMIT),
        cost_estimate=COST,
        name="total",
    )(*ours, *others)


def per_device(
    tokens,
    norm_gain,
    final_gain,
    gate_weight,
    up_weight,
    down_weight,
    picks,
    gates,
    target_rows,
    rest_lse,
    segment_ids,
    ref_logps,
):
    tok_rows = tokens.shape[0]
    spread = FFE // HID_DEV
    devices = lax.axis_size("expert")
    experts = devices // spread
    capacity = (tok_rows * TOPK * 5 // (experts * 4) + 3) // 4 * 4
    capacity = (capacity + 15) // 16 * 16
    own = (lax.axis_index("expert") // spread).astype(jnp.int32).reshape(1)
    picks_t = picks.T
    core, side = 1, 2
    cut_at = capacity * 5 // 8 // 16 * 16
    pieces = [(0, cut_at), (cut_at, capacity - cut_at)] if cut_at else [(0, capacity)]
    weights = (gate_weight, up_weight, down_weight)
    *near, staged = pack(own, tokens, norm_gain, picks_t, weights, experts, capacity)
    weights = [staged, swap(staged, core)]
    order = Order(own)
    far, mine, theirs, back = {}, {}, {}, {}

    def leave(k):
        near[k] = swap(order.late(near[k]), k * spread)

    def arrive(k):
        near[k] = order.mark_one(near[k])

    def share(k):
        far[k] = [swap(order.late(piece), side) for piece in order.mark(*cut(near[k], pieces))]

    def work(k):
        mine[k], theirs[k] = [], []
        for (first, _), piece in zip(pieces, far[k]):
            there = order.mark_one(piece)
            part, other = order.mark(*expert_block(order.late(near[k]), first, there, weights))
            if k == 2 and first:
                far[0], far[1], other = lax.optimization_barrier((far[0], far[1], other))
            mine[k].append(part)
            theirs[k].append(swap(other, side))

    def work_whole(k):
        rows = (order.late(near[k]), 0, order.late(far[k]))
        mine[k], theirs[k] = order.mark(*expert_block(*rows, weights))

    def home(k):
        theirs[k] = order.mark(*theirs[k])
        back[k] = order.mark_one(total(mine[k], theirs[k]))

    def leave_back(k):
        back[k] = swap(order.late(back[k]), k * spread)

    def arrive_back(k):
        back[k] = order.mark_one(back[k])

    leave(2)
    far[1] = [swap(piece, side) for piece in cut(near[1], pieces)]
    leave(1)
    *far[1], weights[1] = order.mark(*far[1], weights[1])
    far[1] = swap(join(far[1]), spread)
    near[0], weights[1] = lax.optimization_barrier((near[0], weights[1]))
    far[0] = swap(near[0], side)
    arrive(2)
    last = (capacity - 16, 16)
    for k in range(3, experts + 1):
        if k > 3:
            near[k - 1], *theirs[k - 2] = lax.optimization_barrier((near[k - 1], *theirs[k - 2]))
        share(k - 1)
        if k < experts:
            leave(k)
        if k == 3:
            arrive(1)
        if k > 3:
            home(k - 2)
            leave_back(k - 2)
        if k == experts:
            work_whole(1)
            theirs[1] = swap(theirs[1], spread)
        work(k - 1)
        if k == experts:
            work_whole(0)
        if k < experts:
            arrive(k)
        if k > 3:
            arrive_back(k - 2)
    home(experts - 1)
    leave_back(experts - 1)
    mine[0], theirs[0] = [mine[0]], [swap(order.late(theirs[0]), side)]
    mine[1] = [swap(order.late(mine[1]), spread)]
    theirs[1] = order.mark(*cut(order.mark_one(theirs[1]), [(0, last[0]), last]))
    theirs[1] = [swap(order.late(piece), side) for piece in theirs[1]]
    order = Order(own)
    arrive_back(experts - 1)
    theirs[0] = order.mark(*theirs[0])
    mine[1] = order.mark(*mine[1])
    own = order.token
    back[0], back[1] = total(mine[0], theirs[0]), total(mine[1], theirs[1])
    blocks = [back[k] for k in range(experts)]
    local = score(
        own,
        tokens,
        final_gain,
        picks_t,
        gates.T,
        target_rows,
        rest_lse[None, :],
        segment_ids[None, :],
        blocks,
        capacity,
        (devices, ref_logps.shape[0]),
    )
    gathered = lax.all_to_all(local, "expert", split_axis=0, concat_axis=0, tiled=True)
    sequence_logps = jnp.sum(gathered, axis=0)
    margin = sequence_logps[0::2] - ref_logps[0::2] - (sequence_logps[1::2] - ref_logps[1::2])
    pair_loss = -jax.nn.log_sigmoid(BETA * margin)
    return (sequence_logps, pair_loss)


def solution(mesh):
    placed = (
        P(("group", "expert"), None),
        P(),
        P(),
        P(None, "expert"),
        P(None, "expert"),
        P("expert", None),
        P(("group", "expert"), None),
        P(("group", "expert"), None),
        P(("group", "expert"), None),
        P(("group", "expert")),
        P(("group", "expert")),
        P("group"),
    )
    return jax.shard_map(
        per_device, mesh=mesh, in_specs=placed, out_specs=(P("group"), P("group")), check_vma=False
    )
```

```python
import functools

import jax
import jax.numpy as jnp
from jax import lax
from jax.experimental import pallas as pl
from jax.experimental.pallas import tpu as pltpu
from jax.sharding import PartitionSpec as P

FFE = 2048
HID_DEV = 512
TOPK = 2

EPS = 1e-06
BETA = 0.01

F32 = jnp.float32
BF16 = jnp.bfloat16
VMEM_LIMIT = 10 * 1024 * 1024
COST = pl.CostEstimate(flops=1024, bytes_accessed=1024, transcendentals=0)


def swap(value, mask):
    pairs = [(source, source ^ mask) for source in range(lax.axis_size("expert"))]
    return lax.ppermute(value, "expert", pairs)


def iota(shape, dim):
    return lax.broadcasted_iota(jnp.int32, shape, dim)


def routing(own, picks, rows):
    tokens = picks.shape[1]
    expert = jnp.bitwise_xor(own, iota((rows, tokens), 0))
    hit = [picks[k : k + 1, :] == expert for k in range(TOPK)]
    member = hit[0] | hit[1]
    earlier = (iota((tokens, tokens), 0) < iota((tokens, tokens), 1)).astype(BF16)
    slot = jnp.dot(member.astype(F32).astype(BF16), earlier, preferred_element_type=F32)
    slot = jnp.where(member, slot.astype(jnp.int32), -1)
    return hit, slot


def pack_kernel(own_ref, tokens_hbm, gain_hbm, picks_hbm, gate_hbm, up_hbm, down_hbm, *refs):
    *out_refs, weights_ref, tokens_ref, gain_ref, picks_ref, arrived = refs
    width, hidden = gate_hbm.shape
    moves = [(tokens_hbm, tokens_ref), (gain_hbm, gain_ref), (picks_hbm, picks_ref)]
    sources = [gate_hbm, up_hbm]
    sources += [down_hbm.at[:, pl.ds(first, hidden)] for first in range(0, width, hidden)]
    first = 0
    for source in sources:
        moves.append((source, weights_ref.at[pl.ds(first, source.shape[0]), :]))
        first += source.shape[0]
    copies = [pltpu.make_async_copy(*move, arrived.at[n]) for n, move in enumerate(moves)]
    for copy in copies:
        copy.start()
    for copy in copies[:3]:
        copy.wait()
    tokens = tokens_ref.shape[0]
    values = tokens_ref[...].astype(F32)
    scale = lax.rsqrt(jnp.mean(values * values, axis=-1, keepdims=True) + EPS)
    normed = (values * scale * gain_ref[...][None, :]).astype(BF16)
    _, slot = routing(own_ref[0], picks_ref[...], max(8, len(out_refs)))
    for k, out_ref in enumerate(out_refs):
        place = iota((out_ref.shape[0], tokens), 0)
        chosen = (slot[k : k + 1, :] == place).astype(F32).astype(BF16)
        out_ref[...] = jnp.dot(chosen, normed, preferred_element_type=F32).astype(BF16)
    for copy in copies[3:]:
        copy.wait()


def pack(own, tokens, gain, picks, weights, experts, capacity):
    width, hidden = weights[0].shape
    smem = pl.BlockSpec(memory_space=pltpu.SMEM)
    vmem = pl.BlockSpec(memory_space=pltpu.VMEM)
    hbm = pl.BlockSpec(memory_space=pltpu.HBM)
    shapes = [(capacity, width)] * experts + [(3 * width, hidden)]
    there = [pltpu.with_memory_space_constraint(array, pltpu.HBM) for array in (tokens, gain, picks, *weights)]
    return pl.pallas_call(
        pack_kernel,
        out_shape=[jax.ShapeDtypeStruct(shape, BF16) for shape in shapes],
        in_specs=[smem] + [hbm] * 6,
        out_specs=[vmem] * len(shapes),
        scratch_shapes=[
            pltpu.VMEM(tokens.shape, BF16),
            pltpu.VMEM(gain.shape, F32),
            pltpu.VMEM(picks.shape, jnp.int32),
            pltpu.SemaphoreType.DMA((5 + width // hidden,)),
        ],
        compiler_params=pltpu.CompilerParams(vmem_limit_bytes=VMEM_LIMIT),
        cost_estimate=COST,
        name="pack",
    )(own, *there)


def expert_kernel(first, near_ref, far_ref, *refs):
    *weight_refs, mine_ref, theirs_ref, rows = refs
    count = mine_ref.shape[0]
    split = 2 * count - far_ref.shape[0]
    rows[:split, :] = near_ref[first : first + split, :]
    rows[split:, :] = far_ref[...]
    width = rows.shape[1]
    size = weight_refs[0].shape[1]
    hidden = []
    for ref in weight_refs:
        gate = jnp.dot(rows[...], ref[:width, :], preferred_element_type=F32)
        up = jnp.dot(rows[...], ref[width : 2 * width, :], preferred_element_type=F32)
        hidden.append((jax.nn.silu(gate) * up).astype(BF16))
    for start in range(0, width, size):
        part = sum(
            jnp.dot(value, ref[pl.ds(2 * width + start, size), :], preferred_element_type=F32)
            for value, ref in zip(hidden, weight_refs)
        ).astype(BF16)
        mine_ref[:, start : start + size] = part[:count]
        theirs_ref[:, start : start + size] = part[count:]


def expert_block(near, first, far, weights, count):
    width = far.shape[1]
    vmem = pl.BlockSpec(memory_space=pltpu.VMEM)
    return pl.pallas_call(
        functools.partial(expert_kernel, first),
        out_shape=[jax.ShapeDtypeStruct((count, width), BF16)] * 2,
        in_specs=[vmem] * (2 + len(weights)),
        out_specs=[vmem] * 2,
        scratch_shapes=[pltpu.VMEM((2 * count, width), BF16)],
        compiler_params=pltpu.CompilerParams(vmem_limit_bytes=VMEM_LIMIT),
        cost_estimate=COST,
        name="expert_block",
    )(near, far, *weights)


def score_kernel(capacity, own_ref, tokens_ref, gain_ref, picks_ref, gates_ref, target_ref, rest_ref, seg_ref, *refs):
    *block_refs, out_ref, stacked, stream = refs
    tokens, width = tokens_ref.shape
    experts = stacked.shape[0] // capacity
    first = 0
    for ref in block_refs:
        stacked[first : first + ref.shape[0], :] = ref[...]
        first += ref.shape[0]
    hit, slot = routing(own_ref[0], picks_ref[...], max(8, experts))
    weight = sum(jnp.where(hit[k], gates_ref[k : k + 1, :], 0.0) for k in range(TOPK))
    place = iota((capacity, tokens), 0)
    parts = [
        jnp.where(slot[k : k + 1, :] == place, weight[k : k + 1, :], 0.0) for k in range(experts)
    ]
    spread = jnp.concatenate(parts, axis=0)
    coarse = spread.astype(BF16)
    fine = (spread - coarse.astype(F32)).astype(BF16)
    chunk = width // 7 if width % 7 == 0 else width
    over_rows = (((0,), (0,)), ((), ()))
    squares = jnp.zeros((tokens, 1), F32)
    for start in range(0, width, chunk):
        cols = slice(start, start + chunk)
        rows = stacked[:, cols]
        moe = lax.dot_general(coarse, rows, over_rows, preferred_element_type=F32)
        moe = moe + lax.dot_general(fine, rows, over_rows, preferred_element_type=F32)
        value = tokens_ref[:, cols].astype(F32) + moe
        stream[:, cols] = value
        squares = squares + jnp.sum(value * value, axis=-1, keepdims=True)
    scale = lax.rsqrt(squares / width + EPS)
    logit = jnp.zeros((tokens, 1), F32)
    for start in range(0, width, chunk):
        cols = slice(start, start + chunk)
        final = (stream[:, cols] * scale * gain_ref[cols][None, :]).astype(BF16).astype(F32)
        logit = logit + jnp.sum(final * target_ref[:, cols].astype(F32), axis=-1, keepdims=True)
    turn = iota((tokens, tokens), 0) == iota((tokens, tokens), 1)
    logit = jnp.sum(jnp.where(turn, logit, 0.0), axis=0, keepdims=True)
    gap = rest_ref[...] - logit
    token_logp = -(jnp.maximum(gap, 0.0) + jnp.log1p(jnp.exp(-jnp.abs(gap))))
    sequences = out_ref.shape[1]
    inside = iota((sequences, tokens), 0) == seg_ref[...]
    sums = jnp.sum(jnp.where(inside, token_logp, 0.0), axis=1, keepdims=True)
    turn = iota((sequences, sequences), 0) == iota((sequences, sequences), 1)
    sums = jnp.sum(jnp.where(turn, sums, 0.0), axis=0, keepdims=True)
    out_ref[...] = jnp.broadcast_to(sums, out_ref.shape)


def score(own, tokens, gain, picks, gates, target, rest, seg, blocks, capacity, outs):
    rows, width = tokens.shape
    slots = sum(block.shape[0] for block in blocks)
    smem = pl.BlockSpec(memory_space=pltpu.SMEM)
    vmem = pl.BlockSpec(memory_space=pltpu.VMEM)
    return pl.pallas_call(
        functools.partial(score_kernel, capacity),
        out_shape=jax.ShapeDtypeStruct(outs, F32),
        in_specs=[smem] + [vmem] * (7 + len(blocks)),
        out_specs=vmem,
        scratch_shapes=[
            pltpu.VMEM((slots, width), BF16),
            pltpu.VMEM((rows, width), F32),
        ],
        compiler_params=pltpu.CompilerParams(vmem_limit_bytes=VMEM_LIMIT),
        cost_estimate=COST,
        name="score",
    )(own, tokens, gain, picks, gates, target, rest, seg, *blocks)


class Order:
    def __init__(self, token):
        self.token = token

    def mark(self, *values):
        *values, self.token = lax.optimization_barrier((*values, self.token))
        return values

    def mark_one(self, value):
        return self.mark(value)[0]

    def late(self, value):
        return lax.optimization_barrier((value, self.token))[0]


def cut_kernel(pieces, whole_ref, *refs):
    for (first, count), ref in zip(pieces, refs):
        ref[...] = whole_ref[first : first + count, :]


def cut(whole, pieces):
    vmem = pl.BlockSpec(memory_space=pltpu.VMEM)
    return pl.pallas_call(
        functools.partial(cut_kernel, tuple(pieces)),
        out_shape=[jax.ShapeDtypeStruct((count, whole.shape[1]), BF16) for _, count in pieces],
        in_specs=[vmem],
        out_specs=[vmem] * len(pieces),
        compiler_params=pltpu.CompilerParams(vmem_limit_bytes=VMEM_LIMIT),
        cost_estimate=COST,
        name="cut",
    )(whole)


def join_kernel(*refs):
    *refs, out_ref = refs
    first = 0
    for ref in refs:
        out_ref[first : first + ref.shape[0], :] = ref[...]
        first += ref.shape[0]


def join(arrays):
    vmem = pl.BlockSpec(memory_space=pltpu.VMEM)
    rows = sum(array.shape[0] for array in arrays)
    return pl.pallas_call(
        join_kernel,
        out_shape=jax.ShapeDtypeStruct((rows, arrays[0].shape[1]), BF16),
        in_specs=[vmem] * len(arrays),
        out_specs=vmem,
        compiler_params=pltpu.CompilerParams(vmem_limit_bytes=VMEM_LIMIT),
        cost_estimate=COST,
        name="join",
    )(*arrays)


def total_kernel(count, *refs):
    *refs, out_ref = refs
    for side in (refs[:count], refs[count:]):
        first = 0
        for ref in side:
            rows = slice(first, first + ref.shape[0])
            if side[0] is refs[0]:
                out_ref[rows, :] = ref[...]
            else:
                out_ref[rows, :] = (out_ref[rows, :].astype(F32) + ref[...].astype(F32)).astype(BF16)
            first += ref.shape[0]


def total(ours, others):
    rows = sum(piece.shape[0] for piece in ours)
    vmem = pl.BlockSpec(memory_space=pltpu.VMEM)
    return pl.pallas_call(
        functools.partial(total_kernel, len(ours)),
        out_shape=jax.ShapeDtypeStruct((rows, ours[0].shape[1]), BF16),
        in_specs=[vmem] * (len(ours) + len(others)),
        out_specs=vmem,
        compiler_params=pltpu.CompilerParams(vmem_limit_bytes=VMEM_LIMIT),
        cost_estimate=COST,
        name="total",
    )(*ours, *others)


def per_device(
    tokens,
    norm_gain,
    final_gain,
    gate_weight,
    up_weight,
    down_weight,
    picks,
    gates,
    target_rows,
    rest_lse,
    segment_ids,
    ref_logps,
):
    tok_rows = tokens.shape[0]
    spread = FFE // HID_DEV
    devices = lax.axis_size("expert")
    experts = devices // spread
    capacity = (tok_rows * TOPK * 5 // (experts * 4) + 3) // 4 * 4
    capacity = (capacity + 15) // 16 * 16
    own = (lax.axis_index("expert") // spread).astype(jnp.int32).reshape(1)
    picks_t = picks.T
    core, side = 1, 2
    cut_at = capacity * 5 // 8 // 16 * 16
    pieces = [(0, cut_at), (cut_at, capacity - cut_at)] if cut_at else [(0, capacity)]
    weights = (gate_weight, up_weight, down_weight)
    *near, staged = pack(own, tokens, norm_gain, picks_t, weights, experts, capacity)
    weights = [staged, swap(staged, core)]
    order = Order(own)
    far, mine, theirs, back = {}, {}, {}, {}

    def leave(k):
        near[k] = swap(order.late(near[k]), k * spread)

    def arrive(k):
        near[k] = order.mark_one(near[k])

    def share(k):
        far[k] = [swap(order.late(piece), side) for piece in order.mark(*cut(near[k], pieces))]

    def work(k):
        mine[k], theirs[k] = [], []
        for (first, count), piece in zip(pieces, far[k]):
            there = order.mark_one(piece)
            part, other = order.mark(*expert_block(order.late(near[k]), first, there, weights, count))
            if k == 2 and first:
                far[0], other = lax.optimization_barrier((far[0], other))
            mine[k].append(part)
            theirs[k].append(swap(other, side))

    def work_whole(k):
        rows = (order.late(near[k]), 0, order.late(far[k]))
        mine[k], theirs[k] = order.mark(*expert_block(*rows, weights, capacity))

    def home(k):
        theirs[k] = order.mark(*theirs[k])
        back[k] = order.mark_one(total(mine[k], theirs[k]))

    def leave_back(k):
        back[k] = swap(order.late(back[k]), k * spread)

    def arrive_back(k):
        back[k] = order.mark_one(back[k])

    leave(2)
    tail_rows = 32 if capacity > 32 else capacity // 2
    *far[1], near[1], tail = cut(near[1], (*pieces, (0, capacity - tail_rows), (capacity - tail_rows, tail_rows)))
    far[1] = [swap(piece, side) for piece in far[1]]
    leave(1)
    *far[1], weights[1] = order.mark(*far[1], weights[1])
    far[1] = swap(join([tail, *far[1]]), spread)
    near[0], weights[1] = lax.optimization_barrier((near[0], weights[1]))
    far[0] = swap(near[0], side)
    arrive(2)
    last = (capacity - 16, 16)
    for k in range(3, experts + 1):
        if k > 3:
            held = (far[1], near[k - 1], *theirs[k - 2])
            far[1], near[k - 1], *theirs[k - 2] = lax.optimization_barrier(held)
        share(k - 1)
        if k < experts:
            leave(k)
        if k == 3:
            arrive(1)
        if k > 3:
            home(k - 2)
            leave_back(k - 2)
        if k == experts:
            work_whole(1)
            theirs[1] = swap(theirs[1], spread)
        work(k - 1)
        if k == experts:
            work_whole(0)
        if k < experts:
            arrive(k)
        if k > 3:
            arrive_back(k - 2)
    home(experts - 1)
    leave_back(experts - 1)
    mine[0], theirs[0] = [mine[0]], [swap(order.late(theirs[0]), side)]
    mine[1] = [swap(order.late(mine[1]), spread)]
    theirs[1] = order.mark(*cut(order.mark_one(theirs[1]), [(0, last[0]), last]))
    theirs[1] = [swap(order.late(piece), side) for piece in theirs[1]]
    order = Order(own)
    arrive_back(experts - 1)
    theirs[0] = order.mark(*theirs[0])
    mine[1] = order.mark(*mine[1])
    own = order.token
    back[0], back[1] = total(mine[0], theirs[0]), total(mine[1], theirs[1])
    blocks = [back[k] for k in range(experts)]
    local = score(
        own,
        tokens,
        final_gain,
        picks_t,
        gates.T,
        target_rows,
        rest_lse[None, :],
        segment_ids[None, :],
        blocks,
        capacity,
        (devices, ref_logps.shape[0]),
    )
    gathered = lax.all_to_all(local, "expert", split_axis=0, concat_axis=0, tiled=True)
    sequence_logps = jnp.sum(gathered, axis=0)
    margin = sequence_logps[0::2] - ref_logps[0::2] - (sequence_logps[1::2] - ref_logps[1::2])
    pair_loss = -jax.nn.log_sigmoid(BETA * margin)
    return (sequence_logps, pair_loss)


def solution(mesh):
    placed = (
        P(("group", "expert"), None),
        P(),
        P(),
        P(None, "expert"),
        P(None, "expert"),
        P("expert", None),
        P(("group", "expert"), None),
        P(("group", "expert"), None),
        P(("group", "expert"), None),
        P(("group", "expert")),
        P(("group", "expert")),
        P("group"),
    )
    return jax.shard_map(
        per_device, mesh=mesh, in_specs=placed, out_specs=(P("group"), P("group")), check_vma=False
    )
```

```python
import functools

import jax
import jax.numpy as jnp
from jax import lax
from jax.experimental import pallas as pl
from jax.experimental.pallas import tpu as pltpu
from jax.sharding import PartitionSpec as P

FFE = 2048
HID_DEV = 512
TOPK = 2

EPS = 1e-06
BETA = 0.01

F32 = jnp.float32
BF16 = jnp.bfloat16
VMEM_LIMIT = 10 * 1024 * 1024
COST = pl.CostEstimate(flops=1024, bytes_accessed=1024, transcendentals=0)


def swap(value, mask):
    pairs = [(source, source ^ mask) for source in range(lax.axis_size("expert"))]
    return lax.ppermute(value, "expert", pairs)


def iota(shape, dim):
    return lax.broadcasted_iota(jnp.int32, shape, dim)


def routing(own, picks, rows):
    tokens = picks.shape[1]
    expert = jnp.bitwise_xor(own, iota((rows, tokens), 0))
    hit = [picks[k : k + 1, :] == expert for k in range(TOPK)]
    member = hit[0] | hit[1]
    earlier = (iota((tokens, tokens), 0) < iota((tokens, tokens), 1)).astype(BF16)
    slot = jnp.dot(member.astype(F32).astype(BF16), earlier, preferred_element_type=F32)
    slot = jnp.where(member, slot.astype(jnp.int32), -1)
    return hit, slot


def pack_kernel(own_ref, tokens_hbm, gain_hbm, picks_hbm, gate_hbm, up_hbm, down_hbm, *refs):
    *out_refs, weights_ref, tokens_ref, gain_ref, picks_ref, arrived = refs
    width, hidden = gate_hbm.shape
    moves = [(tokens_hbm, tokens_ref), (gain_hbm, gain_ref), (picks_hbm, picks_ref)]
    sources = [gate_hbm, up_hbm]
    sources += [down_hbm.at[:, pl.ds(first, hidden)] for first in range(0, width, hidden)]
    first = 0
    for source in sources:
        moves.append((source, weights_ref.at[pl.ds(first, source.shape[0]), :]))
        first += source.shape[0]
    copies = [pltpu.make_async_copy(*move, arrived.at[n]) for n, move in enumerate(moves)]
    for copy in copies:
        copy.start()
    for copy in copies[:3]:
        copy.wait()
    tokens = tokens_ref.shape[0]
    values = tokens_ref[...].astype(F32)
    scale = lax.rsqrt(jnp.mean(values * values, axis=-1, keepdims=True) + EPS)
    normed = (values * scale * gain_ref[...][None, :]).astype(BF16)
    _, slot = routing(own_ref[0], picks_ref[...], max(8, len(out_refs)))
    for k, out_ref in enumerate(out_refs):
        place = iota((out_ref.shape[0], tokens), 0)
        chosen = (slot[k : k + 1, :] == place).astype(F32).astype(BF16)
        out_ref[...] = jnp.dot(chosen, normed, preferred_element_type=F32).astype(BF16)
    for copy in copies[3:]:
        copy.wait()


def pack(own, tokens, gain, picks, weights, experts, capacity):
    width, hidden = weights[0].shape
    smem = pl.BlockSpec(memory_space=pltpu.SMEM)
    vmem = pl.BlockSpec(memory_space=pltpu.VMEM)
    hbm = pl.BlockSpec(memory_space=pltpu.HBM)
    shapes = [(capacity, width)] * experts + [(3 * width, hidden)]
    there = [pltpu.with_memory_space_constraint(array, pltpu.HBM) for array in (tokens, gain, picks, *weights)]
    return pl.pallas_call(
        pack_kernel,
        out_shape=[jax.ShapeDtypeStruct(shape, BF16) for shape in shapes],
        in_specs=[smem] + [hbm] * 6,
        out_specs=[vmem] * len(shapes),
        scratch_shapes=[
            pltpu.VMEM(tokens.shape, BF16),
            pltpu.VMEM(gain.shape, F32),
            pltpu.VMEM(picks.shape, jnp.int32),
            pltpu.SemaphoreType.DMA((5 + width // hidden,)),
        ],
        compiler_params=pltpu.CompilerParams(vmem_limit_bytes=VMEM_LIMIT),
        cost_estimate=COST,
        name="pack",
    )(own, *there)


def expert_kernel(first, near_ref, far_ref, *refs):
    *weight_refs, mine_ref, theirs_ref, rows = refs
    count = far_ref.shape[0]
    rows[:count, :] = near_ref[first : first + count, :]
    rows[count:, :] = far_ref[...]
    width = rows.shape[1]
    size = weight_refs[0].shape[1]
    hidden = []
    for ref in weight_refs:
        gate = jnp.dot(rows[...], ref[:width, :], preferred_element_type=F32)
        up = jnp.dot(rows[...], ref[width : 2 * width, :], preferred_element_type=F32)
        hidden.append((jax.nn.silu(gate) * up).astype(BF16))
    for start in range(0, width, size):
        part = sum(
            jnp.dot(value, ref[pl.ds(2 * width + start, size), :], preferred_element_type=F32)
            for value, ref in zip(hidden, weight_refs)
        ).astype(BF16)
        mine_ref[:, start : start + size] = part[:count]
        theirs_ref[:, start : start + size] = part[count:]


def expert_block(near, first, far, weights):
    count, width = far.shape
    vmem = pl.BlockSpec(memory_space=pltpu.VMEM)
    return pl.pallas_call(
        functools.partial(expert_kernel, first),
        out_shape=[jax.ShapeDtypeStruct((count, width), BF16)] * 2,
        in_specs=[vmem] * (2 + len(weights)),
        out_specs=[vmem] * 2,
        scratch_shapes=[pltpu.VMEM((2 * count, width), BF16)],
        compiler_params=pltpu.CompilerParams(vmem_limit_bytes=VMEM_LIMIT),
        cost_estimate=COST,
        name="expert_block",
    )(near, far, *weights)


def score_kernel(capacity, own_ref, tokens_ref, gain_ref, picks_ref, gates_ref, target_ref, rest_ref, seg_ref, *refs):
    *block_refs, out_ref, stacked, stream = refs
    tokens, width = tokens_ref.shape
    experts = stacked.shape[0] // capacity
    first = 0
    for ref in block_refs:
        stacked[first : first + ref.shape[0], :] = ref[...]
        first += ref.shape[0]
    hit, slot = routing(own_ref[0], picks_ref[...], max(8, experts))
    weight = sum(jnp.where(hit[k], gates_ref[k : k + 1, :], 0.0) for k in range(TOPK))
    place = iota((capacity, tokens), 0)
    parts = [
        jnp.where(slot[k : k + 1, :] == place, weight[k : k + 1, :], 0.0) for k in range(experts)
    ]
    spread = jnp.concatenate(parts, axis=0)
    coarse = spread.astype(BF16)
    fine = (spread - coarse.astype(F32)).astype(BF16)
    chunk = width // 7 if width % 7 == 0 else width
    over_rows = (((0,), (0,)), ((), ()))
    squares = jnp.zeros((tokens, 1), F32)
    for start in range(0, width, chunk):
        cols = slice(start, start + chunk)
        rows = stacked[:, cols]
        moe = lax.dot_general(coarse, rows, over_rows, preferred_element_type=F32)
        moe = moe + lax.dot_general(fine, rows, over_rows, preferred_element_type=F32)
        value = tokens_ref[:, cols].astype(F32) + moe
        stream[:, cols] = value
        squares = squares + jnp.sum(value * value, axis=-1, keepdims=True)
    scale = lax.rsqrt(squares / width + EPS)
    logit = jnp.zeros((tokens, 1), F32)
    for start in range(0, width, chunk):
        cols = slice(start, start + chunk)
        final = (stream[:, cols] * scale * gain_ref[cols][None, :]).astype(BF16).astype(F32)
        logit = logit + jnp.sum(final * target_ref[:, cols].astype(F32), axis=-1, keepdims=True)
    turn = iota((tokens, tokens), 0) == iota((tokens, tokens), 1)
    logit = jnp.sum(jnp.where(turn, logit, 0.0), axis=0, keepdims=True)
    gap = rest_ref[...] - logit
    token_logp = -(jnp.maximum(gap, 0.0) + jnp.log1p(jnp.exp(-jnp.abs(gap))))
    sequences = out_ref.shape[1]
    inside = iota((sequences, tokens), 0) == seg_ref[...]
    sums = jnp.sum(jnp.where(inside, token_logp, 0.0), axis=1, keepdims=True)
    turn = iota((sequences, sequences), 0) == iota((sequences, sequences), 1)
    sums = jnp.sum(jnp.where(turn, sums, 0.0), axis=0, keepdims=True)
    out_ref[...] = jnp.broadcast_to(sums, out_ref.shape)


def score(own, tokens, gain, picks, gates, target, rest, seg, blocks, capacity, outs):
    rows, width = tokens.shape
    slots = sum(block.shape[0] for block in blocks)
    smem = pl.BlockSpec(memory_space=pltpu.SMEM)
    vmem = pl.BlockSpec(memory_space=pltpu.VMEM)
    return pl.pallas_call(
        functools.partial(score_kernel, capacity),
        out_shape=jax.ShapeDtypeStruct(outs, F32),
        in_specs=[smem] + [vmem] * (7 + len(blocks)),
        out_specs=vmem,
        scratch_shapes=[
            pltpu.VMEM((slots, width), BF16),
            pltpu.VMEM((rows, width), F32),
        ],
        compiler_params=pltpu.CompilerParams(vmem_limit_bytes=VMEM_LIMIT),
        cost_estimate=COST,
        name="score",
    )(own, tokens, gain, picks, gates, target, rest, seg, *blocks)


class Order:
    def __init__(self, token):
        self.token = token

    def mark(self, *values):
        *values, self.token = lax.optimization_barrier((*values, self.token))
        return values

    def mark_one(self, value):
        return self.mark(value)[0]

    def late(self, value):
        return lax.optimization_barrier((value, self.token))[0]


def cut_kernel(whole_ref, *refs):
    first = 0
    for ref in refs:
        ref[...] = whole_ref[first : first + ref.shape[0], :]
        first += ref.shape[0]


def cut(whole, pieces):
    vmem = pl.BlockSpec(memory_space=pltpu.VMEM)
    return pl.pallas_call(
        cut_kernel,
        out_shape=[jax.ShapeDtypeStruct((count, whole.shape[1]), BF16) for _, count in pieces],
        in_specs=[vmem],
        out_specs=[vmem] * len(pieces),
        compiler_params=pltpu.CompilerParams(vmem_limit_bytes=VMEM_LIMIT),
        cost_estimate=COST,
        name="cut",
    )(whole)


def join_kernel(*refs):
    *refs, out_ref = refs
    first = 0
    for ref in refs:
        out_ref[first : first + ref.shape[0], :] = ref[...]
        first += ref.shape[0]


def join(arrays):
    vmem = pl.BlockSpec(memory_space=pltpu.VMEM)
    rows = sum(array.shape[0] for array in arrays)
    return pl.pallas_call(
        join_kernel,
        out_shape=jax.ShapeDtypeStruct((rows, arrays[0].shape[1]), BF16),
        in_specs=[vmem] * len(arrays),
        out_specs=vmem,
        compiler_params=pltpu.CompilerParams(vmem_limit_bytes=VMEM_LIMIT),
        cost_estimate=COST,
        name="join",
    )(*arrays)


def total_kernel(count, *refs):
    *refs, out_ref = refs
    for side in (refs[:count], refs[count:]):
        first = 0
        for ref in side:
            rows = slice(first, first + ref.shape[0])
            if side[0] is refs[0]:
                out_ref[rows, :] = ref[...]
            else:
                out_ref[rows, :] = (out_ref[rows, :].astype(F32) + ref[...].astype(F32)).astype(BF16)
            first += ref.shape[0]


def total(ours, others):
    rows = sum(piece.shape[0] for piece in ours)
    vmem = pl.BlockSpec(memory_space=pltpu.VMEM)
    return pl.pallas_call(
        functools.partial(total_kernel, len(ours)),
        out_shape=jax.ShapeDtypeStruct((rows, ours[0].shape[1]), BF16),
        in_specs=[vmem] * (len(ours) + len(others)),
        out_specs=vmem,
        compiler_params=pltpu.CompilerParams(vmem_limit_bytes=VMEM_LIMIT),
        cost_estimate=COST,
        name="total",
    )(*ours, *others)


def per_device(
    tokens,
    norm_gain,
    final_gain,
    gate_weight,
    up_weight,
    down_weight,
    picks,
    gates,
    target_rows,
    rest_lse,
    segment_ids,
    ref_logps,
):
    tok_rows = tokens.shape[0]
    spread = FFE // HID_DEV
    devices = lax.axis_size("expert")
    experts = devices // spread
    capacity = (tok_rows * TOPK * 5 // (experts * 4) + 3) // 4 * 4
    capacity = (capacity + 15) // 16 * 16
    own = (lax.axis_index("expert") // spread).astype(jnp.int32).reshape(1)
    picks_t = picks.T
    core, side = 1, 2
    cut_at = capacity * 5 // 8 // 16 * 16
    pieces = [(0, cut_at), (cut_at, capacity - cut_at)] if cut_at else [(0, capacity)]
    weights = (gate_weight, up_weight, down_weight)
    *near, staged = pack(own, tokens, norm_gain, picks_t, weights, experts, capacity)
    weights = [staged, swap(staged, core)]
    order = Order(own)
    far, mine, theirs, back = {}, {}, {}, {}

    def leave(k):
        near[k] = swap(order.late(near[k]), k * spread)

    def arrive(k):
        near[k] = order.mark_one(near[k])

    def share(k):
        far[k] = [swap(order.late(piece), side) for piece in order.mark(*cut(near[k], pieces))]

    def work(k):
        mine[k], theirs[k] = [], []
        for (first, _), piece in zip(pieces, far[k]):
            there = order.mark_one(piece)
            part, other = order.mark(*expert_block(order.late(near[k]), first, there, weights))
            if k == 2 and first:
                far[1], other = lax.optimization_barrier((far[1], other))
                far[0], other = lax.optimization_barrier((far[0], other))
            mine[k].append(part)
            theirs[k].append(swap(other, side))

    def work_whole(k):
        rows = (order.late(near[k]), 0, order.late(far[k]))
        mine[k], theirs[k] = order.mark(*expert_block(*rows, weights))

    def home(k):
        theirs[k] = order.mark(*theirs[k])
        back[k] = order.mark_one(total(mine[k], theirs[k]))

    def leave_back(k):
        back[k] = swap(order.late(back[k]), k * spread)

    def arrive_back(k):
        back[k] = order.mark_one(back[k])

    leave(2)
    far[1] = [swap(piece, side) for piece in cut(near[1], pieces)]
    leave(1)
    *far[1], weights[1] = order.mark(*far[1], weights[1])
    far[1] = join(far[1])
    near[0], far[1] = lax.optimization_barrier((near[0], far[1]))
    far[1] = swap(far[1], spread)
    far[0] = swap(near[0], side)
    arrive(2)
    last = (capacity - 16, 16)
    for k in range(3, experts + 1):
        if k > 3:
            near[k - 1], *theirs[k - 2] = lax.optimization_barrier((near[k - 1], *theirs[k - 2]))
        share(k - 1)
        if k < experts:
            leave(k)
        if k == 3:
            arrive(1)
        if k > 3:
            home(k - 2)
            leave_back(k - 2)
        if k == experts:
            work_whole(1)
            theirs[1] = swap(theirs[1], spread)
        work(k - 1)
        if k == experts:
            work_whole(0)
        if k < experts:
            arrive(k)
        if k > 3:
            arrive_back(k - 2)
    home(experts - 1)
    leave_back(experts - 1)
    mine[0], theirs[0] = [mine[0]], [swap(order.late(theirs[0]), side)]
    mine[1] = [swap(order.late(mine[1]), spread)]
    theirs[1] = order.mark(*cut(order.mark_one(theirs[1]), [(0, last[0]), last]))
    theirs[1] = [swap(order.late(piece), side) for piece in theirs[1]]
    order = Order(own)
    arrive_back(experts - 1)
    theirs[0] = order.mark(*theirs[0])
    mine[1] = order.mark(*mine[1])
    own = order.token
    back[0], back[1] = total(mine[0], theirs[0]), total(mine[1], theirs[1])
    blocks = [back[k] for k in range(experts)]
    local = score(
        own,
        tokens,
        final_gain,
        picks_t,
        gates.T,
        target_rows,
        rest_lse[None, :],
        segment_ids[None, :],
        blocks,
        capacity,
        (devices, ref_logps.shape[0]),
    )
    gathered = lax.all_to_all(local, "expert", split_axis=0, concat_axis=0, tiled=True)
    sequence_logps = jnp.sum(gathered, axis=0)
    margin = sequence_logps[0::2] - ref_logps[0::2] - (sequence_logps[1::2] - ref_logps[1::2])
    pair_loss = -jax.nn.log_sigmoid(BETA * margin)
    return (sequence_logps, pair_loss)


def solution(mesh):
    placed = (
        P(("group", "expert"), None),
        P(),
        P(),
        P(None, "expert"),
        P(None, "expert"),
        P("expert", None),
        P(("group", "expert"), None),
        P(("group", "expert"), None),
        P(("group", "expert"), None),
        P(("group", "expert")),
        P(("group", "expert")),
        P("group"),
    )
    return jax.shard_map(
        per_device, mesh=mesh, in_specs=placed, out_specs=(P("group"), P("group")), check_vma=False
    )
```

```python
import functools

import jax
import jax.numpy as jnp
from jax import lax
from jax.experimental import pallas as pl
from jax.experimental.pallas import tpu as pltpu
from jax.sharding import PartitionSpec as P

FFE = 2048
HID_DEV = 512
TOPK = 2

EPS = 1e-06
BETA = 0.01

F32 = jnp.float32
BF16 = jnp.bfloat16
VMEM_LIMIT = 10 * 1024 * 1024
COST = pl.CostEstimate(flops=1024, bytes_accessed=1024, transcendentals=0)


def swap(value, mask):
    pairs = [(source, source ^ mask) for source in range(lax.axis_size("expert"))]
    return lax.ppermute(value, "expert", pairs)


def iota(shape, dim):
    return lax.broadcasted_iota(jnp.int32, shape, dim)


def routing(own, picks, rows):
    tokens = picks.shape[1]
    expert = jnp.bitwise_xor(own, iota((rows, tokens), 0))
    hit = [picks[k : k + 1, :] == expert for k in range(TOPK)]
    member = hit[0] | hit[1]
    earlier = (iota((tokens, tokens), 0) < iota((tokens, tokens), 1)).astype(BF16)
    slot = jnp.dot(member.astype(F32).astype(BF16), earlier, preferred_element_type=F32)
    slot = jnp.where(member, slot.astype(jnp.int32), -1)
    return hit, slot


def pack_kernel(own_ref, tokens_hbm, gain_hbm, picks_hbm, gate_hbm, up_hbm, down_hbm, *refs):
    *out_refs, weights_ref, tokens_ref, gain_ref, picks_ref, arrived = refs
    width, hidden = gate_hbm.shape
    moves = [(tokens_hbm, tokens_ref), (gain_hbm, gain_ref), (picks_hbm, picks_ref)]
    sources = [gate_hbm, up_hbm]
    sources += [down_hbm.at[:, pl.ds(first, hidden)] for first in range(0, width, hidden)]
    first = 0
    for source in sources:
        moves.append((source, weights_ref.at[pl.ds(first, source.shape[0]), :]))
        first += source.shape[0]
    copies = [pltpu.make_async_copy(*move, arrived.at[n]) for n, move in enumerate(moves)]
    for copy in copies:
        copy.start()
    for copy in copies[:3]:
        copy.wait()
    tokens = tokens_ref.shape[0]
    values = tokens_ref[...].astype(F32)
    scale = lax.rsqrt(jnp.mean(values * values, axis=-1, keepdims=True) + EPS)
    normed = (values * scale * gain_ref[...][None, :]).astype(BF16)
    _, slot = routing(own_ref[0], picks_ref[...], max(8, len(out_refs)))
    for k, out_ref in enumerate(out_refs):
        place = iota((out_ref.shape[0], tokens), 0)
        chosen = (slot[k : k + 1, :] == place).astype(F32).astype(BF16)
        out_ref[...] = jnp.dot(chosen, normed, preferred_element_type=F32).astype(BF16)
    for copy in copies[3:]:
        copy.wait()


def pack(own, tokens, gain, picks, weights, experts, capacity):
    width, hidden = weights[0].shape
    smem = pl.BlockSpec(memory_space=pltpu.SMEM)
    vmem = pl.BlockSpec(memory_space=pltpu.VMEM)
    hbm = pl.BlockSpec(memory_space=pltpu.HBM)
    shapes = [(capacity, width)] * experts + [(3 * width, hidden)]
    there = [pltpu.with_memory_space_constraint(array, pltpu.HBM) for array in (tokens, gain, picks, *weights)]
    return pl.pallas_call(
        pack_kernel,
        out_shape=[jax.ShapeDtypeStruct(shape, BF16) for shape in shapes],
        in_specs=[smem] + [hbm] * 6,
        out_specs=[vmem] * len(shapes),
        scratch_shapes=[
            pltpu.VMEM(tokens.shape, BF16),
            pltpu.VMEM(gain.shape, F32),
            pltpu.VMEM(picks.shape, jnp.int32),
            pltpu.SemaphoreType.DMA((5 + width // hidden,)),
        ],
        compiler_params=pltpu.CompilerParams(vmem_limit_bytes=VMEM_LIMIT),
        cost_estimate=COST,
        name="pack",
    )(own, *there)


def expert_kernel(first, near_ref, far_ref, *refs):
    *weight_refs, mine_ref, theirs_ref, rows = refs
    count = far_ref.shape[0]
    rows[:count, :] = near_ref[first : first + count, :]
    rows[count:, :] = far_ref[...]
    width = rows.shape[1]
    size = weight_refs[0].shape[1]
    hidden = []
    for ref in weight_refs:
        gate = jnp.dot(rows[...], ref[:width, :], preferred_element_type=F32)
        up = jnp.dot(rows[...], ref[width : 2 * width, :], preferred_element_type=F32)
        hidden.append((jax.nn.silu(gate) * up).astype(BF16))
    for start in range(0, width, size):
        part = sum(
            jnp.dot(value, ref[pl.ds(2 * width + start, size), :], preferred_element_type=F32)
            for value, ref in zip(hidden, weight_refs)
        ).astype(BF16)
        mine_ref[:, start : start + size] = part[:count]
        theirs_ref[:, start : start + size] = part[count:]


def expert_block(near, first, far, weights):
    count, width = far.shape
    vmem = pl.BlockSpec(memory_space=pltpu.VMEM)
    return pl.pallas_call(
        functools.partial(expert_kernel, first),
        out_shape=[jax.ShapeDtypeStruct((count, width), BF16)] * 2,
        in_specs=[vmem] * (2 + len(weights)),
        out_specs=[vmem] * 2,
        scratch_shapes=[pltpu.VMEM((2 * count, width), BF16)],
        compiler_params=pltpu.CompilerParams(vmem_limit_bytes=VMEM_LIMIT),
        cost_estimate=COST,
        name="expert_block",
    )(near, far, *weights)


def score_kernel(capacity, own_ref, tokens_ref, gain_ref, picks_ref, gates_ref, target_ref, rest_ref, seg_ref, *refs):
    *block_refs, out_ref, stacked, stream = refs
    tokens, width = tokens_ref.shape
    experts = stacked.shape[0] // capacity
    first = 0
    for ref in block_refs:
        stacked[first : first + ref.shape[0], :] = ref[...]
        first += ref.shape[0]
    hit, slot = routing(own_ref[0], picks_ref[...], max(8, experts))
    weight = sum(jnp.where(hit[k], gates_ref[k : k + 1, :], 0.0) for k in range(TOPK))
    place = iota((capacity, tokens), 0)
    parts = [
        jnp.where(slot[k : k + 1, :] == place, weight[k : k + 1, :], 0.0) for k in range(experts)
    ]
    spread = jnp.concatenate(parts, axis=0)
    coarse = spread.astype(BF16)
    fine = (spread - coarse.astype(F32)).astype(BF16)
    chunk = width // 7 if width % 7 == 0 else width
    over_rows = (((0,), (0,)), ((), ()))
    squares = jnp.zeros((tokens, 1), F32)
    for start in range(0, width, chunk):
        cols = slice(start, start + chunk)
        rows = stacked[:, cols]
        moe = lax.dot_general(coarse, rows, over_rows, preferred_element_type=F32)
        moe = moe + lax.dot_general(fine, rows, over_rows, preferred_element_type=F32)
        value = tokens_ref[:, cols].astype(F32) + moe
        stream[:, cols] = value
        squares = squares + jnp.sum(value * value, axis=-1, keepdims=True)
    scale = lax.rsqrt(squares / width + EPS)
    logit = jnp.zeros((tokens, 1), F32)
    for start in range(0, width, chunk):
        cols = slice(start, start + chunk)
        final = (stream[:, cols] * scale * gain_ref[cols][None, :]).astype(BF16).astype(F32)
        logit = logit + jnp.sum(final * target_ref[:, cols].astype(F32), axis=-1, keepdims=True)
    turn = iota((tokens, tokens), 0) == iota((tokens, tokens), 1)
    logit = jnp.sum(jnp.where(turn, logit, 0.0), axis=0, keepdims=True)
    gap = rest_ref[...] - logit
    token_logp = -(jnp.maximum(gap, 0.0) + jnp.log1p(jnp.exp(-jnp.abs(gap))))
    sequences = out_ref.shape[1]
    inside = iota((sequences, tokens), 0) == seg_ref[...]
    sums = jnp.sum(jnp.where(inside, token_logp, 0.0), axis=1, keepdims=True)
    turn = iota((sequences, sequences), 0) == iota((sequences, sequences), 1)
    sums = jnp.sum(jnp.where(turn, sums, 0.0), axis=0, keepdims=True)
    out_ref[...] = jnp.broadcast_to(sums, out_ref.shape)


def score(own, tokens, gain, picks, gates, target, rest, seg, blocks, capacity, outs):
    rows, width = tokens.shape
    slots = sum(block.shape[0] for block in blocks)
    smem = pl.BlockSpec(memory_space=pltpu.SMEM)
    vmem = pl.BlockSpec(memory_space=pltpu.VMEM)
    return pl.pallas_call(
        functools.partial(score_kernel, capacity),
        out_shape=jax.ShapeDtypeStruct(outs, F32),
        in_specs=[smem] + [vmem] * (7 + len(blocks)),
        out_specs=vmem,
        scratch_shapes=[
            pltpu.VMEM((slots, width), BF16),
            pltpu.VMEM((rows, width), F32),
        ],
        compiler_params=pltpu.CompilerParams(vmem_limit_bytes=VMEM_LIMIT),
        cost_estimate=COST,
        name="score",
    )(own, tokens, gain, picks, gates, target, rest, seg, *blocks)


class Order:
    def __init__(self, token):
        self.token = token

    def mark(self, *values):
        *values, self.token = lax.optimization_barrier((*values, self.token))
        return values

    def mark_one(self, value):
        return self.mark(value)[0]

    def late(self, value):
        return lax.optimization_barrier((value, self.token))[0]


def cut_kernel(whole_ref, *refs):
    first = 0
    for ref in refs:
        ref[...] = whole_ref[first : first + ref.shape[0], :]
        first += ref.shape[0]


def cut(whole, pieces):
    vmem = pl.BlockSpec(memory_space=pltpu.VMEM)
    return pl.pallas_call(
        cut_kernel,
        out_shape=[jax.ShapeDtypeStruct((count, whole.shape[1]), BF16) for _, count in pieces],
        in_specs=[vmem],
        out_specs=[vmem] * len(pieces),
        compiler_params=pltpu.CompilerParams(vmem_limit_bytes=VMEM_LIMIT),
        cost_estimate=COST,
        name="cut",
    )(whole)


def join_kernel(*refs):
    *refs, out_ref = refs
    first = 0
    for ref in refs:
        out_ref[first : first + ref.shape[0], :] = ref[...]
        first += ref.shape[0]


def join(arrays):
    vmem = pl.BlockSpec(memory_space=pltpu.VMEM)
    rows = sum(array.shape[0] for array in arrays)
    return pl.pallas_call(
        join_kernel,
        out_shape=jax.ShapeDtypeStruct((rows, arrays[0].shape[1]), BF16),
        in_specs=[vmem] * len(arrays),
        out_specs=vmem,
        compiler_params=pltpu.CompilerParams(vmem_limit_bytes=VMEM_LIMIT),
        cost_estimate=COST,
        name="join",
    )(*arrays)


def total_kernel(count, *refs):
    *refs, out_ref = refs
    for side in (refs[:count], refs[count:]):
        first = 0
        for ref in side:
            rows = slice(first, first + ref.shape[0])
            if side[0] is refs[0]:
                out_ref[rows, :] = ref[...]
            else:
                out_ref[rows, :] = (out_ref[rows, :].astype(F32) + ref[...].astype(F32)).astype(BF16)
            first += ref.shape[0]


def total(ours, others):
    rows = sum(piece.shape[0] for piece in ours)
    vmem = pl.BlockSpec(memory_space=pltpu.VMEM)
    return pl.pallas_call(
        functools.partial(total_kernel, len(ours)),
        out_shape=jax.ShapeDtypeStruct((rows, ours[0].shape[1]), BF16),
        in_specs=[vmem] * (len(ours) + len(others)),
        out_specs=vmem,
        compiler_params=pltpu.CompilerParams(vmem_limit_bytes=VMEM_LIMIT),
        cost_estimate=COST,
        name="total",
    )(*ours, *others)


def per_device(
    tokens,
    norm_gain,
    final_gain,
    gate_weight,
    up_weight,
    down_weight,
    picks,
    gates,
    target_rows,
    rest_lse,
    segment_ids,
    ref_logps,
):
    tok_rows = tokens.shape[0]
    spread = FFE // HID_DEV
    devices = lax.axis_size("expert")
    experts = devices // spread
    capacity = (tok_rows * TOPK * 5 // (experts * 4) + 3) // 4 * 4
    capacity = (capacity + 15) // 16 * 16
    own = (lax.axis_index("expert") // spread).astype(jnp.int32).reshape(1)
    picks_t = picks.T
    core, side = 1, 2
    cut_at = capacity * 5 // 8 // 16 * 16
    pieces = [(0, cut_at), (cut_at, capacity - cut_at)] if cut_at else [(0, capacity)]
    weights = (gate_weight, up_weight, down_weight)
    *near, staged = pack(own, tokens, norm_gain, picks_t, weights, experts, capacity)
    weights = [staged, swap(staged, core)]
    order = Order(own)
    far, mine, theirs, back = {}, {}, {}, {}

    def leave(k):
        near[k] = swap(order.late(near[k]), k * spread)

    def arrive(k):
        near[k] = order.mark_one(near[k])

    def share(k):
        far[k] = [swap(order.late(piece), side) for piece in order.mark(*cut(near[k], pieces))]

    def work(k):
        mine[k], theirs[k] = [], []
        for (first, _), piece in zip(pieces, far[k]):
            there = order.mark_one(piece)
            part, other = order.mark(*expert_block(order.late(near[k]), first, there, weights))
            if k == 2 and first:
                far[0], far[1], other = lax.optimization_barrier((far[0], far[1], other))
            mine[k].append(part)
            theirs[k].append(swap(other, side))

    def work_whole(k):
        rows = (order.late(near[k]), 0, order.late(far[k]))
        mine[k], theirs[k] = order.mark(*expert_block(*rows, weights))

    def home(k):
        theirs[k] = order.mark(*theirs[k])
        back[k] = order.mark_one(total(mine[k], theirs[k]))

    def leave_back(k):
        back[k] = swap(order.late(back[k]), k * spread)

    def arrive_back(k):
        back[k] = order.mark_one(back[k])

    leave(2)
    far[1] = [swap(piece, side) for piece in cut(near[1], pieces)]
    leave(1)
    *far[1], weights[1] = order.mark(*far[1], weights[1])
    far[1] = swap(join(far[1]), spread)
    near[0], weights[1] = lax.optimization_barrier((near[0], weights[1]))
    far[0] = swap(near[0], side)
    arrive(2)
    last = pieces[-1]
    for k in range(3, experts + 1):
        if k > 3:
            near[k - 1], *theirs[k - 2] = lax.optimization_barrier((near[k - 1], *theirs[k - 2]))
        share(k - 1)
        if k < experts:
            leave(k)
        if k == 3:
            arrive(1)
        if k > 3:
            home(k - 2)
            leave_back(k - 2)
        if k == experts:
            work_whole(1)
            theirs[1] = swap(theirs[1], spread)
        work(k - 1)
        if k == experts:
            work_whole(0)
        if k < experts:
            arrive(k)
        if k > 3:
            arrive_back(k - 2)
    home(experts - 1)
    leave_back(experts - 1)
    mine[0], theirs[0] = [mine[0]], [swap(order.late(theirs[0]), side)]
    mine[1] = [swap(order.late(mine[1]), spread)]
    theirs[1] = order.mark(*cut(order.mark_one(theirs[1]), [(0, last[0]), last]))
    theirs[1] = [swap(order.late(piece), side) for piece in theirs[1]]
    order = Order(own)
    arrive_back(experts - 1)
    theirs[0] = order.mark(*theirs[0])
    mine[1] = order.mark(*mine[1])
    own = order.token
    back[0], back[1] = total(mine[0], theirs[0]), total(mine[1], theirs[1])
    blocks = [back[k] for k in range(experts)]
    local = score(
        own,
        tokens,
        final_gain,
        picks_t,
        gates.T,
        target_rows,
        rest_lse[None, :],
        segment_ids[None, :],
        blocks,
        capacity,
        (devices, ref_logps.shape[0]),
    )
    gathered = lax.all_to_all(local, "expert", split_axis=0, concat_axis=0, tiled=True)
    sequence_logps = jnp.sum(gathered, axis=0)
    margin = sequence_logps[0::2] - ref_logps[0::2] - (sequence_logps[1::2] - ref_logps[1::2])
    pair_loss = -jax.nn.log_sigmoid(BETA * margin)
    return (sequence_logps, pair_loss)


def solution(mesh):
    placed = (
        P(("group", "expert"), None),
        P(),
        P(),
        P(None, "expert"),
        P(None, "expert"),
        P("expert", None),
        P(("group", "expert"), None),
        P(("group", "expert"), None),
        P(("group", "expert"), None),
        P(("group", "expert")),
        P(("group", "expert")),
        P("group"),
    )
    return jax.shard_map(
        per_device, mesh=mesh, in_specs=placed, out_specs=(P("group"), P("group")), check_vma=False
    )
```
